512 devices in a mesh: gx: 64 (over x, z_lo, core), gy: 8 (over z_hi, y).
Axes of the slice: x: 4, y: 4, z: 16 (z_hi: 2, z_lo: 8; z = z_hi * 8 + z_lo), core: 2. Of those that a mesh axis runs over, the one named last changes fastest.
Arguments:
- ensemble: float32 [32, 2, 2, 256, 1024], P(None, None, None, 'gx', 'gy')
- courant: float32 [2], replicated, may hold values from 0.25 to 0.5
- target_spread: float32 [2, 2], replicated, may hold values from 0.5 to 2
- obs_error: float32 [2], replicated, may hold values from 0.2 to 1
- obs_value: float32 [3, 512], replicated, may hold values from -8 to 8
- obs_owner: int32 [3, 512], replicated, may hold values from 0 to 511, as said below
- obs_cell: int32 [3, 512], replicated, may hold values from 0 to 511
- obs_kind: int32 [3, 512], replicated, may hold values from 0 to 1
- tile_mask: int32 [3, 64, 8, 512], P(None, 'gx', 'gy'), may hold values from 0 to 1, as said below
- batch_order: int32 [3], replicated, may hold values from 0 to 2, each once
Outputs:
- analysis: float32 [32, 2, 2, 256, 1024], P(None, None, None, 'gx', 'gy')
The draws below stay inside these ranges and needn't reach their ends.
Inputs may be any that keep to these rules, and one draw needn't show every extreme that they name: obs_owner[b, j] is the tile tx * 8 + ty whose cells hold observation j; every batch names the first and the last tile. tile_mask[b, tx, ty, j] is 0 wherever the periodic distance between tx and obs_owner[b, j] // 8 exceeds 2 tiles.
All inputs are finite; a program needn't handle non-finite values.
Results may differ from the reference program's by a relative error of at most 0.00011.
Values sent between devices are 32-bit elements; how exact they have to be, the bound alone decides.
No kernel may reach another device: no remote copies, remote signals or barrier semaphores. Data moves between devices by JAX's collectives and lax.ppermute only.
A program may use at most 64 MiB of HBM per device.

```python
import math
import jax
import jax.numpy as jnp
from jax import lax

MEMBERS = 32
FIELDS = 2
LEVELS = 2
CX = 4
CY = 128
OBS = 512
BATCHES = 3
STEPS = 2
RX = 2
NX = 256
NY = 1024
TILES_X = 64
TILES_Y = 8
LOC_X = 12
LOC_Y = 512


def draw_ensemble(key, part):
    key_col = jax.random.fold_in(key, 3)
    key_row = jax.random.fold_in(key, 5)
    key_mean = jax.random.fold_in(key, 7)
    key_dev = jax.random.fold_in(key, 9)
    along = jnp.arange(NX, dtype=jnp.float32) / NX
    rise = 1.0 + 2.0 * along
    column_scale = jnp.exp(jax.random.uniform(key_col, (NX,), jnp.float32, 0.0, math.log(3.0)))
    row_scale = jnp.exp(jax.random.uniform(key_row, (NY,), jnp.float32, 0.0, math.log(3.0)))
    scale = 0.25 * (rise * column_scale)[:, None] * row_scale[None, :]
    centre = jax.random.normal(key_mean, (FIELDS, LEVELS, NX, NY), jnp.float32)
    spread = jax.random.normal(key_dev, (MEMBERS, FIELDS, LEVELS, NX, NY), jnp.float32)
    return (centre[None] + scale[None, None, None] * spread).astype(jnp.float32)


def owner_table(key):
    tiles = TILES_X * TILES_Y
    owner = jax.random.randint(jax.random.fold_in(key, 17), (BATCHES, OBS), 0, tiles)
    first = jax.random.randint(jax.random.fold_in(key, 19), (BATCHES,), 0, OBS)
    second = (first + 1) % OBS
    slots = jnp.arange(OBS)[None, :]
    owner = jnp.where(slots == first[:, None], tiles - 1, owner)
    owner = jnp.where(slots == second[:, None], 0, owner)
    return owner.astype(jnp.int32)


def draw_obs_owner(key, part):
    return owner_table(key)


def draw_tile_mask(key, part):
    owner = owner_table(key)
    owner_x = owner // TILES_Y
    tile_x = jnp.arange(TILES_X)
    gap = jnp.abs(tile_x[None, :, None] - owner_x[:, None, :])
    gap = jnp.minimum(gap, TILES_X - gap)
    near = gap <= RX
    keep = jax.random.randint(jax.random.fold_in(key, 29), (BATCHES, TILES_X, TILES_Y, OBS), 0, 5) > 0
    return jnp.where(near[:, :, None, :] & keep, 1, 0).astype(jnp.int32)


def plant(result, stream_key, smallest, largest):
    spot = [jax.random.randint(jax.random.fold_in(stream_key, axis), (), 0, length) for axis, length in enumerate(result.shape)]
    main_axis = result.shape.index(max(result.shape))
    neighbour = spot[:main_axis] + [(spot[main_axis] + 1) % result.shape[main_axis]] + spot[main_axis + 1:]
    return result.at[tuple(spot)].set(smallest).at[tuple(neighbour)].set(largest)


def bell_draw(own_key, extent, scale, most, kind=jnp.bfloat16):
    drawn = scale * jax.random.normal(own_key, extent, jnp.float32)
    return jnp.clip(drawn, min=-most, max=most).astype(kind)


def setup_inputs(seed: int = 0) -> dict:
    seeds = jax.random.split(jax.random.key(seed), 11)
    return {
        "ensemble": draw_ensemble(jax.random.fold_in(seeds[10], 71), 0),
        "courant": jnp.clip(jax.random.uniform(seeds[1], (LEVELS,), jnp.float32, 0.25, 0.5), 0.25, 0.5),
        "target_spread": jnp.clip(jnp.exp(jax.random.uniform(seeds[2], (FIELDS, LEVELS), jnp.float32, math.log(0.5), math.log(2.0))), 0.5, 2.0),
        "obs_error": jnp.clip(jnp.exp(jax.random.uniform(seeds[3], (FIELDS,), jnp.float32, math.log(0.2), math.log(1.0))), 0.2, 1.0),
        "obs_value": bell_draw(seeds[4], (BATCHES, OBS), 1.5, 8.0, jnp.float32),
        "obs_owner": draw_obs_owner(jax.random.fold_in(seeds[10], 71), 0),
        "obs_cell": plant(jax.random.randint(seeds[6], (BATCHES, OBS), 0, CX * CY), jax.random.fold_in(seeds[6], 1), 0, (CX * CY) - 1).astype(jnp.int32),
        "obs_kind": plant(jax.random.randint(seeds[7], (BATCHES, OBS), 0, FIELDS), jax.random.fold_in(seeds[7], 1), 0, FIELDS - 1).astype(jnp.int32),
        "tile_mask": draw_tile_mask(jax.random.fold_in(seeds[10], 71), 0),
        "batch_order": jax.random.permutation(seeds[9], BATCHES).astype(jnp.int32),
    }


diffuse_rate = 0.1
mixing_rate = 0.05
spread_floor = 1e-05

def vertical(centre):
    below = jnp.concatenate([centre[:, :, :1], centre[:, :, :-1]], axis=2)
    above = jnp.concatenate([centre[:, :, 1:], centre[:, :, -1:]], axis=2)
    return below + above - 2.0 * centre

def advance(state, courant):
    upwind = jnp.roll(state, 1, axis=3)
    downwind = jnp.roll(state, -1, axis=3)
    padded = jnp.pad(state, ((0, 0), (0, 0), (0, 0), (0, 0), (1, 1)))
    lower = padded[..., :-2]
    upper = padded[..., 2:]
    speed = courant[None, None, :, None, None]
    return state + speed * (upwind - state) + diffuse_rate * (upwind + downwind + lower + upper - 4.0 * state) + mixing_rate * vertical(state)

def taper_of(xs, ys, ox, oy, width_x, loc_x, loc_y):
    gap_x = jnp.abs(xs[:, None, None] - ox[None, None, :])
    gap_x = jnp.minimum(gap_x, width_x - gap_x).astype(jnp.float32) / loc_x
    gap_y = jnp.abs(ys[None, :, None] - oy[None, None, :]).astype(jnp.float32) / loc_y
    room = jnp.maximum(1.0 - gap_x * gap_x - gap_y * gap_y, 0.0)
    return room * room

def obs_space(prior, value, error):
    members = prior.shape[0]
    prior_mean = lax.optimization_barrier(jnp.mean(prior, axis=0))
    prior_dev = prior - prior_mean
    prior_var = lax.optimization_barrier(jnp.sum(prior_dev * prior_dev, axis=0)) / (members - 1)
    gain = (value - prior_mean) / (prior_var + error)
    shrink = -1.0 / (jnp.sqrt(error * (error + prior_var)) + error + prior_var)
    return (prior_dev, gain[None, :] + shrink[None, :] * prior_dev)

def reference(ensemble, courant, target_spread, obs_error, obs_value, obs_owner, obs_cell, obs_kind, tile_mask, batch_order):
    state = ensemble
    for step in range(STEPS):
        state = advance(state, courant)
    members = state.shape[0]
    centre = lax.optimization_barrier(jnp.mean(state, axis=0))
    deviation = state - centre
    cell_var = lax.optimization_barrier(jnp.sum(deviation * deviation, axis=0)) / (members - 1)
    mean_var = lax.optimization_barrier(jnp.sum(cell_var, axis=(2, 3))) / float(NX * NY)
    inflation = jnp.sqrt(target_spread / (mean_var + spread_floor))
    state = centre + inflation[None, :, :, None, None] * deviation
    scale = 1.0 / (members - 1)
    for turn in range(BATCHES):
        batch = batch_order[turn]
        owner = obs_owner[batch]
        cell = obs_cell[batch]
        kind = obs_kind[batch]
        ox = owner // TILES_Y * CX + cell // CY
        oy = owner % TILES_Y * CY + cell % CY
        prior = state[:, kind, 0, ox, oy]
        prior_dev, drive = obs_space(prior, obs_value[batch], obs_error[kind])
        state_dev = state - lax.optimization_barrier(jnp.mean(state, axis=0))
        tiles = state_dev.reshape(MEMBERS, FIELDS, LEVELS, TILES_X, CX, NY).transpose(3, 0, 1, 2, 4, 5)
        masks = tile_mask[batch]

        def one_tile(item):
            place, tile = item
            xs = place * CX + jnp.arange(CX, dtype=jnp.int32)
            ys = jnp.arange(NY, dtype=jnp.int32)
            rows_mask = jnp.repeat(masks[place], CY, axis=0).astype(jnp.float32)
            weight = taper_of(xs, ys, ox, oy, NX, float(LOC_X), float(LOC_Y)) * rows_mask[None, :, :]
            covariance = jnp.einsum('mflxy,mj->flxyj', tile, prior_dev, precision=lax.Precision.HIGHEST) * scale
            return jnp.einsum('flxyj,mj->mflxy', covariance * weight[None, None], drive, precision=lax.Precision.HIGHEST)
        increments = lax.map(one_tile, (jnp.arange(TILES_X, dtype=jnp.int32), tiles))
        state = state + increments.transpose(1, 2, 3, 0, 4, 5).reshape(state.shape)
    return state
```

```python
import jax
import jax.numpy as jnp
from jax import lax
from jax.experimental import pallas as pl
from jax.experimental.pallas import tpu as pltpu
from jax.sharding import PartitionSpec as P

MEMBERS = 32
GROUPS = 4
CX = 4
CY = 128
CELLS = CX * CY
OBS = 512
BATCHES = 3
STEPS = 2
TILES_X = 64
TILES_Y = 8
TILES = TILES_X * TILES_Y
NX = TILES_X * CX
NY = TILES_Y * CY
LOC_X = 12.0
LOC_Y = 512.0
REACH = 2
SPAN = 2 * REACH + 1
WINDOW = SPAN * TILES_Y
CHUNK = 256
AHEAD = GROUPS * CELLS

diffuse_rate = 0.1
mixing_rate = 0.05
spread_floor = 1e-05

F32 = jnp.float32
BF16 = jnp.bfloat16
I32 = jnp.int32

VMEM = pl.BlockSpec(memory_space=pltpu.VMEM)
SMEM = pl.BlockSpec(memory_space=pltpu.SMEM)


def rows_of(group, x):
    return pl.ds(group * CX + x, MEMBERS, stride=GROUPS * CX)


def mm(a, b):
    return lax.dot_general(a, b, (((1,), (0,)), ((), ())), preferred_element_type=F32)


def halves(value):
    high = value.astype(BF16)
    return high, (value - high.astype(F32)).astype(BF16)


def thirds(value):
    high = value.astype(BF16)
    rest = value - high.astype(F32)
    middle = rest.astype(BF16)
    return high, middle, (rest - middle.astype(F32)).astype(BF16)


def edges_kernel(ens_ref, low_ref, high_ref):
    turned = ens_ref[...].T
    low_ref[...] = turned[0:2]
    high_ref[...] = turned[CY - 2 : CY]


def advance(rows, courant_ref, keep):
    lowest = min(x for _, x in rows) - 1
    highest = max(x for _, x in rows) + 1
    width = 2 * CY
    after = {}
    for group in range(GROUPS):
        speed = courant_ref[group % 2]
        stay = 1.0 - speed - 4.0 * diffuse_rate - mixing_rate
        for x in range(lowest, highest + 1):
            terms = []
            if (group, x) in rows:
                here = rows[group, x]
                beside = pltpu.roll(here, 1, 1) + pltpu.roll(here, width - 1, 1)
                terms.append(stay * here + diffuse_rate * beside + mixing_rate * rows[group ^ 1, x])
            if (group, x - 1) in rows:
                terms.append((speed + diffuse_rate) * rows[group, x - 1])
            if (group, x + 1) in rows:
                terms.append(diffuse_rate * rows[group, x + 1])
            total = terms[0]
            for term in terms[1:]:
                total = total + term
            after[group, x] = total if keep is None else total * keep
    return after


def spread_kernel(
    order_ref,
    place_ref,
    courant_ref,
    ens_ref,
    before_ref,
    behind_ref,
    owner_ref,
    cell_ref,
    kind_ref,
    mask_ref,
    own_ref,
    left_ref,
    right_ref,
    send_ref,
    outer_ref,
):
    place_x = place_ref[0]
    place_y = place_ref[1]
    rim = jnp.concatenate(
        [behind_ref[...], jnp.zeros((CY - 4, OBS), F32), before_ref[...]], axis=0
    )
    outer_ref[...] = rim.T
    rows = {}
    for group in range(GROUPS):
        for x in range(CX):
            rows[group, x] = jnp.concatenate(
                [ens_ref[rows_of(group, x), :], outer_ref[rows_of(group, x), :]], axis=1
            )
    lane = lax.broadcasted_iota(I32, (1, 2 * CY), 1)
    below = (lane >= 3 * CY // 2) & (place_y == 0)
    above = (lane >= CY) & (lane < 3 * CY // 2) & (place_y == TILES_Y - 1)
    keep = jnp.where(below | above, 0.0, 1.0).astype(F32)
    rows = advance(rows, courant_ref, keep)
    rows = advance(rows, courant_ref, None)
    tile = {at: value[:, :CY] for at, value in rows.items()}
    for group in range(GROUPS):
        for x in range(CX):
            own_ref[group, :, x * CY : (x + 1) * CY] = tile[group, x]
        for x in range(2):
            left_ref[group, :, x * CY : (x + 1) * CY] = tile[group, x - 2]
            right_ref[group, :, x * CY : (x + 1) * CY] = tile[group, x + CX]
    ground = jnp.concatenate(
        [
            jnp.concatenate([tile[2 * field, x] for x in range(-2, CX + 2)], axis=1)
            for field in range(2)
        ],
        axis=0,
    )
    parts = jnp.concatenate(thirds(ground), axis=0)
    blocks = []
    masks = []
    for turn in range(BATCHES):
        batch = order_ref[turn]
        owner = owner_ref[pl.ds(batch, 1), :]
        cell = cell_ref[pl.ds(batch, 1), :]
        kind = kind_ref[pl.ds(batch, 1), :]
        masks.append(mask_ref[pl.ds(batch, 1), :].astype(F32))
        at_x = ((owner >> 3) - place_x) * CX + (cell >> 7) + 2
        at_x = at_x & (NX - 1)
        seen = (at_x < CX + 4) & ((owner & (TILES_Y - 1)) == place_y)
        index = jnp.where(seen, at_x * CY + (cell & (CY - 1)), -1)
        picked = jnp.zeros((parts.shape[0], OBS), F32)
        for start in range(0, (CX + 4) * CY, CHUNK):
            spot = lax.broadcasted_iota(I32, (CHUNK, OBS), 0) + start
            hot = jnp.where(spot == index, 1.0, 0.0).astype(BF16)
            picked = picked + mm(parts[:, start : start + CHUNK], hot)
        picked = picked[0:64] + picked[64:128] + picked[128:192]
        blocks.append(jnp.where(kind == 0, picked[0:32], picked[32:64]))
    sub = lax.broadcasted_iota(I32, (MEMBERS, OBS), 0)
    blocks.append(jnp.where(sub == 0, masks[0], jnp.where(sub == 1, masks[1], 0.0)))
    send_ref[...] = jnp.concatenate(blocks, axis=0).T


def merge_kernel(
    order_ref,
    place_ref,
    relay_ref,
    own_ref,
    from_left_ref,
    from_right_ref,
    recv_ref,
    forecast_ref,
    send_ref,
):
    place = place_ref[0] * TILES_Y + place_ref[1]
    lane = lax.broadcasted_iota(I32, (1, CY), 1)
    top = jnp.sum(recv_ref[...], axis=0, keepdims=True)
    top = jnp.where(lane < BATCHES * MEMBERS, top, 0.0)
    for group in range(GROUPS):
        own = own_ref[group]
        value = jnp.concatenate(
            [
                own[:, : 2 * CY] + from_left_ref[group],
                own[:, 2 * CY :] + from_right_ref[group],
            ],
            axis=1,
        )
        forecast_ref[group] = value
        centre = jnp.sum(value, axis=0, keepdims=True) * (1.0 / MEMBERS)
        deviation = value - centre
        total = jnp.sum(jnp.sum(deviation * deviation, axis=0, keepdims=True), axis=1, keepdims=True)
        top = jnp.where(lane == BATCHES * MEMBERS + group, total, top)
    pieces = []
    for turn in range(2):
        column = relay_ref[order_ref[turn], place] >> 3
        for step in range(SPAN):
            at = (column + (step - REACH)) & (TILES_X - 1)
            start = pl.multiple_of(at * TILES_Y, TILES_Y)
            pieces.append(recv_ref[pl.ds(start, TILES_Y), :])
    pieces.append(jnp.zeros((CY - 2 * WINDOW, CY), F32))
    turned = jnp.concatenate(pieces, axis=0).T
    first = turned[BATCHES * MEMBERS : BATCHES * MEMBERS + 1]
    second = turned[BATCHES * MEMBERS + 1 : BATCHES * MEMBERS + 2]
    bottom = jnp.where(lane < WINDOW, first, jnp.where(lane < 2 * WINDOW, second, 0.0))
    pair = jnp.concatenate([top, bottom] * 4, axis=0)
    send_ref[...] = jnp.concatenate([pair] * (2 * TILES // 8), axis=0)


def assimilate_kernel(
    order_ref,
    place_ref,
    spread_ref,
    error_ref,
    forecast_ref,
    recv_ref,
    owner_ref,
    cell_ref,
    kind_ref,
    value_ref,
    mask_ref,
    out_ref,
    state_ref,
    pack_ref,
    left_ref,
    drive_ref,
    table_ref,
    spots_ref,
    weight_ref,
):
    place_x = place_ref[0]
    place_y = place_ref[1]
    upper = recv_ref[pl.ds(0, TILES, stride=2), :].T
    stretch = []
    for group in range(GROUPS):
        row = BATCHES * MEMBERS + group
        total = jnp.sum(upper[row : row + 1], axis=1, keepdims=True)
        mean_var = total * (1.0 / ((MEMBERS - 1) * float(NX * NY)))
        stretch.append(jnp.sqrt(spread_ref[group // 2, group % 2] / (mean_var + spread_floor)))
    for group in range(GROUPS):
        value = forecast_ref[group]
        centre = jnp.sum(value, axis=0, keepdims=True) * (1.0 / MEMBERS)
        state_ref[:, group * CELLS : (group + 1) * CELLS] = centre + stretch[group] * (value - centre)

    kinds, xs, ys, values = [], [], [], []
    sub = lax.broadcasted_iota(I32, (CY, OBS), 0)
    table_ref[...] = jnp.zeros_like(table_ref)
    table = jnp.zeros((CY, OBS), F32)
    near = 4 * REACH + 1
    for turn in range(BATCHES):
        batch = order_ref[turn]
        owner = owner_ref[pl.ds(batch, 1), :]
        cell = cell_ref[pl.ds(batch, 1), :]
        kinds.append(kind_ref[pl.ds(batch, 1), :])
        values.append(value_ref[pl.ds(batch, 1), :])
        mask = mask_ref[pl.ds(batch, 1), :].astype(F32)
        xs.append(((owner >> 3) * CX + (cell >> 7)).astype(F32))
        ys.append(((owner & (TILES_Y - 1)) * CY + (cell & (CY - 1))).astype(F32))
        offset = ((owner >> 3) - place_x + REACH) & (TILES_X - 1)
        offset = jnp.where(offset >= TILES_X // 2, offset - TILES_X, offset).astype(F32)
        for row, value in enumerate((xs[turn], ys[turn], mask, offset)):
            table = jnp.where(sub == turn * 4 + row, value, table)
        prior = upper[turn * MEMBERS : (turn + 1) * MEMBERS]
        centre = jnp.sum(prior, axis=0, keepdims=True) * (1.0 / MEMBERS)
        factor = jnp.where(kinds[turn] == 0, stretch[0], stretch[2])
        state_ref[:, AHEAD + turn * OBS : AHEAD + (turn + 1) * OBS] = centre + factor * (prior - centre)
        at = ((owner >> 3) - place_x + 2 * REACH) & (TILES_X - 1)
        index = jnp.where(at < near, at * TILES_Y + (owner & (TILES_Y - 1)), -1)
        spots_ref[:, turn * OBS : (turn + 1) * OBS] = jnp.where(sub == index, 1.0, 0.0).astype(BF16)
    table_ref[...] = table.T

    lane = lax.broadcasted_iota(I32, (1, CY), 1)
    cell_x = (place_x * CX).astype(F32)
    cell_y = (place_y * CY + lane).astype(F32)

    for turn in range(BATCHES):
        prior = state_ref[:, AHEAD + turn * OBS : AHEAD + (turn + 1) * OBS]
        error = jnp.where(kinds[turn] == 0, error_ref[0], error_ref[1])
        centre = jnp.sum(prior, axis=0, keepdims=True) * (1.0 / MEMBERS)
        deviation = prior - centre
        variance = jnp.sum(deviation * deviation, axis=0, keepdims=True) / (MEMBERS - 1)
        gain = (values[turn] - centre) / (variance + error)
        shrink = -1.0 / (jnp.sqrt(error * (error + variance)) + error + variance)
        drive_high, drive_low = halves(gain + shrink * deviation)
        drive_ref[:MEMBERS] = drive_high
        drive_ref[MEMBERS:] = drive_low
        scaled = deviation * (1.0 / (MEMBERS - 1))
        scaled_high = scaled.astype(BF16).astype(F32)
        scaled_low = scaled - scaled_high
        packed = jnp.concatenate(
            [scaled_high, scaled_high, scaled_low, jnp.zeros_like(scaled)], axis=0
        )
        left_ref[...] = packed.T.astype(BF16)

        later = list(range(turn + 1, BATCHES))
        blocks = [slice(group * CELLS, (group + 1) * CELLS) for group in range(GROUPS)]
        blocks += [slice(AHEAD + other * OBS, AHEAD + (other + 1) * OBS) for other in later]
        for cols in blocks:
            state = state_ref[:, cols]
            state_dev = state - jnp.sum(state, axis=0, keepdims=True) * (1.0 / MEMBERS)
            high, low = halves(state_dev)
            pack_ref[0:32, cols] = high
            pack_ref[32:64, cols] = low
            pack_ref[64:96, cols] = high
            pack_ref[96:128, cols] = jnp.zeros_like(high)

        @pl.loop(0, OBS // CHUNK)
        def _(step):
            start = pl.multiple_of(step * CHUNK, CHUNK)
            part = pl.ds(start, CHUNK)
            table = table_ref[part, :]
            x_col = table[:, turn * 4 : turn * 4 + 1]
            y_col = table[:, turn * 4 + 1 : turn * 4 + 2]
            mask_col = table[:, turn * 4 + 2 : turn * 4 + 3]
            gap_y = y_col - cell_y
            drop_y = gap_y * gap_y * (1.0 / (LOC_Y * LOC_Y))
            for x in range(CX):
                gap_x = jnp.abs(x_col - (cell_x + x))
                gap_x = jnp.minimum(gap_x, NX - gap_x)
                room = jnp.maximum((1.0 - gap_x * gap_x * (1.0 / (LOC_X * LOC_X))) - drop_y, 0.0)
                weight_ref[:, x * CY : (x + 1) * CY] = room * room * mask_col
            if later:
                offset = table[:, turn * 4 + 3 : turn * 4 + 4]
                seen = recv_ref[pl.ds(2 * start + 1, CHUNK, stride=2), :]
                if turn == 1:
                    seen = pltpu.roll(seen, CY - WINDOW, 1)
                seen = jnp.where(lane < WINDOW, seen, 0.0)
                reach = jnp.zeros_like(seen)
                for hop in range(-(SPAN - 1), near):
                    moved = pltpu.roll(seen, (hop * TILES_Y) % CY, 1) if hop else seen
                    reach = jnp.where(offset == float(hop), moved, reach)
                reach = reach.astype(BF16)
                for place, other in enumerate(later):
                    allowed = mm(reach, spots_ref[:, other * OBS : (other + 1) * OBS])
                    gap_x = jnp.abs(x_col - xs[other])
                    gap_x = jnp.minimum(gap_x, NX - gap_x)
                    gap_y = y_col - ys[other]
                    room = 1.0 - gap_x * gap_x * (1.0 / (LOC_X * LOC_X))
                    room = jnp.maximum(room - gap_y * gap_y * (1.0 / (LOC_Y * LOC_Y)), 0.0)
                    weight_ref[:, (place + 1) * OBS : (place + 2) * OBS] = room * room * allowed

            left = left_ref[part, :]
            drive = drive_ref[:, part]
            for number, cols in enumerate(blocks):
                at = max(0, number - GROUPS + 1) * OBS
                covariance = mm(left, pack_ref[:, cols]) * weight_ref[:, at : at + OBS]
                high, low = halves(covariance)
                both = mm(drive, high)
                rest = mm(drive[:MEMBERS], low)
                state_ref[:, cols] += both[:MEMBERS] + both[MEMBERS:] + rest

    for group in range(GROUPS):
        for x in range(CX):
            at = group * CELLS + x * CY
            out_ref[rows_of(group, x), :] = state_ref[:, at : at + CY]


def call(kernel, specs, outs, scratch=()):
    return pl.pallas_call(
        kernel,
        in_specs=specs,
        out_specs=[VMEM] * len(outs) if len(outs) > 1 else VMEM,
        out_shape=outs if len(outs) > 1 else outs[0],
        scratch_shapes=list(scratch),
        compiler_params=pltpu.CompilerParams(vmem_limit_bytes=48 * 1024 * 1024),
    )


def shape(*dims):
    return jax.ShapeDtypeStruct(dims, F32)


def shifted(value, axis, step, periodic):
    count = lax.axis_size(axis)
    pairs = [
        (source, (source + step) % count)
        for source in range(count)
        if periodic or 0 <= source + step < count
    ]
    return lax.ppermute(value, axis, pairs)


def local(
    ensemble,
    courant,
    target_spread,
    obs_error,
    obs_value,
    obs_owner,
    obs_cell,
    obs_kind,
    tile_mask,
    batch_order,
):
    place = jnp.stack([lax.axis_index("gx"), lax.axis_index("gy")]).astype(I32)
    ens = ensemble.reshape(MEMBERS * GROUPS * CX, CY)
    mask = tile_mask.reshape(BATCHES, OBS)
    low, high = call(edges_kernel, [VMEM], [shape(2, OBS)] * 2)(ens)
    before = shifted(high, "gy", 1, False)
    behind = shifted(low, "gy", -1, False)
    own, left, right, send = call(
        spread_kernel,
        [SMEM] * 3 + [VMEM] * 7,
        [
            shape(GROUPS, MEMBERS, CELLS),
            shape(GROUPS, MEMBERS, 2 * CY),
            shape(GROUPS, MEMBERS, 2 * CY),
            shape(OBS, CY),
        ],
        [pltpu.VMEM((MEMBERS * GROUPS * CX, CY), F32)],
    )(
        batch_order,
        place,
        courant,
        ens,
        before,
        behind,
        obs_owner,
        obs_cell,
        obs_kind,
        mask,
    )
    from_left = shifted(right, "gx", 1, True)
    from_right = shifted(left, "gx", -1, True)
    recv = lax.all_to_all(send.reshape(TILES, 1, CY), ("gx", "gy"), 0, 0)
    forecast, send = call(
        merge_kernel,
        [SMEM] * 3 + [VMEM] * 4,
        [shape(GROUPS, MEMBERS, CELLS), shape(2 * TILES, CY)],
    )(batch_order, place, obs_owner, own, from_left, from_right, recv.reshape(TILES, CY))
    recv = lax.all_to_all(send.reshape(TILES, 2, CY), ("gx", "gy"), 0, 0)
    out = call(
        assimilate_kernel,
        [SMEM] * 4 + [VMEM] * 7,
        [shape(MEMBERS * GROUPS * CX, CY)],
        [
            pltpu.VMEM((MEMBERS, AHEAD + BATCHES * OBS), F32),
            pltpu.VMEM((CY, AHEAD + BATCHES * OBS), BF16),
            pltpu.VMEM((OBS, CY), BF16),
            pltpu.VMEM((2 * MEMBERS, OBS), BF16),
            pltpu.VMEM((OBS, CY), F32),
            pltpu.VMEM((CY, BATCHES * OBS), BF16),
            pltpu.VMEM((CHUNK, BATCHES * OBS), F32),
        ],
    )(
        batch_order,
        place,
        target_spread,
        obs_error,
        forecast,
        recv.reshape(2 * TILES, CY),
        obs_owner,
        obs_cell,
        obs_kind,
        obs_value,
        mask,
    )
    return out.reshape(ensemble.shape)


def solution(mesh):
    in_specs = (
        P(None, None, None, "gx", "gy"),
        P(),
        P(),
        P(),
        P(),
        P(),
        P(),
        P(),
        P(None, "gx", "gy", None),
        P(),
    )
    out_specs = P(None, None, None, "gx", "gy")
    return jax.shard_map(local, mesh=mesh, in_specs=in_specs, out_specs=out_specs, check_vma=False)
```

```python
import jax
import jax.numpy as jnp
from jax import lax
from jax.experimental import pallas as pl
from jax.experimental.pallas import tpu as pltpu
from jax.sharding import Mesh
from jax.sharding import PartitionSpec as P

MEMBERS = 32
GROUPS = 4
CX = 4
CY = 128
CELLS = CX * CY
OBS = 512
BATCHES = 3
STEPS = 2
TILES_X = 64
TILES_Y = 8
TILES = TILES_X * TILES_Y
NX = TILES_X * CX
NY = TILES_Y * CY
LOC_X = 12.0
LOC_Y = 512.0
REACH = 2
SPAN = 2 * REACH + 1
PLANES = 32
LAYERS = 16
HALF = CY // 2
GX = ("x", "z_lo", "core")
GY = ("z_hi", "y")
PLANE = ("x", "core", "y")
LAYER = ("z_lo", "z_hi")
CHUNK = 256
AHEAD = GROUPS * CELLS
PAIRS = ((0, 1), (0, 2), (1, 2))

diffuse_rate = 0.1
mixing_rate = 0.05
spread_floor = 1e-05

F32 = jnp.float32
BF16 = jnp.bfloat16
I32 = jnp.int32

VMEM = pl.BlockSpec(memory_space=pltpu.VMEM)
SMEM = pl.BlockSpec(memory_space=pltpu.SMEM)


def rows_of(group, x):
    return pl.ds(group * CX + x, MEMBERS, stride=GROUPS * CX)


def mm(a, b):
    return lax.dot_general(a, b, (((1,), (0,)), ((), ())), preferred_element_type=F32)


def halves(value):
    high = value.astype(BF16)
    return high, (value - high.astype(F32)).astype(BF16)


def thirds(value):
    high = value.astype(BF16)
    rest = value - high.astype(F32)
    middle = rest.astype(BF16)
    return high, middle, (rest - middle.astype(F32)).astype(BF16)


def edges_kernel(ens_ref, low_ref, high_ref):
    turned = ens_ref[...].T
    low_ref[...] = turned[0:2]
    high_ref[...] = turned[CY - 2 : CY]


def advance(rows, courant_ref, keep):
    lowest = min(x for _, x in rows) - 1
    highest = max(x for _, x in rows) + 1
    width = 2 * CY
    after = {}
    for group in range(GROUPS):
        speed = courant_ref[group % 2]
        stay = 1.0 - speed - 4.0 * diffuse_rate - mixing_rate
        for x in range(lowest, highest + 1):
            terms = []
            if (group, x) in rows:
                here = rows[group, x]
                beside = pltpu.roll(here, 1, 1) + pltpu.roll(here, width - 1, 1)
                terms.append(stay * here + diffuse_rate * beside + mixing_rate * rows[group ^ 1, x])
            if (group, x - 1) in rows:
                terms.append((speed + diffuse_rate) * rows[group, x - 1])
            if (group, x + 1) in rows:
                terms.append(diffuse_rate * rows[group, x + 1])
            total = terms[0]
            for term in terms[1:]:
                total = total + term
            after[group, x] = total if keep is None else total * keep
    return after


def spread_kernel(
    order_ref,
    place_ref,
    courant_ref,
    ens_ref,
    before_ref,
    behind_ref,
    owner_ref,
    cell_ref,
    kind_ref,
    mask_ref,
    own_ref,
    left_ref,
    right_ref,
    send_ref,
    outer_ref,
):
    place_x = place_ref[0]
    place_y = place_ref[1]
    rim = jnp.concatenate(
        [behind_ref[...], jnp.zeros((CY - 4, OBS), F32), before_ref[...]], axis=0
    )
    outer_ref[...] = rim.T
    rows = {}
    for group in range(GROUPS):
        for x in range(CX):
            rows[group, x] = jnp.concatenate(
                [ens_ref[rows_of(group, x), :], outer_ref[rows_of(group, x), :]], axis=1
            )
    lane = lax.broadcasted_iota(I32, (1, 2 * CY), 1)
    below = (lane >= 3 * CY // 2) & (place_y == 0)
    above = (lane >= CY) & (lane < 3 * CY // 2) & (place_y == TILES_Y - 1)
    keep = jnp.where(below | above, 0.0, 1.0).astype(F32)
    rows = advance(rows, courant_ref, keep)
    rows = advance(rows, courant_ref, None)
    tile = {at: value[:, :CY] for at, value in rows.items()}
    for group in range(GROUPS):
        for x in range(CX):
            own_ref[group, :, x * CY : (x + 1) * CY] = tile[group, x]
        for x in range(2):
            left_ref[group, :, x * CY : (x + 1) * CY] = tile[group, x - 2]
            right_ref[group, :, x * CY : (x + 1) * CY] = tile[group, x + CX]
    ground = jnp.concatenate(
        [
            jnp.concatenate([tile[2 * field, x] for x in range(-2, CX + 2)], axis=1)
            for field in range(2)
        ],
        axis=0,
    )
    parts = jnp.concatenate(thirds(ground), axis=0)
    blocks = []
    masks = []
    for turn in range(BATCHES):
        batch = order_ref[turn]
        owner = owner_ref[pl.ds(batch, 1), :]
        cell = cell_ref[pl.ds(batch, 1), :]
        kind = kind_ref[pl.ds(batch, 1), :]
        masks.append(mask_ref[pl.ds(batch, 1), :].astype(F32))
        at_x = ((owner >> 3) - place_x) * CX + (cell >> 7) + 2
        at_x = at_x & (NX - 1)
        seen = (at_x < CX + 4) & ((owner & (TILES_Y - 1)) == place_y)
        index = jnp.where(seen, at_x * CY + (cell & (CY - 1)), -1)
        picked = jnp.zeros((parts.shape[0], OBS), F32)
        for start in range(0, (CX + 4) * CY, CHUNK):
            spot = lax.broadcasted_iota(I32, (CHUNK, OBS), 0) + start
            hot = jnp.where(spot == index, 1.0, 0.0).astype(BF16)
            picked = picked + mm(parts[:, start : start + CHUNK], hot)
        picked = picked[0:64] + picked[64:128] + picked[128:192]
        blocks.append(jnp.where(kind == 0, picked[0:32], picked[32:64]))
    sub = lax.broadcasted_iota(I32, (MEMBERS, OBS), 0)
    blocks.append(jnp.where(sub == 0, masks[0], jnp.where(sub == 1, masks[1], 0.0)))
    send_ref[...] = jnp.concatenate(blocks, axis=0).T


def collect_kernel(recv_ref, send_ref):
    lane = lax.broadcasted_iota(I32, (LAYERS, CY), 1)
    total = jnp.zeros((LAYERS, CY), F32)
    marks = jnp.zeros((LAYERS, CY), F32)
    for plane in range(PLANES):
        rows = recv_ref[plane * LAYERS : (plane + 1) * LAYERS, :]
        total = total + rows
        for turn in range(2):
            at = BATCHES * MEMBERS + turn
            marks = jnp.where(lane == turn * PLANES + plane, rows[:, at : at + 1], marks)
    send_ref[pl.ds(0, LAYERS, stride=2), :] = total
    send_ref[pl.ds(1, LAYERS, stride=2), :] = marks


def merge_kernel(
    order_ref,
    place_ref,
    relay_ref,
    own_ref,
    from_left_ref,
    from_right_ref,
    recv_ref,
    forecast_ref,
    send_ref,
):
    relay = place_ref[2]
    lane = lax.broadcasted_iota(I32, (1, CY), 1)
    top = jnp.sum(recv_ref[pl.ds(0, LAYERS, stride=2), :], axis=0, keepdims=True)
    top = jnp.where(lane < BATCHES * MEMBERS, top, 0.0)
    for group in range(GROUPS):
        own = own_ref[group]
        value = jnp.concatenate(
            [
                own[:, : 2 * CY] + from_left_ref[group],
                own[:, 2 * CY :] + from_right_ref[group],
            ],
            axis=1,
        )
        forecast_ref[group] = value
        centre = jnp.sum(value, axis=0, keepdims=True) * (1.0 / MEMBERS)
        deviation = value - centre
        total = jnp.sum(jnp.sum(deviation * deviation, axis=0, keepdims=True), axis=1, keepdims=True)
        top = jnp.where(lane == BATCHES * MEMBERS + group, total, top)

    marks = recv_ref[pl.ds(1, LAYERS, stride=2), :]
    lanes = lax.broadcasted_iota(I32, (LAYERS, CY), 1)
    subs = lax.broadcasted_iota(I32, (LAYERS, CY), 0)
    tile_x = ((lanes >> 3) & 3) * 16 + (subs >> 1) * 2 + ((lanes >> 2) & 1)
    first = relay_ref[order_ref[0], relay] >> 3
    second = relay_ref[order_ref[1], relay] >> 3
    column = jnp.where(lanes < PLANES, first, second)
    near = ((tile_x - column + REACH) & (TILES_X - 1)) < SPAN
    marks = jnp.where(near & (lanes < 2 * PLANES), marks, 0.0)
    marks = marks[:8] + marks[8:]
    folded = marks
    for step in (8, 16, 24):
        folded = folded + pltpu.roll(marks, CY - step, 1)
    lanes = lax.broadcasted_iota(I32, (8, CY), 1)
    subs = lax.broadcasted_iota(I32, (8, CY), 0)
    bottom = jnp.zeros((8, CY), F32)
    for row in range(8):
        for turn in range(2):
            moved = pltpu.roll(folded, (turn * PLANES + row * 8) % CY, 1)
            there = (subs == row) & ((lanes >> 3) == turn * 8 + row)
            bottom = jnp.where(there, moved, bottom)
    bottom = jnp.sum(bottom, axis=0, keepdims=True)
    pair = jnp.concatenate([top, bottom] * 4, axis=0)
    send_ref[...] = jnp.concatenate([pair] * (2 * LAYERS // 8), axis=0)


def assimilate_kernel(
    order_ref,
    place_ref,
    spread_ref,
    error_ref,
    forecast_ref,
    recv_ref,
    owner_ref,
    cell_ref,
    kind_ref,
    value_ref,
    mask_ref,
    out_ref,
    state_ref,
    pack_ref,
    left_ref,
    drive_ref,
    table_ref,
    spots_ref,
    weight_ref,
):
    place_x = place_ref[0]
    place_y = place_ref[1]
    upper = recv_ref[pl.ds(0, TILES, stride=2), :].T
    stretch = []
    for group in range(GROUPS):
        row = BATCHES * MEMBERS + group
        total = jnp.sum(upper[row : row + 1], axis=1, keepdims=True)
        mean_var = total * (1.0 / ((MEMBERS - 1) * float(NX * NY)))
        stretch.append(jnp.sqrt(spread_ref[group // 2, group % 2] / (mean_var + spread_floor)))
    for group in range(GROUPS):
        value = forecast_ref[group]
        centre = jnp.sum(value, axis=0, keepdims=True) * (1.0 / MEMBERS)
        state_ref[:, group * CELLS : (group + 1) * CELLS] = centre + stretch[group] * (value - centre)

    kinds, xs, ys, values = [], [], [], []
    sub = lax.broadcasted_iota(I32, (CY, OBS), 0)
    table_ref[...] = jnp.zeros_like(table_ref)
    table = jnp.zeros((CY, OBS), F32)
    columns, spots = [], []
    for turn in range(BATCHES):
        batch = order_ref[turn]
        owner = owner_ref[pl.ds(batch, 1), :]
        cell = cell_ref[pl.ds(batch, 1), :]
        kinds.append(kind_ref[pl.ds(batch, 1), :])
        values.append(value_ref[pl.ds(batch, 1), :])
        mask = mask_ref[pl.ds(batch, 1), :].astype(F32)
        xs.append(((owner >> 3) * CX + (cell >> 7)).astype(F32))
        ys.append(((owner & (TILES_Y - 1)) * CY + (cell & (CY - 1))).astype(F32))
        tile_x = owner >> 3
        columns.append(tile_x + REACH)
        for row, value in enumerate((xs[turn], ys[turn], mask, tile_x.astype(F32))):
            table = jnp.where(sub == turn * 4 + row, value, table)
        prior = upper[turn * MEMBERS : (turn + 1) * MEMBERS]
        centre = jnp.sum(prior, axis=0, keepdims=True) * (1.0 / MEMBERS)
        factor = jnp.where(kinds[turn] == 0, stretch[0], stretch[2])
        state_ref[:, AHEAD + turn * OBS : AHEAD + (turn + 1) * OBS] = centre + factor * (prior - centre)
        strip = ((tile_x >> 1) & 3) * 2 + ((owner >> 2) & 1)
        spots.append(strip * 8 + (tile_x & 1) * 4 + (owner & 3))
    for number, (turn, other) in enumerate(PAIRS):
        hot = jnp.where(sub == spots[other] + turn * HALF, 1.0, 0.0)
        spots_ref[:, number * OBS : (number + 1) * OBS] = hot.astype(BF16)
    table_ref[...] = table.T

    lane = lax.broadcasted_iota(I32, (1, CY), 1)
    cell_x = (place_x * CX).astype(F32)
    cell_y = (place_y * CY + lane).astype(F32)

    for turn in range(BATCHES):
        prior = state_ref[:, AHEAD + turn * OBS : AHEAD + (turn + 1) * OBS]
        error = jnp.where(kinds[turn] == 0, error_ref[0], error_ref[1])
        centre = jnp.sum(prior, axis=0, keepdims=True) * (1.0 / MEMBERS)
        deviation = prior - centre
        variance = jnp.sum(deviation * deviation, axis=0, keepdims=True) / (MEMBERS - 1)
        gain = (values[turn] - centre) / (variance + error)
        shrink = -1.0 / (jnp.sqrt(error * (error + variance)) + error + variance)
        drive_high, drive_low = halves(gain + shrink * deviation)
        drive_ref[:MEMBERS] = drive_high
        drive_ref[MEMBERS:] = drive_low
        scaled = deviation * (1.0 / (MEMBERS - 1))
        scaled_high = scaled.astype(BF16).astype(F32)
        scaled_low = scaled - scaled_high
        packed = jnp.concatenate(
            [scaled_high, scaled_high, scaled_low, jnp.zeros_like(scaled)], axis=0
        )
        left_ref[...] = packed.T.astype(BF16)

        later = list(range(turn + 1, BATCHES))
        blocks = [slice(group * CELLS, (group + 1) * CELLS) for group in range(GROUPS)]
        blocks += [slice(AHEAD + other * OBS, AHEAD + (other + 1) * OBS) for other in later]
        for cols in blocks:
            state = state_ref[:, cols]
            state_dev = state - jnp.sum(state, axis=0, keepdims=True) * (1.0 / MEMBERS)
            high, low = halves(state_dev)
            pack_ref[0:32, cols] = high
            pack_ref[32:64, cols] = low
            pack_ref[64:96, cols] = high
            pack_ref[96:128, cols] = jnp.zeros_like(high)

        @pl.loop(0, OBS // CHUNK)
        def _(step):
            start = pl.multiple_of(step * CHUNK, CHUNK)
            part = pl.ds(start, CHUNK)
            table = table_ref[part, :]
            x_col = table[:, turn * 4 : turn * 4 + 1]
            y_col = table[:, turn * 4 + 1 : turn * 4 + 2]
            mask_col = table[:, turn * 4 + 2 : turn * 4 + 3]
            gap_y = y_col - cell_y
            drop_y = gap_y * gap_y * (1.0 / (LOC_Y * LOC_Y))
            for x in range(CX):
                gap_x = jnp.abs(x_col - (cell_x + x))
                gap_x = jnp.minimum(gap_x, NX - gap_x)
                room = jnp.maximum((1.0 - gap_x * gap_x * (1.0 / (LOC_X * LOC_X))) - drop_y, 0.0)
                weight_ref[:, x * CY : (x + 1) * CY] = room * room * mask_col
            if later:
                column = table[:, turn * 4 + 3 : turn * 4 + 4].astype(I32)
                marks = recv_ref[pl.ds(2 * start + 1, CHUNK, stride=2), :].astype(BF16)
                for place, other in enumerate(later):
                    number = PAIRS.index((turn, other))
                    allowed = mm(marks, spots_ref[:, number * OBS : (number + 1) * OBS])
                    apart = (columns[other] - column) & (TILES_X - 1)
                    allowed = jnp.where(apart < SPAN, allowed, 0.0)
                    gap_x = jnp.abs(x_col - xs[other])
                    gap_x = jnp.minimum(gap_x, NX - gap_x)
                    gap_y = y_col - ys[other]
                    room = 1.0 - gap_x * gap_x * (1.0 / (LOC_X * LOC_X))
                    room = jnp.maximum(room - gap_y * gap_y * (1.0 / (LOC_Y * LOC_Y)), 0.0)
                    weight_ref[:, (place + 1) * OBS : (place + 2) * OBS] = room * room * allowed

            left = left_ref[part, :]
            drive = drive_ref[:, part]
            for number, cols in enumerate(blocks):
                at = max(0, number - GROUPS + 1) * OBS
                covariance = mm(left, pack_ref[:, cols]) * weight_ref[:, at : at + OBS]
                high, low = halves(covariance)
                both = mm(drive, high)
                rest = mm(drive[:MEMBERS], low)
                state_ref[:, cols] += both[:MEMBERS] + both[MEMBERS:] + rest

    for group in range(GROUPS):
        for x in range(CX):
            at = group * CELLS + x * CY
            out_ref[rows_of(group, x), :] = state_ref[:, at : at + CY]


def call(kernel, specs, outs, scratch=()):
    return pl.pallas_call(
        kernel,
        in_specs=specs,
        out_specs=[VMEM] * len(outs) if len(outs) > 1 else VMEM,
        out_shape=outs if len(outs) > 1 else outs[0],
        scratch_shapes=list(scratch),
        compiler_params=pltpu.CompilerParams(vmem_limit_bytes=48 * 1024 * 1024),
    )


def shape(*dims):
    return jax.ShapeDtypeStruct(dims, F32)


def shifted(value, axis, step, periodic):
    count = lax.axis_size(axis)
    pairs = [
        (source, (source + step) % count)
        for source in range(count)
        if periodic or 0 <= source + step < count
    ]
    return lax.ppermute(value, axis, pairs)


def local(
    ensemble,
    courant,
    target_spread,
    obs_error,
    obs_value,
    obs_owner,
    obs_cell,
    obs_kind,
    tile_mask,
    batch_order,
):
    place_x = lax.axis_index(GX)
    place_y = lax.axis_index(GY)
    relay = lax.axis_index(PLANE) * LAYERS + lax.axis_index(LAYER)
    place = jnp.stack([place_x, place_y, relay]).astype(I32)
    ens = ensemble.reshape(MEMBERS * GROUPS * CX, CY)
    mask = tile_mask.reshape(BATCHES, OBS)
    low, high = call(edges_kernel, [VMEM], [shape(2, OBS)] * 2)(ens)
    before = shifted(high, GY, 1, False)
    behind = shifted(low, GY, -1, False)
    own, left, right, send = call(
        spread_kernel,
        [SMEM] * 3 + [VMEM] * 7,
        [
            shape(GROUPS, MEMBERS, CELLS),
            shape(GROUPS, MEMBERS, 2 * CY),
            shape(GROUPS, MEMBERS, 2 * CY),
            shape(OBS, CY),
        ],
        [pltpu.VMEM((MEMBERS * GROUPS * CX, CY), F32)],
    )(
        batch_order,
        place,
        courant,
        ens,
        before,
        behind,
        obs_owner,
        obs_cell,
        obs_kind,
        mask,
    )
    from_left = shifted(right, GX, 1, True)
    from_right = shifted(left, GX, -1, True)
    recv = lax.all_to_all(send.reshape(PLANES, LAYERS, CY), PLANE, 0, 0)
    send = call(collect_kernel, [VMEM], [shape(2 * LAYERS, CY)])(recv.reshape(TILES, CY))
    recv = lax.all_to_all(send.reshape(LAYERS, 2, CY), LAYER, 0, 0)
    forecast, send = call(
        merge_kernel,
        [SMEM] * 3 + [VMEM] * 4,
        [shape(GROUPS, MEMBERS, CELLS), shape(2 * LAYERS, CY)],
    )(batch_order, place, obs_owner, own, from_left, from_right, recv.reshape(2 * LAYERS, CY))
    recv = lax.all_to_all(send.reshape(LAYERS, 2, CY), LAYER, 0, 0)
    send = jnp.broadcast_to(recv.reshape(1, 2 * LAYERS, CY), (PLANES, 2 * LAYERS, CY))
    recv = lax.all_to_all(send, PLANE, 0, 0)
    out = call(
        assimilate_kernel,
        [SMEM] * 4 + [VMEM] * 7,
        [shape(MEMBERS * GROUPS * CX, CY)],
        [
            pltpu.VMEM((MEMBERS, AHEAD + BATCHES * OBS), F32),
            pltpu.VMEM((CY, AHEAD + BATCHES * OBS), BF16),
            pltpu.VMEM((OBS, CY), BF16),
            pltpu.VMEM((2 * MEMBERS, OBS), BF16),
            pltpu.VMEM((OBS, CY), F32),
            pltpu.VMEM((CY, BATCHES * OBS), BF16),
            pltpu.VMEM((CHUNK, BATCHES * OBS), F32),
        ],
    )(
        batch_order,
        place,
        target_spread,
        obs_error,
        forecast,
        recv.reshape(2 * TILES, CY),
        obs_owner,
        obs_cell,
        obs_kind,
        obs_value,
        mask,
    )
    return out.reshape(ensemble.shape)


def solution(mesh):
    fine = Mesh(mesh.devices.reshape(4, 8, 2, 2, 4), ("x", "z_lo", "core", "z_hi", "y"))
    in_specs = (
        P(None, None, None, GX, GY),
        P(),
        P(),
        P(),
        P(),
        P(),
        P(),
        P(),
        P(None, GX, GY, None),
        P(),
    )
    out_specs = P(None, None, None, GX, GY)
    return jax.shard_map(local, mesh=fine, in_specs=in_specs, out_specs=out_specs, check_vma=False)
```

```python
import jax
import jax.numpy as jnp
from jax import lax
from jax.experimental import pallas as pl
from jax.experimental.pallas import tpu as pltpu
from jax.sharding import Mesh
from jax.sharding import PartitionSpec as P

MEMBERS = 32
GROUPS = 4
CX = 4
CY = 128
CELLS = CX * CY
OBS = 512
BATCHES = 3
STEPS = 2
TILES_X = 64
TILES_Y = 8
TILES = TILES_X * TILES_Y
NX = TILES_X * CX
NY = TILES_Y * CY
LOC_X = 12.0
LOC_Y = 512.0
REACH = 2
SPAN = 2 * REACH + 1
PLANES = 32
LAYERS = 16
HALF = CY // 2
RIM = 16
SLOT = TILES_X + RIM
VALUES = BATCHES * MEMBERS
WIDE = (CX + 4) * CY
GX = ("x", "z_lo", "core")
GY = ("z_hi", "y")
PLANE = ("x", "core", "y")
LAYER = ("z_lo", "z_hi")
CHUNK = 256
AHEAD = GROUPS * CELLS
PAIRS = ((0, 1), (0, 2), (1, 2))

diffuse_rate = 0.1
mixing_rate = 0.05
spread_floor = 1e-05

F32 = jnp.float32
BF16 = jnp.bfloat16
I32 = jnp.int32

VMEM = pl.BlockSpec(memory_space=pltpu.VMEM)
SMEM = pl.BlockSpec(memory_space=pltpu.SMEM)


def rows_of(group, x):
    return pl.ds(group * CX + x, MEMBERS, stride=GROUPS * CX)


def mm(a, b):
    return lax.dot_general(a, b, (((1,), (0,)), ((), ())), preferred_element_type=F32)


def halves(value):
    high = value.astype(BF16)
    return high, (value - high.astype(F32)).astype(BF16)


def thirds(value):
    high = value.astype(BF16)
    rest = value - high.astype(F32)
    middle = rest.astype(BF16)
    return high, middle, (rest - middle.astype(F32)).astype(BF16)


def advance(rows, courant_ref, keep):
    lowest = min(x for _, x in rows) - 1
    highest = max(x for _, x in rows) + 1
    width = 2 * CY
    after = {}
    for group in range(GROUPS):
        speed = courant_ref[group % 2]
        stay = 1.0 - speed - 4.0 * diffuse_rate - mixing_rate
        for x in range(lowest, highest + 1):
            terms = []
            if (group, x) in rows:
                here = rows[group, x]
                beside = pltpu.roll(here, 1, 1) + pltpu.roll(here, width - 1, 1)
                terms.append(stay * here + diffuse_rate * beside + mixing_rate * rows[group ^ 1, x])
            if (group, x - 1) in rows:
                terms.append((speed + diffuse_rate) * rows[group, x - 1])
            if (group, x + 1) in rows:
                terms.append(diffuse_rate * rows[group, x + 1])
            total = terms[0]
            for term in terms[1:]:
                total = total + term
            after[group, x] = total if keep is None else total * keep
    return after


def spread_kernel(
    order_ref,
    place_ref,
    courant_ref,
    ens_ref,
    owner_ref,
    cell_ref,
    kind_ref,
    mask_ref,
    tile_ref,
    send_ref,
):
    place_x = place_ref[0]
    place_y = place_ref[1]
    rows = {}
    for group in range(GROUPS):
        for x in range(CX):
            own = ens_ref[rows_of(group, x), :]
            rows[group, x] = jnp.concatenate([own, jnp.zeros_like(own)], axis=1)
    lane = lax.broadcasted_iota(I32, (1, 2 * CY), 1)
    below = (lane >= 3 * CY // 2) & (place_y == 0)
    above = (lane >= CY) & (lane < 3 * CY // 2) & (place_y == TILES_Y - 1)
    keep = jnp.where(below | above, 0.0, 1.0).astype(F32)
    rows = advance(rows, courant_ref, keep)
    rows = advance(rows, courant_ref, None)
    lane = lax.broadcasted_iota(I32, (MEMBERS, CY), 1)
    low = jnp.zeros((MEMBERS, CY), F32)
    high = jnp.zeros((MEMBERS, CY), F32)
    tile = {}
    for (group, x), value in rows.items():
        tile[group, x] = value[:, :CY]
        tile_ref[group, :, (x + 2) * CY : (x + 3) * CY] = tile[group, x]
        rim = value[:, CY:]
        at = group * 16 + (x + 2) * 2
        there = (lane >> 1) == at // 2
        low = jnp.where(there, pltpu.roll(rim, at + 2, 1), low)
        high = jnp.where(there, pltpu.roll(rim, at, 1) if at else rim, high)
    ground = jnp.concatenate(
        [
            jnp.concatenate([tile[2 * field, x] for x in range(-2, CX + 2)], axis=1)
            for field in range(2)
        ],
        axis=0,
    )
    parts = jnp.concatenate(thirds(ground), axis=0)
    rims = jnp.concatenate(thirds(low + pltpu.roll(high, HALF, 1)), axis=0)
    blocks = []
    masks = []
    for turn in range(BATCHES):
        batch = order_ref[turn]
        owner = owner_ref[pl.ds(batch, 1), :]
        cell = cell_ref[pl.ds(batch, 1), :]
        kind = kind_ref[pl.ds(batch, 1), :]
        masks.append(mask_ref[pl.ds(batch, 1), :].astype(F32))
        at_x = ((owner >> 3) - place_x) * CX + (cell >> 7) + 2
        at_x = at_x & (NX - 1)
        at_y = ((owner & (TILES_Y - 1)) - place_y) * CY + (cell & (CY - 1))
        seen = at_x < CX + 4
        index = jnp.where(seen & (at_y >= 0) & (at_y < CY), at_x * CY + at_y, -1)
        corner = kind * 32 + at_x * 2
        edge = jnp.where(seen & (at_y >= -2) & (at_y < 0), corner + at_y + 2, -1)
        edge = jnp.where(seen & (at_y >= CY) & (at_y < CY + 2), corner + at_y - CY + HALF, edge)
        picked = jnp.zeros((parts.shape[0], OBS), F32)
        for start in range(0, WIDE, CHUNK):
            spot = lax.broadcasted_iota(I32, (CHUNK, OBS), 0) + start
            hot = jnp.where(spot == index, 1.0, 0.0).astype(BF16)
            picked = picked + mm(parts[:, start : start + CHUNK], hot)
        picked = picked[0:64] + picked[64:128] + picked[128:192]
        spot = lax.broadcasted_iota(I32, (CY, OBS), 0)
        found = mm(rims, jnp.where(spot == edge, 1.0, 0.0).astype(BF16))
        found = found[0:32] + found[32:64] + found[64:96]
        blocks.append(jnp.where(kind == 0, picked[0:32], picked[32:64]) + found)
    sub = lax.broadcasted_iota(I32, (MEMBERS, OBS), 0)
    blocks.append(jnp.where(sub == 0, masks[0], jnp.where(sub == TILES_Y, masks[1], 0.0)))
    turned = jnp.concatenate(blocks, axis=0).T
    lane = lax.broadcasted_iota(I32, (RIM, CY), 1)
    low = jnp.where(lane < HALF, low[:RIM], pltpu.roll(low[RIM:], HALF, 1))
    high = jnp.where(lane < HALF, high[:RIM], pltpu.roll(high[RIM:], HALF, 1))
    for slot in range(TILES_Y):
        at = slot * SLOT
        send_ref[at : at + TILES_X, :] = turned[slot * TILES_X : (slot + 1) * TILES_X]
        after = jnp.where(place_y == slot - 1, 1.0, 0.0).astype(F32)
        before = jnp.where(place_y == slot + 1, 1.0, 0.0).astype(F32)
        send_ref[at + TILES_X : at + SLOT, :] = after * high + before * low


def collect_kernel(place_ref, recv_ref, tile_ref, own_ref, left_ref, right_ref, send_ref):
    place_y = place_ref[1]
    lane = lax.broadcasted_iota(I32, (TILES_X, CY), 1)
    total = jnp.zeros((TILES_X, CY), F32)
    for row in range(TILES_Y):
        rows = recv_ref[row * SLOT : row * SLOT + TILES_X, :]
        if row:
            marks = pltpu.roll(jnp.where(lane < VALUES, 0.0, rows), row, 1)
            rows = jnp.where(lane < VALUES, rows, marks)
        total = total + rows
    send_ref[...] = total

    def rim(row):
        start = pl.multiple_of(row * SLOT + TILES_X, RIM)
        rows = recv_ref[pl.ds(start, RIM), :]
        return jnp.concatenate([rows, pltpu.roll(rows, HALF, 1)], axis=0)

    below = rim(jnp.maximum(place_y - 1, 0))
    above = rim(jnp.minimum(place_y + 1, TILES_Y - 1))
    lane = lax.broadcasted_iota(I32, (MEMBERS, CY), 1)
    for group in range(GROUPS):
        for x in range(-2, CX + 2):
            at = group * 16 + (x + 2) * 2
            value = tile_ref[group, :, (x + 2) * CY : (x + 3) * CY]
            first = pltpu.roll(below, CY - at, 1) if at else below
            value = value + jnp.where(lane < 2, first, 0.0)
            value = value + jnp.where(lane >= CY - 2, pltpu.roll(above, CY - 2 - at, 1), 0.0)
            if x < 0:
                left_ref[group, :, (x + 2) * CY : (x + 3) * CY] = value
            elif x < CX:
                own_ref[group, :, x * CY : (x + 1) * CY] = value
            else:
                right_ref[group, :, (x - CX) * CY : (x - CX + 1) * CY] = value


def merge_kernel(
    order_ref,
    place_ref,
    relay_ref,
    own_ref,
    from_left_ref,
    from_right_ref,
    recv_ref,
    forecast_ref,
    send_ref,
):
    relay = place_ref[1] * TILES_X + place_ref[0]
    lane = lax.broadcasted_iota(I32, (1, CY), 1)
    recv = recv_ref[...]
    top = jnp.sum(recv, axis=0, keepdims=True)
    top = jnp.where(lane < VALUES, top, 0.0)
    for group in range(GROUPS):
        own = own_ref[group]
        value = jnp.concatenate(
            [
                own[:, : 2 * CY] + from_left_ref[group],
                own[:, 2 * CY :] + from_right_ref[group],
            ],
            axis=1,
        )
        forecast_ref[group] = value
        centre = jnp.sum(value, axis=0, keepdims=True) * (1.0 / MEMBERS)
        deviation = value - centre
        total = jnp.sum(jnp.sum(deviation * deviation, axis=0, keepdims=True), axis=1, keepdims=True)
        top = jnp.where(lane == BATCHES * MEMBERS + group, total, top)

    lanes = lax.broadcasted_iota(I32, (TILES_X, CY), 1)
    tile_x = lax.broadcasted_iota(I32, (TILES_X, CY), 0)
    first = relay_ref[order_ref[0], relay] >> 3
    second = relay_ref[order_ref[1], relay] >> 3
    column = jnp.where(lanes < VALUES + TILES_Y, first, second)
    near = ((tile_x - column + REACH) & (TILES_X - 1)) < SPAN
    marks = jnp.where(near, recv, 0.0)
    folded = marks[0:8]
    for start in range(8, TILES_X, 8):
        folded = folded + marks[start : start + 8]
    lanes = lax.broadcasted_iota(I32, (8, CY), 1)
    subs = lax.broadcasted_iota(I32, (8, CY), 0)
    bottom = jnp.zeros((8, CY), F32)
    for row in range(8):
        for turn in range(2):
            step = turn * HALF + row * TILES_Y - VALUES - turn * TILES_Y
            moved = pltpu.roll(folded, step % CY, 1) if step % CY else folded
            there = (subs == row) & ((lanes >> 3) == turn * 8 + row)
            bottom = jnp.where(there, moved, bottom)
    bottom = jnp.sum(bottom, axis=0, keepdims=True)
    pair = jnp.concatenate([top, bottom] * 4, axis=0)
    send_ref[...] = jnp.concatenate([pair] * (2 * LAYERS // 8), axis=0)


def assimilate_kernel(
    order_ref,
    place_ref,
    spread_ref,
    error_ref,
    forecast_ref,
    recv_ref,
    owner_ref,
    cell_ref,
    kind_ref,
    value_ref,
    mask_ref,
    out_ref,
    state_ref,
    pack_ref,
    left_ref,
    drive_ref,
    table_ref,
    spots_ref,
    weight_ref,
    rows_ref,
):
    place_x = place_ref[0]
    place_y = place_ref[1]
    for x in range(4):
        for core in range(2):
            for y in range(4):
                for z_hi in range(2):
                    source = 2 * (x * 128 + core * 64 + y * 16 + z_hi)
                    target = z_hi * 256 + y * 64 + x * 16 + core
                    for half in range(2):
                        rows = recv_ref[pl.ds(source + half, 8, stride=4), :]
                        rows_ref[pl.ds(half * OBS + target, 8, stride=2), :] = rows
    upper = rows_ref[:OBS].T
    stretch = []
    for group in range(GROUPS):
        row = BATCHES * MEMBERS + group
        total = jnp.sum(upper[row : row + 1], axis=1, keepdims=True)
        mean_var = total * (1.0 / ((MEMBERS - 1) * float(NX * NY)))
        stretch.append(jnp.sqrt(spread_ref[group // 2, group % 2] / (mean_var + spread_floor)))
    for group in range(GROUPS):
        value = forecast_ref[group]
        centre = jnp.sum(value, axis=0, keepdims=True) * (1.0 / MEMBERS)
        state_ref[:, group * CELLS : (group + 1) * CELLS] = centre + stretch[group] * (value - centre)

    kinds, xs, ys, values = [], [], [], []
    sub = lax.broadcasted_iota(I32, (CY, OBS), 0)
    table_ref[...] = jnp.zeros_like(table_ref)
    table = jnp.zeros((CY, OBS), F32)
    columns, spots = [], []
    for turn in range(BATCHES):
        batch = order_ref[turn]
        owner = owner_ref[pl.ds(batch, 1), :]
        cell = cell_ref[pl.ds(batch, 1), :]
        kinds.append(kind_ref[pl.ds(batch, 1), :])
        values.append(value_ref[pl.ds(batch, 1), :])
        mask = mask_ref[pl.ds(batch, 1), :].astype(F32)
        xs.append(((owner >> 3) * CX + (cell >> 7)).astype(F32))
        ys.append(((owner & (TILES_Y - 1)) * CY + (cell & (CY - 1))).astype(F32))
        tile_x = owner >> 3
        columns.append(tile_x + REACH)
        for row, value in enumerate((xs[turn], ys[turn], mask, tile_x.astype(F32))):
            table = jnp.where(sub == turn * 4 + row, value, table)
        prior = upper[turn * MEMBERS : (turn + 1) * MEMBERS]
        centre = jnp.sum(prior, axis=0, keepdims=True) * (1.0 / MEMBERS)
        factor = jnp.where(kinds[turn] == 0, stretch[0], stretch[2])
        state_ref[:, AHEAD + turn * OBS : AHEAD + (turn + 1) * OBS] = centre + factor * (prior - centre)
        spots.append((tile_x & 7) * TILES_Y + (owner & (TILES_Y - 1)))
    for number, (turn, other) in enumerate(PAIRS):
        hot = jnp.where(sub == spots[other] + turn * HALF, 1.0, 0.0)
        spots_ref[:, number * OBS : (number + 1) * OBS] = hot.astype(BF16)
    table_ref[...] = table.T

    lane = lax.broadcasted_iota(I32, (1, CY), 1)
    cell_x = (place_x * CX).astype(F32)
    cell_y = (place_y * CY + lane).astype(F32)

    for turn in range(BATCHES):
        prior = state_ref[:, AHEAD + turn * OBS : AHEAD + (turn + 1) * OBS]
        error = jnp.where(kinds[turn] == 0, error_ref[0], error_ref[1])
        centre = jnp.sum(prior, axis=0, keepdims=True) * (1.0 / MEMBERS)
        deviation = prior - centre
        variance = jnp.sum(deviation * deviation, axis=0, keepdims=True) / (MEMBERS - 1)
        gain = (values[turn] - centre) / (variance + error)
        shrink = -1.0 / (jnp.sqrt(error * (error + variance)) + error + variance)
        drive_high, drive_low = halves(gain + shrink * deviation)
        drive_ref[:MEMBERS] = drive_high
        drive_ref[MEMBERS:] = drive_low
        scaled = deviation * (1.0 / (MEMBERS - 1))
        scaled_high = scaled.astype(BF16).astype(F32)
        scaled_low = scaled - scaled_high
        packed = jnp.concatenate(
            [scaled_high, scaled_high, scaled_low, jnp.zeros_like(scaled)], axis=0
        )
        left_ref[...] = packed.T.astype(BF16)

        later = list(range(turn + 1, BATCHES))
        blocks = [slice(group * CELLS, (group + 1) * CELLS) for group in range(GROUPS)]
        blocks += [slice(AHEAD + other * OBS, AHEAD + (other + 1) * OBS) for other in later]
        for cols in blocks:
            state = state_ref[:, cols]
            state_dev = state - jnp.sum(state, axis=0, keepdims=True) * (1.0 / MEMBERS)
            high, low = halves(state_dev)
            pack_ref[0:32, cols] = high
            pack_ref[32:64, cols] = low
            pack_ref[64:96, cols] = high
            pack_ref[96:128, cols] = jnp.zeros_like(high)

        @pl.loop(0, OBS // CHUNK)
        def _(step):
            start = pl.multiple_of(step * CHUNK, CHUNK)
            part = pl.ds(start, CHUNK)
            table = table_ref[part, :]
            x_col = table[:, turn * 4 : turn * 4 + 1]
            y_col = table[:, turn * 4 + 1 : turn * 4 + 2]
            mask_col = table[:, turn * 4 + 2 : turn * 4 + 3]
            gap_y = y_col - cell_y
            drop_y = gap_y * gap_y * (1.0 / (LOC_Y * LOC_Y))
            for x in range(CX):
                gap_x = jnp.abs(x_col - (cell_x + x))
                gap_x = jnp.minimum(gap_x, NX - gap_x)
                room = jnp.maximum((1.0 - gap_x * gap_x * (1.0 / (LOC_X * LOC_X))) - drop_y, 0.0)
                weight_ref[:, x * CY : (x + 1) * CY] = room * room * mask_col
            if later:
                column = table[:, turn * 4 + 3 : turn * 4 + 4].astype(I32)
                marks = rows_ref[pl.ds(OBS + start, CHUNK), :].astype(BF16)
                for place, other in enumerate(later):
                    number = PAIRS.index((turn, other))
                    allowed = mm(marks, spots_ref[:, number * OBS : (number + 1) * OBS])
                    apart = (columns[other] - column) & (TILES_X - 1)
                    allowed = jnp.where(apart < SPAN, allowed, 0.0)
                    gap_x = jnp.abs(x_col - xs[other])
                    gap_x = jnp.minimum(gap_x, NX - gap_x)
                    gap_y = y_col - ys[other]
                    room = 1.0 - gap_x * gap_x * (1.0 / (LOC_X * LOC_X))
                    room = jnp.maximum(room - gap_y * gap_y * (1.0 / (LOC_Y * LOC_Y)), 0.0)
                    weight_ref[:, (place + 1) * OBS : (place + 2) * OBS] = room * room * allowed

            left = left_ref[part, :]
            drive = drive_ref[:, part]
            for number, cols in enumerate(blocks):
                at = max(0, number - GROUPS + 1) * OBS
                covariance = mm(left, pack_ref[:, cols]) * weight_ref[:, at : at + OBS]
                high, low = halves(covariance)
                both = mm(drive, high)
                rest = mm(drive[:MEMBERS], low)
                state_ref[:, cols] += both[:MEMBERS] + both[MEMBERS:] + rest

    for group in range(GROUPS):
        for x in range(CX):
            at = group * CELLS + x * CY
            out_ref[rows_of(group, x), :] = state_ref[:, at : at + CY]


def call(kernel, specs, outs, scratch=()):
    return pl.pallas_call(
        kernel,
        in_specs=specs,
        out_specs=[VMEM] * len(outs) if len(outs) > 1 else VMEM,
        out_shape=outs if len(outs) > 1 else outs[0],
        scratch_shapes=list(scratch),
        compiler_params=pltpu.CompilerParams(vmem_limit_bytes=48 * 1024 * 1024),
    )


def shape(*dims):
    return jax.ShapeDtypeStruct(dims, F32)


def shifted(value, axis, step, periodic):
    count = lax.axis_size(axis)
    pairs = [
        (source, (source + step) % count)
        for source in range(count)
        if periodic or 0 <= source + step < count
    ]
    return lax.ppermute(value, axis, pairs)


def local(
    ensemble,
    courant,
    target_spread,
    obs_error,
    obs_value,
    obs_owner,
    obs_cell,
    obs_kind,
    tile_mask,
    batch_order,
):
    place_x = lax.axis_index(GX)
    place_y = lax.axis_index(GY)
    place = jnp.stack([place_x, place_y]).astype(I32)
    ens = ensemble.reshape(MEMBERS * GROUPS * CX, CY)
    mask = tile_mask.reshape(BATCHES, OBS)
    tile, send = call(
        spread_kernel,
        [SMEM] * 3 + [VMEM] * 5,
        [shape(GROUPS, MEMBERS, WIDE), shape(TILES_Y * SLOT, CY)],
    )(batch_order, place, courant, ens, obs_owner, obs_cell, obs_kind, mask)
    recv = lax.all_to_all(send.reshape(TILES_Y, SLOT, CY), GY, 0, 0)
    own, left, right, send = call(
        collect_kernel,
        [SMEM] + [VMEM] * 2,
        [
            shape(GROUPS, MEMBERS, CELLS),
            shape(GROUPS, MEMBERS, 2 * CY),
            shape(GROUPS, MEMBERS, 2 * CY),
            shape(TILES_X, CY),
        ],
    )(place, recv.reshape(TILES_Y * SLOT, CY), tile)
    from_left = shifted(right, GX, 1, True)
    from_right = shifted(left, GX, -1, True)
    recv = lax.all_to_all(send.reshape(TILES_X, 1, CY), GX, 0, 0)
    forecast, send = call(
        merge_kernel,
        [SMEM] * 3 + [VMEM] * 4,
        [shape(GROUPS, MEMBERS, CELLS), shape(2 * LAYERS, CY)],
    )(batch_order, place, obs_owner, own, from_left, from_right, recv.reshape(TILES_X, CY))
    recv = lax.all_to_all(send.reshape(LAYERS, 2, CY), LAYER, 0, 0)
    send = jnp.broadcast_to(recv.reshape(1, 2 * LAYERS, CY), (PLANES, 2 * LAYERS, CY))
    recv = lax.all_to_all(send, PLANE, 0, 0)
    out = call(
        assimilate_kernel,
        [SMEM] * 4 + [VMEM] * 7,
        [shape(MEMBERS * GROUPS * CX, CY)],
        [
            pltpu.VMEM((MEMBERS, AHEAD + BATCHES * OBS), F32),
            pltpu.VMEM((CY, AHEAD + BATCHES * OBS), BF16),
            pltpu.VMEM((OBS, CY), BF16),
            pltpu.VMEM((2 * MEMBERS, OBS), BF16),
            pltpu.VMEM((OBS, CY), F32),
            pltpu.VMEM((CY, BATCHES * OBS), BF16),
            pltpu.VMEM((CHUNK, BATCHES * OBS), F32),
            pltpu.VMEM((2 * OBS, CY), F32),
        ],
    )(
        batch_order,
        place,
        target_spread,
        obs_error,
        forecast,
        recv.reshape(2 * TILES, CY),
        obs_owner,
        obs_cell,
        obs_kind,
        obs_value,
        mask,
    )
    return out.reshape(ensemble.shape)


def solution(mesh):
    fine = Mesh(mesh.devices.reshape(4, 8, 2, 2, 4), ("x", "z_lo", "core", "z_hi", "y"))
    in_specs = (
        P(None, None, None, GX, GY),
        P(),
        P(),
        P(),
        P(),
        P(),
        P(),
        P(),
        P(None, GX, GY, None),
        P(),
    )
    out_specs = P(None, None, None, GX, GY)
    return jax.shard_map(local, mesh=fine, in_specs=in_specs, out_specs=out_specs, check_vma=False)
```

```python
import jax
import jax.numpy as jnp
from jax import lax
from jax.experimental import pallas as pl
from jax.experimental.pallas import tpu as pltpu
from jax.sharding import Mesh
from jax.sharding import PartitionSpec as P

MEMBERS = 32
GROUPS = 4
CX = 4
CY = 128
CELLS = CX * CY
OBS = 512
BATCHES = 3
STEPS = 2
TILES_X = 64
TILES_Y = 8
TILES = TILES_X * TILES_Y
NX = TILES_X * CX
NY = TILES_Y * CY
LOC_X = 12.0
LOC_Y = 512.0
REACH = 2
SPAN = 2 * REACH + 1
PLANES = 32
LAYERS = 16
HALF = CY // 2
RIM = 16
VALUES = BATCHES * MEMBERS
WIDE = (CX + 4) * CY
SIDE = 2 * GROUPS * MEMBERS
GX = ("x", "z_lo", "core")
GY = ("z_hi", "y")
PLANE = ("x", "core", "y")
LAYER = ("z_lo", "z_hi")
CHUNK = 256
AHEAD = GROUPS * CELLS
PAIRS = ((0, 1), (0, 2), (1, 2))

diffuse_rate = 0.1
mixing_rate = 0.05
spread_floor = 1e-05

F32 = jnp.float32
BF16 = jnp.bfloat16
I32 = jnp.int32

VMEM = pl.BlockSpec(memory_space=pltpu.VMEM)
SMEM = pl.BlockSpec(memory_space=pltpu.SMEM)


def rows_of(group, x):
    return pl.ds(group * CX + x, MEMBERS, stride=GROUPS * CX)


def mm(a, b):
    return lax.dot_general(a, b, (((1,), (0,)), ((), ())), preferred_element_type=F32)


def halves(value):
    high = value.astype(BF16)
    return high, (value - high.astype(F32)).astype(BF16)


def thirds(value):
    high = value.astype(BF16)
    rest = value - high.astype(F32)
    middle = rest.astype(BF16)
    return high, middle, (rest - middle.astype(F32)).astype(BF16)


def advance(rows, courant_ref, keep):
    lowest = min(x for _, x in rows) - 1
    highest = max(x for _, x in rows) + 1
    width = 2 * CY
    after = {}
    for group in range(GROUPS):
        speed = courant_ref[group % 2]
        stay = 1.0 - speed - 4.0 * diffuse_rate - mixing_rate
        for x in range(lowest, highest + 1):
            terms = []
            if (group, x) in rows:
                here = rows[group, x]
                beside = pltpu.roll(here, 1, 1) + pltpu.roll(here, width - 1, 1)
                terms.append(stay * here + diffuse_rate * beside + mixing_rate * rows[group ^ 1, x])
            if (group, x - 1) in rows:
                terms.append((speed + diffuse_rate) * rows[group, x - 1])
            if (group, x + 1) in rows:
                terms.append(diffuse_rate * rows[group, x + 1])
            total = terms[0]
            for term in terms[1:]:
                total = total + term
            after[group, x] = total if keep is None else total * keep
    return after


def spread_kernel(
    order_ref,
    place_ref,
    courant_ref,
    ens_ref,
    owner_ref,
    cell_ref,
    kind_ref,
    mask_ref,
    own_ref,
    rim_ref,
    first_ref,
    second_ref,
    send_ref,
):
    place_x = place_ref[0]
    place_y = place_ref[1]
    rows = {}
    for group in range(GROUPS):
        for x in range(CX):
            own = ens_ref[rows_of(group, x), :]
            rows[group, x] = jnp.concatenate([own, jnp.zeros_like(own)], axis=1)
    lane = lax.broadcasted_iota(I32, (1, 2 * CY), 1)
    below = (lane >= 3 * CY // 2) & (place_y == 0)
    above = (lane >= CY) & (lane < 3 * CY // 2) & (place_y == TILES_Y - 1)
    keep = jnp.where(below | above, 0.0, 1.0).astype(F32)
    rows = advance(rows, courant_ref, keep)
    rows = advance(rows, courant_ref, None)
    lane = lax.broadcasted_iota(I32, (MEMBERS, CY), 1)
    low = jnp.zeros((MEMBERS, CY), F32)
    high = jnp.zeros((MEMBERS, CY), F32)
    tile = {}
    for (group, x), value in rows.items():
        tile[group, x] = value[:, :CY]
        if 0 <= x < CX:
            own_ref[group, :, x * CY : (x + 1) * CY] = tile[group, x]
        edge = value[:, CY:]
        at = group * 16 + (x + 2) * 2
        there = (lane >> 1) == at // 2
        low = jnp.where(there, pltpu.roll(edge, at + 2, 1), low)
        high = jnp.where(there, pltpu.roll(edge, at, 1) if at else edge, high)
    rim = low + pltpu.roll(high, HALF, 1)
    rim_ref[...] = rim
    first_ref[SIDE:] = rim
    second_ref[SIDE:] = rim
    even = (place_x & 1) == 0
    for group in range(GROUPS):
        for x in range(2):
            at = (group * 2 + x) * MEMBERS
            first_ref[at : at + MEMBERS] = jnp.where(even, tile[group, CX + x], tile[group, x - 2])
            second_ref[at : at + MEMBERS] = jnp.where(even, tile[group, x - 2], tile[group, CX + x])
    ground = jnp.concatenate(
        [
            jnp.concatenate([tile[2 * field, x] for x in range(-2, CX + 2)], axis=1)
            for field in range(2)
        ],
        axis=0,
    )
    parts = jnp.concatenate(thirds(ground), axis=0)
    rims = jnp.concatenate(thirds(rim), axis=0)
    blocks = []
    masks = []
    for turn in range(BATCHES):
        batch = order_ref[turn]
        owner = owner_ref[pl.ds(batch, 1), :]
        cell = cell_ref[pl.ds(batch, 1), :]
        kind = kind_ref[pl.ds(batch, 1), :]
        masks.append(mask_ref[pl.ds(batch, 1), :].astype(F32))
        at_x = ((owner >> 3) - place_x) * CX + (cell >> 7) + 2
        at_x = at_x & (NX - 1)
        at_y = ((owner & (TILES_Y - 1)) - place_y) * CY + (cell & (CY - 1))
        seen = at_x < CX + 4
        index = jnp.where(seen & (at_y >= 0) & (at_y < CY), at_x * CY + at_y, -1)
        corner = kind * 32 + at_x * 2
        edge = jnp.where(seen & (at_y >= -2) & (at_y < 0), corner + at_y + 2, -1)
        edge = jnp.where(seen & (at_y >= CY) & (at_y < CY + 2), corner + at_y - CY + HALF, edge)
        picked = jnp.zeros((parts.shape[0], OBS), F32)
        for start in range(0, WIDE, CHUNK):
            spot = lax.broadcasted_iota(I32, (CHUNK, OBS), 0) + start
            hot = jnp.where(spot == index, 1.0, 0.0).astype(BF16)
            picked = picked + mm(parts[:, start : start + CHUNK], hot)
        picked = picked[0:64] + picked[64:128] + picked[128:192]
        spot = lax.broadcasted_iota(I32, (CY, OBS), 0)
        found = mm(rims, jnp.where(spot == edge, 1.0, 0.0).astype(BF16))
        found = found[0:32] + found[32:64] + found[64:96]
        blocks.append(jnp.where(kind == 0, picked[0:32], picked[32:64]) + found)
    sub = lax.broadcasted_iota(I32, (MEMBERS, OBS), 0)
    blocks.append(jnp.where(sub == 0, masks[0], jnp.where(sub == 1, masks[1], 0.0)))
    send_ref[...] = jnp.concatenate(blocks, axis=0).T


def collect_kernel(
    place_ref,
    recv_ref,
    own_ref,
    rim_ref,
    first_ref,
    second_ref,
    joined_ref,
    third_ref,
    fourth_ref,
    send_ref,
):
    even = (place_ref[0] & 1) == 0
    for group in range(GROUPS):
        for x in range(CX):
            at = (group * 2 + x % 2) * MEMBERS
            part = slice(at, at + MEMBERS)
            near = first_ref[part], second_ref[part]
            other = jnp.where(even, near[1], near[0]) if x < 2 else jnp.where(even, near[0], near[1])
            cells = slice(x * CY, (x + 1) * CY)
            joined_ref[group, :, cells] = own_ref[group, :, cells] + other
    lane = lax.broadcasted_iota(I32, (MEMBERS, CY), 1)
    from_left = pltpu.roll(jnp.where(even, second_ref[SIDE:], first_ref[SIDE:]), CY - 8, 1)
    from_right = pltpu.roll(jnp.where(even, first_ref[SIDE:], second_ref[SIDE:]), 8, 1)
    rim = rim_ref[...] + jnp.where((lane & 15) < 8, from_left, from_right)
    lane = lax.broadcasted_iota(I32, (RIM, CY), 1)
    low = jnp.where(lane < HALF, rim[:RIM], pltpu.roll(rim[RIM:], HALF, 1))
    high = jnp.where(lane < HALF, pltpu.roll(rim[:RIM], HALF, 1), rim[RIM:])
    even = (place_ref[1] & 1) == 0
    third_ref[...] = jnp.where(even, high, low)
    fourth_ref[...] = jnp.where(even, low, high)
    lane = lax.broadcasted_iota(I32, (LAYERS, CY), 1)
    total = jnp.zeros((LAYERS, CY), F32)
    marks = jnp.zeros((LAYERS, CY), F32)
    for plane in range(PLANES):
        rows = recv_ref[plane * LAYERS : (plane + 1) * LAYERS, :]
        total = total + rows
        for turn in range(2):
            at = BATCHES * MEMBERS + turn
            marks = jnp.where(lane == turn * PLANES + plane, rows[:, at : at + 1], marks)
    send_ref[pl.ds(0, LAYERS, stride=2), :] = total
    send_ref[pl.ds(1, LAYERS, stride=2), :] = marks


def merge_kernel(
    order_ref,
    place_ref,
    relay_ref,
    joined_ref,
    third_ref,
    fourth_ref,
    recv_ref,
    forecast_ref,
    send_ref,
):
    relay = place_ref[2]
    lane = lax.broadcasted_iota(I32, (1, CY), 1)
    top = jnp.sum(recv_ref[pl.ds(0, LAYERS, stride=2), :], axis=0, keepdims=True)
    top = jnp.where(lane < BATCHES * MEMBERS, top, 0.0)
    even = (place_ref[1] & 1) == 0
    below = jnp.where(even, fourth_ref[...], third_ref[...])
    above = jnp.where(even, third_ref[...], fourth_ref[...])
    below = jnp.concatenate([below, pltpu.roll(below, HALF, 1)], axis=0)
    above = jnp.concatenate([above, pltpu.roll(above, HALF, 1)], axis=0)
    wide = lax.broadcasted_iota(I32, (MEMBERS, CY), 1)
    for group in range(GROUPS):
        pieces = []
        for x in range(CX):
            at = group * 16 + (x + 2) * 2
            piece = joined_ref[group, :, x * CY : (x + 1) * CY]
            piece = piece + jnp.where(wide < 2, pltpu.roll(below, CY - at, 1), 0.0)
            piece = piece + jnp.where(wide >= CY - 2, pltpu.roll(above, CY - 2 - at, 1), 0.0)
            pieces.append(piece)
        value = jnp.concatenate(pieces, axis=1)
        forecast_ref[group] = value
        centre = jnp.sum(value, axis=0, keepdims=True) * (1.0 / MEMBERS)
        deviation = value - centre
        total = jnp.sum(jnp.sum(deviation * deviation, axis=0, keepdims=True), axis=1, keepdims=True)
        top = jnp.where(lane == BATCHES * MEMBERS + group, total, top)

    marks = recv_ref[pl.ds(1, LAYERS, stride=2), :]
    lanes = lax.broadcasted_iota(I32, (LAYERS, CY), 1)
    subs = lax.broadcasted_iota(I32, (LAYERS, CY), 0)
    tile_x = ((lanes >> 3) & 3) * 16 + (subs >> 1) * 2 + ((lanes >> 2) & 1)
    first = relay_ref[order_ref[0], relay] >> 3
    second = relay_ref[order_ref[1], relay] >> 3
    column = jnp.where(lanes < PLANES, first, second)
    near = ((tile_x - column + REACH) & (TILES_X - 1)) < SPAN
    marks = jnp.where(near & (lanes < 2 * PLANES), marks, 0.0)
    marks = marks[:8] + marks[8:]
    folded = marks
    for step in (8, 16, 24):
        folded = folded + pltpu.roll(marks, CY - step, 1)
    lanes = lax.broadcasted_iota(I32, (8, CY), 1)
    subs = lax.broadcasted_iota(I32, (8, CY), 0)
    bottom = jnp.zeros((8, CY), F32)
    for row in range(8):
        for turn in range(2):
            moved = pltpu.roll(folded, (turn * PLANES + row * 8) % CY, 1)
            there = (subs == row) & ((lanes >> 3) == turn * 8 + row)
            bottom = jnp.where(there, moved, bottom)
    bottom = jnp.sum(bottom, axis=0, keepdims=True)
    pair = jnp.concatenate([top, bottom] * 4, axis=0)
    send_ref[...] = jnp.concatenate([pair] * (2 * LAYERS // 8), axis=0)


def assimilate_kernel(
    order_ref,
    place_ref,
    spread_ref,
    error_ref,
    forecast_ref,
    recv_ref,
    owner_ref,
    cell_ref,
    kind_ref,
    value_ref,
    mask_ref,
    out_ref,
    state_ref,
    pack_ref,
    left_ref,
    drive_ref,
    table_ref,
    spots_ref,
    weight_ref,
):
    place_x = place_ref[0]
    place_y = place_ref[1]
    upper = recv_ref[pl.ds(0, TILES, stride=2), :].T
    stretch = []
    for group in range(GROUPS):
        row = BATCHES * MEMBERS + group
        total = jnp.sum(upper[row : row + 1], axis=1, keepdims=True)
        mean_var = total * (1.0 / ((MEMBERS - 1) * float(NX * NY)))
        stretch.append(jnp.sqrt(spread_ref[group // 2, group % 2] / (mean_var + spread_floor)))
    for group in range(GROUPS):
        value = forecast_ref[group]
        centre = jnp.sum(value, axis=0, keepdims=True) * (1.0 / MEMBERS)
        state_ref[:, group * CELLS : (group + 1) * CELLS] = centre + stretch[group] * (value - centre)

    kinds, xs, ys, values = [], [], [], []
    sub = lax.broadcasted_iota(I32, (CY, OBS), 0)
    table_ref[...] = jnp.zeros_like(table_ref)
    table = jnp.zeros((CY, OBS), F32)
    columns, spots = [], []
    for turn in range(BATCHES):
        batch = order_ref[turn]
        owner = owner_ref[pl.ds(batch, 1), :]
        cell = cell_ref[pl.ds(batch, 1), :]
        kinds.append(kind_ref[pl.ds(batch, 1), :])
        values.append(value_ref[pl.ds(batch, 1), :])
        mask = mask_ref[pl.ds(batch, 1), :].astype(F32)
        xs.append(((owner >> 3) * CX + (cell >> 7)).astype(F32))
        ys.append(((owner & (TILES_Y - 1)) * CY + (cell & (CY - 1))).astype(F32))
        tile_x = owner >> 3
        columns.append(tile_x + REACH)
        for row, value in enumerate((xs[turn], ys[turn], mask, tile_x.astype(F32))):
            table = jnp.where(sub == turn * 4 + row, value, table)
        prior = upper[turn * MEMBERS : (turn + 1) * MEMBERS]
        centre = jnp.sum(prior, axis=0, keepdims=True) * (1.0 / MEMBERS)
        factor = jnp.where(kinds[turn] == 0, stretch[0], stretch[2])
        state_ref[:, AHEAD + turn * OBS : AHEAD + (turn + 1) * OBS] = centre + factor * (prior - centre)
        strip = ((tile_x >> 1) & 3) * 2 + ((owner >> 2) & 1)
        spots.append(strip * 8 + (tile_x & 1) * 4 + (owner & 3))
    for number, (turn, other) in enumerate(PAIRS):
        hot = jnp.where(sub == spots[other] + turn * HALF, 1.0, 0.0)
        spots_ref[:, number * OBS : (number + 1) * OBS] = hot.astype(BF16)
    table_ref[...] = table.T

    lane = lax.broadcasted_iota(I32, (1, CY), 1)
    cell_x = (place_x * CX).astype(F32)
    cell_y = (place_y * CY + lane).astype(F32)

    for turn in range(BATCHES):
        prior = state_ref[:, AHEAD + turn * OBS : AHEAD + (turn + 1) * OBS]
        error = jnp.where(kinds[turn] == 0, error_ref[0], error_ref[1])
        centre = jnp.sum(prior, axis=0, keepdims=True) * (1.0 / MEMBERS)
        deviation = prior - centre
        variance = jnp.sum(deviation * deviation, axis=0, keepdims=True) / (MEMBERS - 1)
        gain = (values[turn] - centre) / (variance + error)
        shrink = -1.0 / (jnp.sqrt(error * (error + variance)) + error + variance)
        drive_high, drive_low = halves(gain + shrink * deviation)
        drive_ref[:MEMBERS] = drive_high
        drive_ref[MEMBERS:] = drive_low
        scaled = deviation * (1.0 / (MEMBERS - 1))
        scaled_high = scaled.astype(BF16).astype(F32)
        scaled_low = scaled - scaled_high
        packed = jnp.concatenate(
            [scaled_high, scaled_high, scaled_low, jnp.zeros_like(scaled)], axis=0
        )
        left_ref[...] = packed.T.astype(BF16)

        later = list(range(turn + 1, BATCHES))
        blocks = [slice(group * CELLS, (group + 1) * CELLS) for group in range(GROUPS)]
        blocks += [slice(AHEAD + other * OBS, AHEAD + (other + 1) * OBS) for other in later]
        for cols in blocks:
            state = state_ref[:, cols]
            state_dev = state - jnp.sum(state, axis=0, keepdims=True) * (1.0 / MEMBERS)
            high, low = halves(state_dev)
            pack_ref[0:32, cols] = high
            pack_ref[32:64, cols] = low
            pack_ref[64:96, cols] = high
            pack_ref[96:128, cols] = jnp.zeros_like(high)

        @pl.loop(0, OBS // CHUNK)
        def _(step):
            start = pl.multiple_of(step * CHUNK, CHUNK)
            part = pl.ds(start, CHUNK)
            table = table_ref[part, :]
            x_col = table[:, turn * 4 : turn * 4 + 1]
            y_col = table[:, turn * 4 + 1 : turn * 4 + 2]
            mask_col = table[:, turn * 4 + 2 : turn * 4 + 3]
            gap_y = y_col - cell_y
            drop_y = gap_y * gap_y * (1.0 / (LOC_Y * LOC_Y))
            for x in range(CX):
                gap_x = jnp.abs(x_col - (cell_x + x))
                gap_x = jnp.minimum(gap_x, NX - gap_x)
                room = jnp.maximum((1.0 - gap_x * gap_x * (1.0 / (LOC_X * LOC_X))) - drop_y, 0.0)
                weight_ref[:, x * CY : (x + 1) * CY] = room * room * mask_col
            if later:
                column = table[:, turn * 4 + 3 : turn * 4 + 4].astype(I32)
                marks = recv_ref[pl.ds(2 * start + 1, CHUNK, stride=2), :].astype(BF16)
                for place, other in enumerate(later):
                    number = PAIRS.index((turn, other))
                    allowed = mm(marks, spots_ref[:, number * OBS : (number + 1) * OBS])
                    apart = (columns[other] - column) & (TILES_X - 1)
                    allowed = jnp.where(apart < SPAN, allowed, 0.0)
                    gap_x = jnp.abs(x_col - xs[other])
                    gap_x = jnp.minimum(gap_x, NX - gap_x)
                    gap_y = y_col - ys[other]
                    room = 1.0 - gap_x * gap_x * (1.0 / (LOC_X * LOC_X))
                    room = jnp.maximum(room - gap_y * gap_y * (1.0 / (LOC_Y * LOC_Y)), 0.0)
                    weight_ref[:, (place + 1) * OBS : (place + 2) * OBS] = room * room * allowed

            left = left_ref[part, :]
            drive = drive_ref[:, part]
            for number, cols in enumerate(blocks):
                at = max(0, number - GROUPS + 1) * OBS
                covariance = mm(left, pack_ref[:, cols]) * weight_ref[:, at : at + OBS]
                high, low = halves(covariance)
                both = mm(drive, high)
                rest = mm(drive[:MEMBERS], low)
                state_ref[:, cols] += both[:MEMBERS] + both[MEMBERS:] + rest

    for group in range(GROUPS):
        for x in range(CX):
            at = group * CELLS + x * CY
            out_ref[rows_of(group, x), :] = state_ref[:, at : at + CY]


def call(kernel, specs, outs, scratch=()):
    return pl.pallas_call(
        kernel,
        in_specs=specs,
        out_specs=[VMEM] * len(outs) if len(outs) > 1 else VMEM,
        out_shape=outs if len(outs) > 1 else outs[0],
        scratch_shapes=list(scratch),
        compiler_params=pltpu.CompilerParams(vmem_limit_bytes=48 * 1024 * 1024),
    )


def shape(*dims):
    return jax.ShapeDtypeStruct(dims, F32)


def swapped(value, axis, step, periodic):
    count = lax.axis_size(axis)
    pairs = []
    for source in range(count):
        target = source + (step if source % 2 == 0 else -step)
        if periodic or 0 <= target < count:
            pairs.append((source, target % count))
    return lax.ppermute(value, axis, pairs)


def local(
    ensemble,
    courant,
    target_spread,
    obs_error,
    obs_value,
    obs_owner,
    obs_cell,
    obs_kind,
    tile_mask,
    batch_order,
):
    place_x = lax.axis_index(GX)
    place_y = lax.axis_index(GY)
    relay = lax.axis_index(PLANE) * LAYERS + lax.axis_index(LAYER)
    place = jnp.stack([place_x, place_y, relay]).astype(I32)
    ens = ensemble.reshape(MEMBERS * GROUPS * CX, CY)
    mask = tile_mask.reshape(BATCHES, OBS)
    own, rim, first, second, send = call(
        spread_kernel,
        [SMEM] * 3 + [VMEM] * 5,
        [
            shape(GROUPS, MEMBERS, CELLS),
            shape(MEMBERS, CY),
            shape(SIDE + MEMBERS, CY),
            shape(SIDE + MEMBERS, CY),
            shape(OBS, CY),
        ],
    )(batch_order, place, courant, ens, obs_owner, obs_cell, obs_kind, mask)
    recv = lax.all_to_all(send.reshape(PLANES, LAYERS, CY), PLANE, 0, 0)
    first = swapped(first, GX, 1, True)
    second = swapped(second, GX, -1, True)
    joined, third, fourth, send = call(
        collect_kernel,
        [SMEM] + [VMEM] * 5,
        [
            shape(GROUPS, MEMBERS, CELLS),
            shape(RIM, CY),
            shape(RIM, CY),
            shape(2 * LAYERS, CY),
        ],
    )(place, recv.reshape(TILES, CY), own, rim, first, second)
    third = swapped(third, GY, 1, False)
    fourth = swapped(fourth, GY, -1, False)
    recv = lax.all_to_all(send.reshape(LAYERS, 2, CY), LAYER, 0, 0)
    forecast, send = call(
        merge_kernel,
        [SMEM] * 3 + [VMEM] * 4,
        [shape(GROUPS, MEMBERS, CELLS), shape(2 * LAYERS, CY)],
    )(batch_order, place, obs_owner, joined, third, fourth, recv.reshape(2 * LAYERS, CY))
    recv = lax.all_to_all(send.reshape(LAYERS, 2, CY), LAYER, 0, 0)
    send = jnp.broadcast_to(recv.reshape(1, 2 * LAYERS, CY), (PLANES, 2 * LAYERS, CY))
    recv = lax.all_to_all(send, PLANE, 0, 0)
    out = call(
        assimilate_kernel,
        [SMEM] * 4 + [VMEM] * 7,
        [shape(MEMBERS * GROUPS * CX, CY)],
        [
            pltpu.VMEM((MEMBERS, AHEAD + BATCHES * OBS), F32),
            pltpu.VMEM((CY, AHEAD + BATCHES * OBS), BF16),
            pltpu.VMEM((OBS, CY), BF16),
            pltpu.VMEM((2 * MEMBERS, OBS), BF16),
            pltpu.VMEM((OBS, CY), F32),
            pltpu.VMEM((CY, BATCHES * OBS), BF16),
            pltpu.VMEM((CHUNK, BATCHES * OBS), F32),
        ],
    )(
        batch_order,
        place,
        target_spread,
        obs_error,
        forecast,
        recv.reshape(2 * TILES, CY),
        obs_owner,
        obs_cell,
        obs_kind,
        obs_value,
        mask,
    )
    return out.reshape(ensemble.shape)


def solution(mesh):
    fine = Mesh(mesh.devices.reshape(4, 8, 2, 2, 4), ("x", "z_lo", "core", "z_hi", "y"))
    in_specs = (
        P(None, None, None, GX, GY),
        P(),
        P(),
        P(),
        P(),
        P(),
        P(),
        P(),
        P(None, GX, GY, None),
        P(),
    )
    out_specs = P(None, None, None, GX, GY)
    return jax.shard_map(local, mesh=fine, in_specs=in_specs, out_specs=out_specs, check_vma=False)
```

```python
import jax
import jax.numpy as jnp
from jax import lax
from jax.experimental import pallas as pl
from jax.experimental.pallas import tpu as pltpu
from jax.sharding import Mesh
from jax.sharding import PartitionSpec as P

MEMBERS = 32
GROUPS = 4
CX = 4
CY = 128
CELLS = CX * CY
OBS = 512
BATCHES = 3
STEPS = 2
TILES_X = 64
TILES_Y = 8
TILES = TILES_X * TILES_Y
NX = TILES_X * CX
NY = TILES_Y * CY
LOC_X = 12.0
LOC_Y = 512.0
REACH = 2
SPAN = 2 * REACH + 1
PLANES = 32
LAYERS = 16
HALF = CY // 2
RIM = 16
VALUES = BATCHES * MEMBERS
PLANE_ROWS = LAYERS + RIM
LAYER_ROWS = 24
WIDE = (CX + 4) * CY
SIDE = 2 * GROUPS * MEMBERS
GX = ("x", "z_lo", "core")
GY = ("z_hi", "y")
PLANE = ("x", "core", "y")
LAYER = ("z_lo", "z_hi")
CHUNK = 256
AHEAD = GROUPS * CELLS
PAIRS = ((0, 1), (0, 2), (1, 2))

diffuse_rate = 0.1
mixing_rate = 0.05
spread_floor = 1e-05

F32 = jnp.float32
BF16 = jnp.bfloat16
I32 = jnp.int32

VMEM = pl.BlockSpec(memory_space=pltpu.VMEM)
SMEM = pl.BlockSpec(memory_space=pltpu.SMEM)


def rows_of(group, x):
    return pl.ds(group * CX + x, MEMBERS, stride=GROUPS * CX)


def mm(a, b):
    return lax.dot_general(a, b, (((1,), (0,)), ((), ())), preferred_element_type=F32)


def flag(condition):
    return jnp.where(condition, 1.0, 0.0).astype(F32)


def halves(value):
    high = value.astype(BF16)
    return high, (value - high.astype(F32)).astype(BF16)


def thirds(value):
    high = value.astype(BF16)
    rest = value - high.astype(F32)
    middle = rest.astype(BF16)
    return high, middle, (rest - middle.astype(F32)).astype(BF16)


def advance(rows, courant_ref, keep):
    lowest = min(x for _, x in rows) - 1
    highest = max(x for _, x in rows) + 1
    width = 2 * CY
    after = {}
    for group in range(GROUPS):
        speed = courant_ref[group % 2]
        stay = 1.0 - speed - 4.0 * diffuse_rate - mixing_rate
        for x in range(lowest, highest + 1):
            terms = []
            if (group, x) in rows:
                here = rows[group, x]
                beside = pltpu.roll(here, 1, 1) + pltpu.roll(here, width - 1, 1)
                terms.append(stay * here + diffuse_rate * beside + mixing_rate * rows[group ^ 1, x])
            if (group, x - 1) in rows:
                terms.append((speed + diffuse_rate) * rows[group, x - 1])
            if (group, x + 1) in rows:
                terms.append(diffuse_rate * rows[group, x + 1])
            total = terms[0]
            for term in terms[1:]:
                total = total + term
            after[group, x] = total if keep is None else total * keep
    return after


def spread_kernel(
    order_ref,
    place_ref,
    courant_ref,
    ens_ref,
    owner_ref,
    cell_ref,
    kind_ref,
    mask_ref,
    own_ref,
    first_ref,
    second_ref,
    send_ref,
):
    place_x = place_ref[0]
    place_y = place_ref[1]
    rows = {}
    for group in range(GROUPS):
        for x in range(CX):
            own = ens_ref[rows_of(group, x), :]
            rows[group, x] = jnp.concatenate([own, jnp.zeros_like(own)], axis=1)
    lane = lax.broadcasted_iota(I32, (1, 2 * CY), 1)
    below = (lane >= 3 * CY // 2) & (place_y == 0)
    above = (lane >= CY) & (lane < 3 * CY // 2) & (place_y == TILES_Y - 1)
    keep = jnp.where(below | above, 0.0, 1.0).astype(F32)
    rows = advance(rows, courant_ref, keep)
    rows = advance(rows, courant_ref, None)
    lane = lax.broadcasted_iota(I32, (MEMBERS, CY), 1)
    low = jnp.zeros((MEMBERS, CY), F32)
    high = jnp.zeros((MEMBERS, CY), F32)
    tile = {}
    for (group, x), value in rows.items():
        tile[group, x] = value[:, :CY]
        if 0 <= x < CX:
            own_ref[group, :, x * CY : (x + 1) * CY] = tile[group, x]
        edge = value[:, CY:]
        at = group * 16 + (x + 2) * 2
        there = (lane >> 1) == at // 2
        low = jnp.where(there, pltpu.roll(edge, at + 2, 1), low)
        high = jnp.where(there, pltpu.roll(edge, at, 1) if at else edge, high)
    rim = low + pltpu.roll(high, HALF, 1)
    even = (place_x & 1) == 0
    for group in range(GROUPS):
        for x in range(2):
            at = (group * 2 + x) * MEMBERS
            first_ref[at : at + MEMBERS] = jnp.where(even, tile[group, CX + x], tile[group, x - 2])
            second_ref[at : at + MEMBERS] = jnp.where(even, tile[group, x - 2], tile[group, CX + x])
    ground = jnp.concatenate(
        [
            jnp.concatenate([tile[2 * field, x] for x in range(-2, CX + 2)], axis=1)
            for field in range(2)
        ],
        axis=0,
    )
    parts = jnp.concatenate(thirds(ground), axis=0)
    rims = jnp.concatenate(thirds(rim), axis=0)
    blocks = []
    masks = []
    for turn in range(BATCHES):
        batch = order_ref[turn]
        owner = owner_ref[pl.ds(batch, 1), :]
        cell = cell_ref[pl.ds(batch, 1), :]
        kind = kind_ref[pl.ds(batch, 1), :]
        masks.append(mask_ref[pl.ds(batch, 1), :].astype(F32))
        at_x = ((owner >> 3) - place_x) * CX + (cell >> 7) + 2
        at_x = at_x & (NX - 1)
        at_y = ((owner & (TILES_Y - 1)) - place_y) * CY + (cell & (CY - 1))
        seen = at_x < CX + 4
        index = jnp.where(seen & (at_y >= 0) & (at_y < CY), at_x * CY + at_y, -1)
        corner = kind * 32 + at_x * 2
        edge = jnp.where(seen & (at_y >= -2) & (at_y < 0), corner + at_y + 2, -1)
        edge = jnp.where(seen & (at_y >= CY) & (at_y < CY + 2), corner + at_y - CY + HALF, edge)
        picked = jnp.zeros((parts.shape[0], OBS), F32)
        for start in range(0, WIDE, CHUNK):
            spot = lax.broadcasted_iota(I32, (CHUNK, OBS), 0) + start
            hot = jnp.where(spot == index, 1.0, 0.0).astype(BF16)
            picked = picked + mm(parts[:, start : start + CHUNK], hot)
        picked = picked[0:64] + picked[64:128] + picked[128:192]
        spot = lax.broadcasted_iota(I32, (CY, OBS), 0)
        found = mm(rims, jnp.where(spot == edge, 1.0, 0.0).astype(BF16))
        found = found[0:32] + found[32:64] + found[64:96]
        blocks.append(jnp.where(kind == 0, picked[0:32], picked[32:64]) + found)
    sub = lax.broadcasted_iota(I32, (MEMBERS, OBS), 0)
    blocks.append(jnp.where(sub == 0, masks[0], jnp.where(sub == 1, masks[1], 0.0)))
    turned = jnp.concatenate(blocks, axis=0).T
    lane = lax.broadcasted_iota(I32, (RIM, CY), 1)
    low = jnp.where(lane < HALF, low[:RIM], pltpu.roll(low[RIM:], HALF, 1))
    high = jnp.where(lane < HALF, high[:RIM], pltpu.roll(high[RIM:], HALF, 1))
    y = place_y & 3
    for plane in range(PLANES):
        at = plane * PLANE_ROWS
        send_ref[at : at + LAYERS, :] = turned[plane * LAYERS : (plane + 1) * LAYERS]
        up = flag((y + 1) & 3 == plane & 3)
        down = flag((y + 3) & 3 == plane & 3)
        send_ref[at + LAYERS : at + PLANE_ROWS, :] = up * high + down * low


def collect_kernel(place_ref, recv_ref, send_ref):
    place_x = place_ref[0]
    place_y = place_ref[1]
    x, z_lo, core = place_x >> 4, (place_x >> 1) & 7, place_x & 1
    z_hi, y = place_y >> 2, place_y & 3
    lane = lax.broadcasted_iota(I32, (LAYERS, CY), 1)
    total = jnp.zeros((LAYERS, CY), F32)
    marks = jnp.zeros((LAYERS, CY), F32)
    for plane in range(PLANES):
        rows = recv_ref[plane * PLANE_ROWS : plane * PLANE_ROWS + LAYERS, :]
        total = total + rows
        for turn in range(2):
            at = VALUES + turn
            marks = jnp.where(lane == turn * PLANES + plane, rows[:, at : at + 1], marks)

    spot = lane & 15
    hop = jnp.where(core == 0, z_lo == 7, z_lo == 0)
    side = jnp.where(hop, (x + jnp.where(core == 0, 3, 1)) & 3, x)
    first = flag(core == 0)
    second = 1.0 - first

    def rim(column, other, step):
        plane = (column * 2 + other) * 4 + ((y + step) & 3)
        start = pl.multiple_of(plane * PLANE_ROWS + LAYERS, RIM)
        return recv_ref[pl.ds(start, RIM), :]

    def from_left(block):
        return jnp.where((spot >= 4) & (spot < 8), pltpu.roll(block, CY - 8, 1), 0.0)

    def from_right(block):
        return jnp.where((spot >= 8) & (spot < 12), pltpu.roll(block, 8, 1), 0.0)

    here, there = [], []
    for step in (3, 1):
        mine = jnp.where((spot >= 4) & (spot < 12), rim(x, core, step), 0.0)
        twin = rim(x, 1 - core, step)
        far = rim(side, 1 - core, step)
        block = mine + first * from_right(twin) + second * from_left(twin)
        other = first * from_left(far) + second * from_right(far)
        here.append(pltpu.roll(block, 8, 1) if step == 1 else block)
        there.append(pltpu.roll(other, 8, 1) if step == 1 else other)
    target = jnp.where(core == 0, z_lo + 1, z_lo + 7) & 7
    below = jnp.where(y > 0, z_hi, jnp.where(z_hi == 0, 1, -1))
    above = jnp.where(y < 3, z_hi, jnp.where(z_hi == 1, 0, -1))
    for layer in range(LAYERS):
        lower, higher = flag(below == layer % 2), flag(above == layer % 2)
        same, next_to = flag(z_lo == layer // 2), flag(target == layer // 2)
        at = layer * LAYER_ROWS
        send_ref[at : at + RIM, :] = same * (lower * here[0] + higher * here[1]) + next_to * (
            lower * there[0] + higher * there[1]
        )
        pair = jnp.concatenate([total[layer : layer + 1], marks[layer : layer + 1]], axis=0)
        send_ref[at + RIM : at + RIM + 2, :] = pair
        send_ref[at + RIM + 2 : at + LAYER_ROWS, :] = jnp.zeros((LAYER_ROWS - RIM - 2, CY), F32)


def merge_kernel(
    order_ref,
    place_ref,
    relay_ref,
    own_ref,
    first_ref,
    second_ref,
    recv_ref,
    forecast_ref,
    send_ref,
):
    relay = place_ref[2]
    lane = lax.broadcasted_iota(I32, (1, CY), 1)
    sums = recv_ref[pl.ds(RIM, LAYERS, stride=LAYER_ROWS), :]
    marks = recv_ref[pl.ds(RIM + 1, LAYERS, stride=LAYER_ROWS), :]
    top = jnp.sum(sums, axis=0, keepdims=True)
    top = jnp.where(lane < BATCHES * MEMBERS, top, 0.0)
    below = recv_ref[0:RIM, :]
    for layer in range(1, LAYERS):
        below = below + recv_ref[layer * LAYER_ROWS : layer * LAYER_ROWS + RIM, :]
    above = pltpu.roll(below, CY - 8, 1)
    below = jnp.concatenate([below, pltpu.roll(below, HALF, 1)], axis=0)
    above = jnp.concatenate([above, pltpu.roll(above, HALF, 1)], axis=0)
    even = (place_ref[0] & 1) == 0
    wide = lax.broadcasted_iota(I32, (MEMBERS, CY), 1)
    for group in range(GROUPS):
        pieces = []
        for x in range(CX):
            at = group * 16 + (x + 2) * 2
            part = (group * 2 + x % 2) * MEMBERS
            part = slice(part, part + MEMBERS)
            near = first_ref[part], second_ref[part]
            other = jnp.where(even, near[1], near[0]) if x < 2 else jnp.where(even, near[0], near[1])
            piece = own_ref[group, :, x * CY : (x + 1) * CY] + other
            piece = piece + jnp.where(wide < 2, pltpu.roll(below, CY - at, 1), 0.0)
            piece = piece + jnp.where(wide >= CY - 2, pltpu.roll(above, CY - 2 - at, 1), 0.0)
            pieces.append(piece)
        value = jnp.concatenate(pieces, axis=1)
        forecast_ref[group] = value
        centre = jnp.sum(value, axis=0, keepdims=True) * (1.0 / MEMBERS)
        deviation = value - centre
        total = jnp.sum(jnp.sum(deviation * deviation, axis=0, keepdims=True), axis=1, keepdims=True)
        top = jnp.where(lane == BATCHES * MEMBERS + group, total, top)

    lanes = lax.broadcasted_iota(I32, (LAYERS, CY), 1)
    subs = lax.broadcasted_iota(I32, (LAYERS, CY), 0)
    tile_x = ((lanes >> 3) & 3) * 16 + (subs >> 1) * 2 + ((lanes >> 2) & 1)
    first = relay_ref[order_ref[0], relay] >> 3
    second = relay_ref[order_ref[1], relay] >> 3
    column = jnp.where(lanes < PLANES, first, second)
    near = ((tile_x - column + REACH) & (TILES_X - 1)) < SPAN
    marks = jnp.where(near & (lanes < 2 * PLANES), marks, 0.0)
    marks = marks[:8] + marks[8:]
    folded = marks
    for step in (8, 16, 24):
        folded = folded + pltpu.roll(marks, CY - step, 1)
    lanes = lax.broadcasted_iota(I32, (8, CY), 1)
    subs = lax.broadcasted_iota(I32, (8, CY), 0)
    bottom = jnp.zeros((8, CY), F32)
    for row in range(8):
        for turn in range(2):
            moved = pltpu.roll(folded, (turn * PLANES + row * 8) % CY, 1)
            there = (subs == row) & ((lanes >> 3) == turn * 8 + row)
            bottom = jnp.where(there, moved, bottom)
    bottom = jnp.sum(bottom, axis=0, keepdims=True)
    pair = jnp.concatenate([top, bottom] * 4, axis=0)
    send_ref[...] = jnp.concatenate([pair] * (2 * LAYERS // 8), axis=0)


def assimilate_kernel(
    order_ref,
    place_ref,
    spread_ref,
    error_ref,
    forecast_ref,
    recv_ref,
    owner_ref,
    cell_ref,
    kind_ref,
    value_ref,
    mask_ref,
    out_ref,
    state_ref,
    pack_ref,
    left_ref,
    drive_ref,
    table_ref,
    spots_ref,
    weight_ref,
):
    place_x = place_ref[0]
    place_y = place_ref[1]
    upper = recv_ref[pl.ds(0, TILES, stride=2), :].T
    stretch = []
    for group in range(GROUPS):
        row = BATCHES * MEMBERS + group
        total = jnp.sum(upper[row : row + 1], axis=1, keepdims=True)
        mean_var = total * (1.0 / ((MEMBERS - 1) * float(NX * NY)))
        stretch.append(jnp.sqrt(spread_ref[group // 2, group % 2] / (mean_var + spread_floor)))
    for group in range(GROUPS):
        value = forecast_ref[group]
        centre = jnp.sum(value, axis=0, keepdims=True) * (1.0 / MEMBERS)
        state_ref[:, group * CELLS : (group + 1) * CELLS] = centre + stretch[group] * (value - centre)

    kinds, xs, ys, values = [], [], [], []
    sub = lax.broadcasted_iota(I32, (CY, OBS), 0)
    table_ref[...] = jnp.zeros_like(table_ref)
    table = jnp.zeros((CY, OBS), F32)
    columns, spots = [], []
    for turn in range(BATCHES):
        batch = order_ref[turn]
        owner = owner_ref[pl.ds(batch, 1), :]
        cell = cell_ref[pl.ds(batch, 1), :]
        kinds.append(kind_ref[pl.ds(batch, 1), :])
        values.append(value_ref[pl.ds(batch, 1), :])
        mask = mask_ref[pl.ds(batch, 1), :].astype(F32)
        xs.append(((owner >> 3) * CX + (cell >> 7)).astype(F32))
        ys.append(((owner & (TILES_Y - 1)) * CY + (cell & (CY - 1))).astype(F32))
        tile_x = owner >> 3
        columns.append(tile_x + REACH)
        for row, value in enumerate((xs[turn], ys[turn], mask, tile_x.astype(F32))):
            table = jnp.where(sub == turn * 4 + row, value, table)
        prior = upper[turn * MEMBERS : (turn + 1) * MEMBERS]
        centre = jnp.sum(prior, axis=0, keepdims=True) * (1.0 / MEMBERS)
        factor = jnp.where(kinds[turn] == 0, stretch[0], stretch[2])
        state_ref[:, AHEAD + turn * OBS : AHEAD + (turn + 1) * OBS] = centre + factor * (prior - centre)
        strip = ((tile_x >> 1) & 3) * 2 + ((owner >> 2) & 1)
        spots.append(strip * 8 + (tile_x & 1) * 4 + (owner & 3))
    for number, (turn, other) in enumerate(PAIRS):
        hot = jnp.where(sub == spots[other] + turn * HALF, 1.0, 0.0)
        spots_ref[:, number * OBS : (number + 1) * OBS] = hot.astype(BF16)
    table_ref[...] = table.T

    lane = lax.broadcasted_iota(I32, (1, CY), 1)
    cell_x = (place_x * CX).astype(F32)
    cell_y = (place_y * CY + lane).astype(F32)

    for turn in range(BATCHES):
        prior = state_ref[:, AHEAD + turn * OBS : AHEAD + (turn + 1) * OBS]
        error = jnp.where(kinds[turn] == 0, error_ref[0], error_ref[1])
        centre = jnp.sum(prior, axis=0, keepdims=True) * (1.0 / MEMBERS)
        deviation = prior - centre
        variance = jnp.sum(deviation * deviation, axis=0, keepdims=True) / (MEMBERS - 1)
        gain = (values[turn] - centre) / (variance + error)
        shrink = -1.0 / (jnp.sqrt(error * (error + variance)) + error + variance)
        drive_high, drive_low = halves(gain + shrink * deviation)
        drive_ref[:MEMBERS] = drive_high
        drive_ref[MEMBERS:] = drive_low
        scaled = deviation * (1.0 / (MEMBERS - 1))
        scaled_high = scaled.astype(BF16).astype(F32)
        scaled_low = scaled - scaled_high
        packed = jnp.concatenate(
            [scaled_high, scaled_high, scaled_low, jnp.zeros_like(scaled)], axis=0
        )
        left_ref[...] = packed.T.astype(BF16)

        later = list(range(turn + 1, BATCHES))
        blocks = [slice(group * CELLS, (group + 1) * CELLS) for group in range(GROUPS)]
        blocks += [slice(AHEAD + other * OBS, AHEAD + (other + 1) * OBS) for other in later]
        for cols in blocks:
            state = state_ref[:, cols]
            state_dev = state - jnp.sum(state, axis=0, keepdims=True) * (1.0 / MEMBERS)
            high, low = halves(state_dev)
            pack_ref[0:32, cols] = high
            pack_ref[32:64, cols] = low
            pack_ref[64:96, cols] = high
            pack_ref[96:128, cols] = jnp.zeros_like(high)

        @pl.loop(0, OBS // CHUNK)
        def _(step):
            start = pl.multiple_of(step * CHUNK, CHUNK)
            part = pl.ds(start, CHUNK)
            table = table_ref[part, :]
            x_col = table[:, turn * 4 : turn * 4 + 1]
            y_col = table[:, turn * 4 + 1 : turn * 4 + 2]
            mask_col = table[:, turn * 4 + 2 : turn * 4 + 3]
            gap_y = y_col - cell_y
            drop_y = gap_y * gap_y * (1.0 / (LOC_Y * LOC_Y))
            for x in range(CX):
                gap_x = jnp.abs(x_col - (cell_x + x))
                gap_x = jnp.minimum(gap_x, NX - gap_x)
                room = jnp.maximum((1.0 - gap_x * gap_x * (1.0 / (LOC_X * LOC_X))) - drop_y, 0.0)
                weight_ref[:, x * CY : (x + 1) * CY] = room * room * mask_col
            if later:
                column = table[:, turn * 4 + 3 : turn * 4 + 4].astype(I32)
                marks = recv_ref[pl.ds(2 * start + 1, CHUNK, stride=2), :].astype(BF16)
                for place, other in enumerate(later):
                    number = PAIRS.index((turn, other))
                    allowed = mm(marks, spots_ref[:, number * OBS : (number + 1) * OBS])
                    apart = (columns[other] - column) & (TILES_X - 1)
                    allowed = jnp.where(apart < SPAN, allowed, 0.0)
                    gap_x = jnp.abs(x_col - xs[other])
                    gap_x = jnp.minimum(gap_x, NX - gap_x)
                    gap_y = y_col - ys[other]
                    room = 1.0 - gap_x * gap_x * (1.0 / (LOC_X * LOC_X))
                    room = jnp.maximum(room - gap_y * gap_y * (1.0 / (LOC_Y * LOC_Y)), 0.0)
                    weight_ref[:, (place + 1) * OBS : (place + 2) * OBS] = room * room * allowed

            left = left_ref[part, :]
            drive = drive_ref[:, part]
            for number, cols in enumerate(blocks):
                at = max(0, number - GROUPS + 1) * OBS
                covariance = mm(left, pack_ref[:, cols]) * weight_ref[:, at : at + OBS]
                high, low = halves(covariance)
                both = mm(drive, high)
                rest = mm(drive[:MEMBERS], low)
                state_ref[:, cols] += both[:MEMBERS] + both[MEMBERS:] + rest

    for group in range(GROUPS):
        for x in range(CX):
            at = group * CELLS + x * CY
            out_ref[rows_of(group, x), :] = state_ref[:, at : at + CY]


def call(kernel, specs, outs, scratch=()):
    return pl.pallas_call(
        kernel,
        in_specs=specs,
        out_specs=[VMEM] * len(outs) if len(outs) > 1 else VMEM,
        out_shape=outs if len(outs) > 1 else outs[0],
        scratch_shapes=list(scratch),
        compiler_params=pltpu.CompilerParams(vmem_limit_bytes=48 * 1024 * 1024),
    )


def shape(*dims):
    return jax.ShapeDtypeStruct(dims, F32)


def swapped(value, axis, step, periodic):
    count = lax.axis_size(axis)
    pairs = []
    for source in range(count):
        target = source + (step if source % 2 == 0 else -step)
        if periodic or 0 <= target < count:
            pairs.append((source, target % count))
    return lax.ppermute(value, axis, pairs)


def local(
    ensemble,
    courant,
    target_spread,
    obs_error,
    obs_value,
    obs_owner,
    obs_cell,
    obs_kind,
    tile_mask,
    batch_order,
):
    place_x = lax.axis_index(GX)
    place_y = lax.axis_index(GY)
    relay = lax.axis_index(PLANE) * LAYERS + lax.axis_index(LAYER)
    place = jnp.stack([place_x, place_y, relay]).astype(I32)
    ens = ensemble.reshape(MEMBERS * GROUPS * CX, CY)
    mask = tile_mask.reshape(BATCHES, OBS)
    own, first, second, send = call(
        spread_kernel,
        [SMEM] * 3 + [VMEM] * 5,
        [
            shape(GROUPS, MEMBERS, CELLS),
            shape(SIDE, CY),
            shape(SIDE, CY),
            shape(PLANES * PLANE_ROWS, CY),
        ],
    )(batch_order, place, courant, ens, obs_owner, obs_cell, obs_kind, mask)
    recv = lax.all_to_all(send.reshape(PLANES, PLANE_ROWS, CY), PLANE, 0, 0)
    first = swapped(first, GX, 1, True)
    second = swapped(second, GX, -1, True)
    send = call(collect_kernel, [SMEM, VMEM], [shape(LAYERS * LAYER_ROWS, CY)])(
        place, recv.reshape(PLANES * PLANE_ROWS, CY)
    )
    recv = lax.all_to_all(send.reshape(LAYERS, LAYER_ROWS, CY), LAYER, 0, 0)
    recv = recv.reshape(LAYERS * LAYER_ROWS, CY)
    forecast, send = call(
        merge_kernel,
        [SMEM] * 3 + [VMEM] * 4,
        [shape(GROUPS, MEMBERS, CELLS), shape(2 * LAYERS, CY)],
    )(batch_order, place, obs_owner, own, first, second, recv)
    recv = lax.all_to_all(send.reshape(LAYERS, 2, CY), LAYER, 0, 0)
    send = jnp.broadcast_to(recv.reshape(1, 2 * LAYERS, CY), (PLANES, 2 * LAYERS, CY))
    recv = lax.all_to_all(send, PLANE, 0, 0)
    out = call(
        assimilate_kernel,
        [SMEM] * 4 + [VMEM] * 7,
        [shape(MEMBERS * GROUPS * CX, CY)],
        [
            pltpu.VMEM((MEMBERS, AHEAD + BATCHES * OBS), F32),
            pltpu.VMEM((CY, AHEAD + BATCHES * OBS), BF16),
            pltpu.VMEM((OBS, CY), BF16),
            pltpu.VMEM((2 * MEMBERS, OBS), BF16),
            pltpu.VMEM((OBS, CY), F32),
            pltpu.VMEM((CY, BATCHES * OBS), BF16),
            pltpu.VMEM((CHUNK, BATCHES * OBS), F32),
        ],
    )(
        batch_order,
        place,
        target_spread,
        obs_error,
        forecast,
        recv.reshape(2 * TILES, CY),
        obs_owner,
        obs_cell,
        obs_kind,
        obs_value,
        mask,
    )
    return out.reshape(ensemble.shape)


def solution(mesh):
    fine = Mesh(mesh.devices.reshape(4, 8, 2, 2, 4), ("x", "z_lo", "core", "z_hi", "y"))
    in_specs = (
        P(None, None, None, GX, GY),
        P(),
        P(),
        P(),
        P(),
        P(),
        P(),
        P(),
        P(None, GX, GY, None),
        P(),
    )
    out_specs = P(None, None, None, GX, GY)
    return jax.shard_map(local, mesh=fine, in_specs=in_specs, out_specs=out_specs, check_vma=False)
```

```python
import jax
import jax.numpy as jnp
from jax import lax
from jax.experimental import pallas as pl
from jax.experimental.pallas import tpu as pltpu
from jax.sharding import Mesh
from jax.sharding import PartitionSpec as P

MEMBERS = 32
GROUPS = 4
CX = 4
CY = 128
CELLS = CX * CY
OBS = 512
BATCHES = 3
STEPS = 2
TILES_X = 64
TILES_Y = 8
TILES = TILES_X * TILES_Y
NX = TILES_X * CX
NY = TILES_Y * CY
LOC_X = 12.0
LOC_Y = 512.0
REACH = 2
SPAN = 2 * REACH + 1
PLANES = 32
LAYERS = 16
HALF = CY // 2
RIM = 16
VALUES = BATCHES * MEMBERS
PLANE_ROWS = LAYERS + RIM
LAYER_ROWS = 24
WIDE = (CX + 4) * CY
SIDE = 2 * GROUPS * MEMBERS
GX = ("x", "z_lo", "core")
GY = ("z_hi", "y")
PLANE = ("x", "core", "y")
LAYER = ("z_lo", "z_hi")
CHUNK = 256
AHEAD = GROUPS * CELLS
PAIRS = ((0, 1), (0, 2), (1, 2))

diffuse_rate = 0.1
mixing_rate = 0.05
spread_floor = 1e-05

F32 = jnp.float32
BF16 = jnp.bfloat16
I32 = jnp.int32

VMEM = pl.BlockSpec(memory_space=pltpu.VMEM)
SMEM = pl.BlockSpec(memory_space=pltpu.SMEM)


def rows_of(group, x):
    return pl.ds(group * CX + x, MEMBERS, stride=GROUPS * CX)


def mm(a, b):
    return lax.dot_general(a, b, (((1,), (0,)), ((), ())), preferred_element_type=F32)


def flag(condition):
    return jnp.where(condition, 1.0, 0.0).astype(F32)


def halves(value):
    high = value.astype(BF16)
    return high, (value - high.astype(F32)).astype(BF16)


def thirds(value):
    high = value.astype(BF16)
    rest = value - high.astype(F32)
    middle = rest.astype(BF16)
    return high, middle, (rest - middle.astype(F32)).astype(BF16)


def advance(rows, courant_ref, keep):
    lowest = min(x for _, x in rows) - 1
    highest = max(x for _, x in rows) + 1
    width = 2 * CY
    after = {}
    for group in range(GROUPS):
        speed = courant_ref[group % 2]
        stay = 1.0 - speed - 4.0 * diffuse_rate - mixing_rate
        for x in range(lowest, highest + 1):
            terms = []
            if (group, x) in rows:
                here = rows[group, x]
                beside = pltpu.roll(here, 1, 1) + pltpu.roll(here, width - 1, 1)
                terms.append(stay * here + diffuse_rate * beside + mixing_rate * rows[group ^ 1, x])
            if (group, x - 1) in rows:
                terms.append((speed + diffuse_rate) * rows[group, x - 1])
            if (group, x + 1) in rows:
                terms.append(diffuse_rate * rows[group, x + 1])
            total = terms[0]
            for term in terms[1:]:
                total = total + term
            after[group, x] = total if keep is None else total * keep
    return after


def spread_kernel(
    order_ref,
    place_ref,
    courant_ref,
    ens_ref,
    owner_ref,
    cell_ref,
    kind_ref,
    mask_ref,
    own_ref,
    first_ref,
    second_ref,
    send_ref,
):
    place_x = place_ref[0]
    place_y = place_ref[1]
    rows = {}
    for group in range(GROUPS):
        for x in range(CX):
            own = ens_ref[rows_of(group, x), :]
            rows[group, x] = jnp.concatenate([own, jnp.zeros_like(own)], axis=1)
    lane = lax.broadcasted_iota(I32, (1, 2 * CY), 1)
    below = (lane >= 3 * CY // 2) & (place_y == 0)
    above = (lane >= CY) & (lane < 3 * CY // 2) & (place_y == TILES_Y - 1)
    keep = jnp.where(below | above, 0.0, 1.0).astype(F32)
    rows = advance(rows, courant_ref, keep)
    rows = advance(rows, courant_ref, None)
    lane = lax.broadcasted_iota(I32, (MEMBERS, CY), 1)
    low = jnp.zeros((MEMBERS, CY), F32)
    high = jnp.zeros((MEMBERS, CY), F32)
    tile = {}
    for (group, x), value in rows.items():
        tile[group, x] = value[:, :CY]
        if 0 <= x < CX:
            own_ref[group, :, x * CY : (x + 1) * CY] = tile[group, x]
        edge = value[:, CY:]
        at = group * 16 + (x + 2) * 2
        there = (lane >> 1) == at // 2
        low = jnp.where(there, pltpu.roll(edge, at + 2, 1), low)
        high = jnp.where(there, pltpu.roll(edge, at, 1) if at else edge, high)
    rim = low + pltpu.roll(high, HALF, 1)
    even = (place_x & 1) == 0
    for group in range(GROUPS):
        for x in range(2):
            at = (group * 2 + x) * MEMBERS
            first_ref[at : at + MEMBERS] = jnp.where(even, tile[group, CX + x], tile[group, x - 2])
            second_ref[at : at + MEMBERS] = jnp.where(even, tile[group, x - 2], tile[group, CX + x])
    ground = jnp.concatenate(
        [
            jnp.concatenate([tile[2 * field, x] for x in range(-2, CX + 2)], axis=1)
            for field in range(2)
        ],
        axis=0,
    )
    parts = jnp.concatenate(thirds(ground), axis=0)
    rims = jnp.concatenate(thirds(rim), axis=0)
    blocks = []
    masks = []
    for turn in range(BATCHES):
        batch = order_ref[turn]
        owner = owner_ref[pl.ds(batch, 1), :]
        cell = cell_ref[pl.ds(batch, 1), :]
        kind = kind_ref[pl.ds(batch, 1), :]
        masks.append(mask_ref[pl.ds(batch, 1), :].astype(F32))
        at_x = ((owner >> 3) - place_x) * CX + (cell >> 7) + 2
        at_x = at_x & (NX - 1)
        at_y = ((owner & (TILES_Y - 1)) - place_y) * CY + (cell & (CY - 1))
        seen = at_x < CX + 4
        index = jnp.where(seen & (at_y >= 0) & (at_y < CY), at_x * CY + at_y, -1)
        corner = kind * 32 + at_x * 2
        edge = jnp.where(seen & (at_y >= -2) & (at_y < 0), corner + at_y + 2, -1)
        edge = jnp.where(seen & (at_y >= CY) & (at_y < CY + 2), corner + at_y - CY + HALF, edge)
        picked = jnp.zeros((parts.shape[0], OBS), F32)
        for start in range(0, WIDE, CHUNK):
            spot = lax.broadcasted_iota(I32, (CHUNK, OBS), 0) + start
            hot = jnp.where(spot == index, 1.0, 0.0).astype(BF16)
            picked = picked + mm(parts[:, start : start + CHUNK], hot)
        picked = picked[0:64] + picked[64:128] + picked[128:192]
        spot = lax.broadcasted_iota(I32, (CY, OBS), 0)
        found = mm(rims, jnp.where(spot == edge, 1.0, 0.0).astype(BF16))
        found = found[0:32] + found[32:64] + found[64:96]
        blocks.append(jnp.where(kind == 0, picked[0:32], picked[32:64]) + found)
    sub = lax.broadcasted_iota(I32, (MEMBERS, OBS), 0)
    blocks.append(jnp.where(sub == 0, masks[0], jnp.where(sub == 1, masks[1], 0.0)))
    turned = jnp.concatenate(blocks, axis=0).T
    lane = lax.broadcasted_iota(I32, (RIM, CY), 1)
    low = jnp.where(lane < HALF, low[:RIM], pltpu.roll(low[RIM:], HALF, 1))
    high = jnp.where(lane < HALF, high[:RIM], pltpu.roll(high[RIM:], HALF, 1))
    y = place_y & 3
    for plane in range(PLANES):
        at = plane * PLANE_ROWS
        send_ref[at : at + LAYERS, :] = turned[plane * LAYERS : (plane + 1) * LAYERS]
        up = flag((y + 1) & 3 == plane & 3)
        down = flag((y + 3) & 3 == plane & 3)
        send_ref[at + LAYERS : at + PLANE_ROWS, :] = up * high + down * low


def collect_kernel(place_ref, recv_ref, own_ref, near_ref, far_ref, joined_ref, send_ref):
    even = (place_ref[0] & 1) == 0
    for group in range(GROUPS):
        for column in range(CX):
            at = (group * 2 + column % 2) * MEMBERS
            part = slice(at, at + MEMBERS)
            near, far = near_ref[part], far_ref[part]
            other = jnp.where(even, far, near) if column < 2 else jnp.where(even, near, far)
            cells = slice(column * CY, (column + 1) * CY)
            joined_ref[group, :, cells] = own_ref[group, :, cells] + other
    place_x = place_ref[0]
    place_y = place_ref[1]
    x, z_lo, core = place_x >> 4, (place_x >> 1) & 7, place_x & 1
    z_hi, y = place_y >> 2, place_y & 3
    lane = lax.broadcasted_iota(I32, (LAYERS, CY), 1)
    total = jnp.zeros((LAYERS, CY), F32)
    marks = jnp.zeros((LAYERS, CY), F32)
    for plane in range(PLANES):
        rows = recv_ref[plane * PLANE_ROWS : plane * PLANE_ROWS + LAYERS, :]
        total = total + rows
        for turn in range(2):
            at = VALUES + turn
            marks = jnp.where(lane == turn * PLANES + plane, rows[:, at : at + 1], marks)

    spot = lane & 15
    hop = jnp.where(core == 0, z_lo == 7, z_lo == 0)
    side = jnp.where(hop, (x + jnp.where(core == 0, 3, 1)) & 3, x)
    first = flag(core == 0)
    second = 1.0 - first

    def rim(column, other, step):
        plane = (column * 2 + other) * 4 + ((y + step) & 3)
        start = pl.multiple_of(plane * PLANE_ROWS + LAYERS, RIM)
        return recv_ref[pl.ds(start, RIM), :]

    def from_left(block):
        return jnp.where((spot >= 4) & (spot < 8), pltpu.roll(block, CY - 8, 1), 0.0)

    def from_right(block):
        return jnp.where((spot >= 8) & (spot < 12), pltpu.roll(block, 8, 1), 0.0)

    here, there = [], []
    for step in (3, 1):
        mine = jnp.where((spot >= 4) & (spot < 12), rim(x, core, step), 0.0)
        twin = rim(x, 1 - core, step)
        far = rim(side, 1 - core, step)
        block = mine + first * from_right(twin) + second * from_left(twin)
        other = first * from_left(far) + second * from_right(far)
        here.append(pltpu.roll(block, 8, 1) if step == 1 else block)
        there.append(pltpu.roll(other, 8, 1) if step == 1 else other)
    target = jnp.where(core == 0, z_lo + 1, z_lo + 7) & 7
    below = jnp.where(y > 0, z_hi, jnp.where(z_hi == 0, 1, -1))
    above = jnp.where(y < 3, z_hi, jnp.where(z_hi == 1, 0, -1))
    for layer in range(LAYERS):
        lower, higher = flag(below == layer % 2), flag(above == layer % 2)
        same, next_to = flag(z_lo == layer // 2), flag(target == layer // 2)
        at = layer * LAYER_ROWS
        send_ref[at : at + RIM, :] = same * (lower * here[0] + higher * here[1]) + next_to * (
            lower * there[0] + higher * there[1]
        )
        pair = jnp.concatenate([total[layer : layer + 1], marks[layer : layer + 1]], axis=0)
        send_ref[at + RIM : at + RIM + 2, :] = pair
        send_ref[at + RIM + 2 : at + LAYER_ROWS, :] = jnp.zeros((LAYER_ROWS - RIM - 2, CY), F32)


def merge_kernel(
    order_ref,
    place_ref,
    relay_ref,
    joined_ref,
    recv_ref,
    forecast_ref,
    send_ref,
):
    relay = place_ref[2]
    lane = lax.broadcasted_iota(I32, (1, CY), 1)
    sums = recv_ref[pl.ds(RIM, LAYERS, stride=LAYER_ROWS), :]
    marks = recv_ref[pl.ds(RIM + 1, LAYERS, stride=LAYER_ROWS), :]
    top = jnp.sum(sums, axis=0, keepdims=True)
    top = jnp.where(lane < BATCHES * MEMBERS, top, 0.0)
    below = recv_ref[0:RIM, :]
    for layer in range(1, LAYERS):
        below = below + recv_ref[layer * LAYER_ROWS : layer * LAYER_ROWS + RIM, :]
    above = pltpu.roll(below, CY - 8, 1)
    below = jnp.concatenate([below, pltpu.roll(below, HALF, 1)], axis=0)
    above = jnp.concatenate([above, pltpu.roll(above, HALF, 1)], axis=0)
    wide = lax.broadcasted_iota(I32, (MEMBERS, CY), 1)
    for group in range(GROUPS):
        pieces = []
        for x in range(CX):
            at = group * 16 + (x + 2) * 2
            piece = joined_ref[group, :, x * CY : (x + 1) * CY]
            piece = piece + jnp.where(wide < 2, pltpu.roll(below, CY - at, 1), 0.0)
            piece = piece + jnp.where(wide >= CY - 2, pltpu.roll(above, CY - 2 - at, 1), 0.0)
            pieces.append(piece)
        value = jnp.concatenate(pieces, axis=1)
        forecast_ref[group] = value
        centre = jnp.sum(value, axis=0, keepdims=True) * (1.0 / MEMBERS)
        deviation = value - centre
        total = jnp.sum(jnp.sum(deviation * deviation, axis=0, keepdims=True), axis=1, keepdims=True)
        top = jnp.where(lane == BATCHES * MEMBERS + group, total, top)

    lanes = lax.broadcasted_iota(I32, (LAYERS, CY), 1)
    subs = lax.broadcasted_iota(I32, (LAYERS, CY), 0)
    tile_x = ((lanes >> 3) & 3) * 16 + (subs >> 1) * 2 + ((lanes >> 2) & 1)
    first = relay_ref[order_ref[0], relay] >> 3
    second = relay_ref[order_ref[1], relay] >> 3
    column = jnp.where(lanes < PLANES, first, second)
    near = ((tile_x - column + REACH) & (TILES_X - 1)) < SPAN
    marks = jnp.where(near & (lanes < 2 * PLANES), marks, 0.0)
    marks = marks[:8] + marks[8:]
    folded = marks
    for step in (8, 16, 24):
        folded = folded + pltpu.roll(marks, CY - step, 1)
    lanes = lax.broadcasted_iota(I32, (8, CY), 1)
    subs = lax.broadcasted_iota(I32, (8, CY), 0)
    bottom = jnp.zeros((8, CY), F32)
    for row in range(8):
        for turn in range(2):
            moved = pltpu.roll(folded, (turn * PLANES + row * 8) % CY, 1)
            there = (subs == row) & ((lanes >> 3) == turn * 8 + row)
            bottom = jnp.where(there, moved, bottom)
    bottom = jnp.sum(bottom, axis=0, keepdims=True)
    pair = jnp.concatenate([top, bottom] * 4, axis=0)
    send_ref[...] = jnp.concatenate([pair] * (2 * LAYERS // 8), axis=0)


def assimilate_kernel(
    order_ref,
    place_ref,
    spread_ref,
    error_ref,
    forecast_ref,
    recv_ref,
    owner_ref,
    cell_ref,
    kind_ref,
    value_ref,
    mask_ref,
    out_ref,
    state_ref,
    pack_ref,
    left_ref,
    drive_ref,
    table_ref,
    spots_ref,
    weight_ref,
):
    place_x = place_ref[0]
    place_y = place_ref[1]
    upper = recv_ref[pl.ds(0, TILES, stride=2), :].T
    stretch = []
    for group in range(GROUPS):
        row = BATCHES * MEMBERS + group
        total = jnp.sum(upper[row : row + 1], axis=1, keepdims=True)
        mean_var = total * (1.0 / ((MEMBERS - 1) * float(NX * NY)))
        stretch.append(jnp.sqrt(spread_ref[group // 2, group % 2] / (mean_var + spread_floor)))
    for group in range(GROUPS):
        value = forecast_ref[group]
        centre = jnp.sum(value, axis=0, keepdims=True) * (1.0 / MEMBERS)
        state_ref[:, group * CELLS : (group + 1) * CELLS] = centre + stretch[group] * (value - centre)

    kinds, xs, ys, values = [], [], [], []
    sub = lax.broadcasted_iota(I32, (CY, OBS), 0)
    table_ref[...] = jnp.zeros_like(table_ref)
    table = jnp.zeros((CY, OBS), F32)
    columns, spots = [], []
    for turn in range(BATCHES):
        batch = order_ref[turn]
        owner = owner_ref[pl.ds(batch, 1), :]
        cell = cell_ref[pl.ds(batch, 1), :]
        kinds.append(kind_ref[pl.ds(batch, 1), :])
        values.append(value_ref[pl.ds(batch, 1), :])
        mask = mask_ref[pl.ds(batch, 1), :].astype(F32)
        xs.append(((owner >> 3) * CX + (cell >> 7)).astype(F32))
        ys.append(((owner & (TILES_Y - 1)) * CY + (cell & (CY - 1))).astype(F32))
        tile_x = owner >> 3
        columns.append(tile_x + REACH)
        for row, value in enumerate((xs[turn], ys[turn], mask, tile_x.astype(F32))):
            table = jnp.where(sub == turn * 4 + row, value, table)
        prior = upper[turn * MEMBERS : (turn + 1) * MEMBERS]
        centre = jnp.sum(prior, axis=0, keepdims=True) * (1.0 / MEMBERS)
        factor = jnp.where(kinds[turn] == 0, stretch[0], stretch[2])
        state_ref[:, AHEAD + turn * OBS : AHEAD + (turn + 1) * OBS] = centre + factor * (prior - centre)
        strip = ((tile_x >> 1) & 3) * 2 + ((owner >> 2) & 1)
        spots.append(strip * 8 + (tile_x & 1) * 4 + (owner & 3))
    for number, (turn, other) in enumerate(PAIRS):
        hot = jnp.where(sub == spots[other] + turn * HALF, 1.0, 0.0)
        spots_ref[:, number * OBS : (number + 1) * OBS] = hot.astype(BF16)
    table_ref[...] = table.T

    lane = lax.broadcasted_iota(I32, (1, CY), 1)
    cell_x = (place_x * CX).astype(F32)
    cell_y = (place_y * CY + lane).astype(F32)

    for turn in range(BATCHES):
        prior = state_ref[:, AHEAD + turn * OBS : AHEAD + (turn + 1) * OBS]
        error = jnp.where(kinds[turn] == 0, error_ref[0], error_ref[1])
        centre = jnp.sum(prior, axis=0, keepdims=True) * (1.0 / MEMBERS)
        deviation = prior - centre
        variance = jnp.sum(deviation * deviation, axis=0, keepdims=True) / (MEMBERS - 1)
        gain = (values[turn] - centre) / (variance + error)
        shrink = -1.0 / (jnp.sqrt(error * (error + variance)) + error + variance)
        drive_high, drive_low = halves(gain + shrink * deviation)
        drive_ref[:MEMBERS] = drive_high
        drive_ref[MEMBERS:] = drive_low
        scaled = deviation * (1.0 / (MEMBERS - 1))
        scaled_high = scaled.astype(BF16).astype(F32)
        scaled_low = scaled - scaled_high
        packed = jnp.concatenate(
            [scaled_high, scaled_high, scaled_low, jnp.zeros_like(scaled)], axis=0
        )
        left_ref[...] = packed.T.astype(BF16)

        later = list(range(turn + 1, BATCHES))
        blocks = [slice(group * CELLS, (group + 1) * CELLS) for group in range(GROUPS)]
        blocks += [slice(AHEAD + other * OBS, AHEAD + (other + 1) * OBS) for other in later]
        for cols in blocks:
            state = state_ref[:, cols]
            state_dev = state - jnp.sum(state, axis=0, keepdims=True) * (1.0 / MEMBERS)
            high, low = halves(state_dev)
            pack_ref[0:32, cols] = high
            pack_ref[32:64, cols] = low
            pack_ref[64:96, cols] = high
            pack_ref[96:128, cols] = jnp.zeros_like(high)

        @pl.loop(0, OBS // CHUNK)
        def _(step):
            start = pl.multiple_of(step * CHUNK, CHUNK)
            part = pl.ds(start, CHUNK)
            table = table_ref[part, :]
            x_col = table[:, turn * 4 : turn * 4 + 1]
            y_col = table[:, turn * 4 + 1 : turn * 4 + 2]
            mask_col = table[:, turn * 4 + 2 : turn * 4 + 3]
            gap_y = y_col - cell_y
            drop_y = gap_y * gap_y * (1.0 / (LOC_Y * LOC_Y))
            for x in range(CX):
                gap_x = jnp.abs(x_col - (cell_x + x))
                gap_x = jnp.minimum(gap_x, NX - gap_x)
                room = jnp.maximum((1.0 - gap_x * gap_x * (1.0 / (LOC_X * LOC_X))) - drop_y, 0.0)
                weight_ref[:, x * CY : (x + 1) * CY] = room * room * mask_col
            if later:
                column = table[:, turn * 4 + 3 : turn * 4 + 4].astype(I32)
                marks = recv_ref[pl.ds(2 * start + 1, CHUNK, stride=2), :].astype(BF16)
                for place, other in enumerate(later):
                    number = PAIRS.index((turn, other))
                    allowed = mm(marks, spots_ref[:, number * OBS : (number + 1) * OBS])
                    apart = (columns[other] - column) & (TILES_X - 1)
                    allowed = jnp.where(apart < SPAN, allowed, 0.0)
                    gap_x = jnp.abs(x_col - xs[other])
                    gap_x = jnp.minimum(gap_x, NX - gap_x)
                    gap_y = y_col - ys[other]
                    room = 1.0 - gap_x * gap_x * (1.0 / (LOC_X * LOC_X))
                    room = jnp.maximum(room - gap_y * gap_y * (1.0 / (LOC_Y * LOC_Y)), 0.0)
                    weight_ref[:, (place + 1) * OBS : (place + 2) * OBS] = room * room * allowed

            left = left_ref[part, :]
            drive = drive_ref[:, part]
            for number, cols in enumerate(blocks):
                at = max(0, number - GROUPS + 1) * OBS
                covariance = mm(left, pack_ref[:, cols]) * weight_ref[:, at : at + OBS]
                high, low = halves(covariance)
                both = mm(drive, high)
                rest = mm(drive[:MEMBERS], low)
                state_ref[:, cols] += both[:MEMBERS] + both[MEMBERS:] + rest

    for group in range(GROUPS):
        for x in range(CX):
            at = group * CELLS + x * CY
            out_ref[rows_of(group, x), :] = state_ref[:, at : at + CY]


def call(kernel, specs, outs, scratch=()):
    return pl.pallas_call(
        kernel,
        in_specs=specs,
        out_specs=[VMEM] * len(outs) if len(outs) > 1 else VMEM,
        out_shape=outs if len(outs) > 1 else outs[0],
        scratch_shapes=list(scratch),
        compiler_params=pltpu.CompilerParams(vmem_limit_bytes=48 * 1024 * 1024),
    )


def shape(*dims):
    return jax.ShapeDtypeStruct(dims, F32)


def swapped(value, axis, step, periodic):
    count = lax.axis_size(axis)
    pairs = []
    for source in range(count):
        target = source + (step if source % 2 == 0 else -step)
        if periodic or 0 <= target < count:
            pairs.append((source, target % count))
    return lax.ppermute(value, axis, pairs)


def local(
    ensemble,
    courant,
    target_spread,
    obs_error,
    obs_value,
    obs_owner,
    obs_cell,
    obs_kind,
    tile_mask,
    batch_order,
):
    place_x = lax.axis_index(GX)
    place_y = lax.axis_index(GY)
    relay = lax.axis_index(PLANE) * LAYERS + lax.axis_index(LAYER)
    place = jnp.stack([place_x, place_y, relay]).astype(I32)
    ens = ensemble.reshape(MEMBERS * GROUPS * CX, CY)
    mask = tile_mask.reshape(BATCHES, OBS)
    own, first, second, send = call(
        spread_kernel,
        [SMEM] * 3 + [VMEM] * 5,
        [
            shape(GROUPS, MEMBERS, CELLS),
            shape(SIDE, CY),
            shape(SIDE, CY),
            shape(PLANES * PLANE_ROWS, CY),
        ],
    )(batch_order, place, courant, ens, obs_owner, obs_cell, obs_kind, mask)
    recv = lax.all_to_all(send.reshape(PLANES, PLANE_ROWS, CY), PLANE, 0, 0)
    first = swapped(first, GX, 1, True)
    second = swapped(second, GX, -1, True)
    joined, send = call(
        collect_kernel,
        [SMEM] + [VMEM] * 4,
        [shape(GROUPS, MEMBERS, CELLS), shape(LAYERS * LAYER_ROWS, CY)],
    )(place, recv.reshape(PLANES * PLANE_ROWS, CY), own, first, second)
    recv = lax.all_to_all(send.reshape(LAYERS, LAYER_ROWS, CY), LAYER, 0, 0)
    recv = recv.reshape(LAYERS * LAYER_ROWS, CY)
    forecast, send = call(
        merge_kernel,
        [SMEM] * 3 + [VMEM] * 2,
        [shape(GROUPS, MEMBERS, CELLS), shape(2 * LAYERS, CY)],
    )(batch_order, place, obs_owner, joined, recv)
    recv = lax.all_to_all(send.reshape(LAYERS, 2, CY), LAYER, 0, 0)
    send = jnp.broadcast_to(recv.reshape(1, 2 * LAYERS, CY), (PLANES, 2 * LAYERS, CY))
    recv = lax.all_to_all(send, PLANE, 0, 0)
    out = call(
        assimilate_kernel,
        [SMEM] * 4 + [VMEM] * 7,
        [shape(MEMBERS * GROUPS * CX, CY)],
        [
            pltpu.VMEM((MEMBERS, AHEAD + BATCHES * OBS), F32),
            pltpu.VMEM((CY, AHEAD + BATCHES * OBS), BF16),
            pltpu.VMEM((OBS, CY), BF16),
            pltpu.VMEM((2 * MEMBERS, OBS), BF16),
            pltpu.VMEM((OBS, CY), F32),
            pltpu.VMEM((CY, BATCHES * OBS), BF16),
            pltpu.VMEM((CHUNK, BATCHES * OBS), F32),
        ],
    )(
        batch_order,
        place,
        target_spread,
        obs_error,
        forecast,
        recv.reshape(2 * TILES, CY),
        obs_owner,
        obs_cell,
        obs_kind,
        obs_value,
        mask,
    )
    return out.reshape(ensemble.shape)


def solution(mesh):
    fine = Mesh(mesh.devices.reshape(4, 8, 2, 2, 4), ("x", "z_lo", "core", "z_hi", "y"))
    in_specs = (
        P(None, None, None, GX, GY),
        P(),
        P(),
        P(),
        P(),
        P(),
        P(),
        P(),
        P(None, GX, GY, None),
        P(),
    )
    out_specs = P(None, None, None, GX, GY)
    return jax.shard_map(local, mesh=fine, in_specs=in_specs, out_specs=out_specs, check_vma=False)
```

```python
import jax
import jax.numpy as jnp
from jax import lax
from jax.experimental import pallas as pl
from jax.experimental.pallas import tpu as pltpu
from jax.sharding import Mesh
from jax.sharding import PartitionSpec as P

MEMBERS = 32
GROUPS = 4
CX = 4
CY = 128
CELLS = CX * CY
OBS = 512
BATCHES = 3
STEPS = 2
TILES_X = 64
TILES_Y = 8
TILES = TILES_X * TILES_Y
NX = TILES_X * CX
NY = TILES_Y * CY
LOC_X = 12.0
LOC_Y = 512.0
REACH = 2
SPAN = 2 * REACH + 1
PLANES = 32
LAYERS = 16
HALF = CY // 2
RIM = 16
VALUES = BATCHES * MEMBERS
PLANE_ROWS = LAYERS + RIM
LAYER_ROWS = 24
WIDE = (CX + 4) * CY
SIDE = 2 * GROUPS * MEMBERS
GX = ("x", "z_lo", "core")
GY = ("z_hi", "y")
PLANE = ("x", "core", "y")
LAYER = ("z_lo", "z_hi")
CHUNK = 256
GATHER = 128
AHEAD = GROUPS * CELLS
PAIRS = ((0, 1), (0, 2), (1, 2))

diffuse_rate = 0.1
mixing_rate = 0.05
spread_floor = 1e-05

F32 = jnp.float32
BF16 = jnp.bfloat16
I32 = jnp.int32

VMEM = pl.BlockSpec(memory_space=pltpu.VMEM)
SMEM = pl.BlockSpec(memory_space=pltpu.SMEM)


def rows_of(group, x):
    return pl.ds(group * CX + x, MEMBERS, stride=GROUPS * CX)


def mm(a, b):
    return lax.dot_general(a, b, (((1,), (0,)), ((), ())), preferred_element_type=F32)


def flag(condition):
    return jnp.where(condition, 1.0, 0.0).astype(F32)


def halves(value):
    high = value.astype(BF16)
    return high, (value - high.astype(F32)).astype(BF16)


def thirds(value):
    high = value.astype(BF16)
    rest = value - high.astype(F32)
    middle = rest.astype(BF16)
    return high, middle, (rest - middle.astype(F32)).astype(BF16)


def advance(rows, courant_ref, keep):
    lowest = min(x for _, x in rows) - 1
    highest = max(x for _, x in rows) + 1
    width = 2 * CY
    after = {}
    for group in range(GROUPS):
        speed = courant_ref[group % 2]
        stay = 1.0 - speed - 4.0 * diffuse_rate - mixing_rate
        for x in range(lowest, highest + 1):
            terms = []
            if (group, x) in rows:
                here = rows[group, x]
                beside = pltpu.roll(here, 1, 1) + pltpu.roll(here, width - 1, 1)
                terms.append(stay * here + diffuse_rate * beside + mixing_rate * rows[group ^ 1, x])
            if (group, x - 1) in rows:
                terms.append((speed + diffuse_rate) * rows[group, x - 1])
            if (group, x + 1) in rows:
                terms.append(diffuse_rate * rows[group, x + 1])
            total = terms[0]
            for term in terms[1:]:
                total = total + term
            after[group, x] = total if keep is None else total * keep
    return after


def spread_kernel(
    order_ref,
    place_ref,
    courant_ref,
    ens_ref,
    owner_ref,
    cell_ref,
    kind_ref,
    mask_ref,
    own_ref,
    first_ref,
    second_ref,
    send_ref,
):
    place_x = place_ref[0]
    place_y = place_ref[1]
    rows = {}
    for group in range(GROUPS):
        for x in range(CX):
            own = ens_ref[rows_of(group, x), :]
            rows[group, x] = jnp.concatenate([own, jnp.zeros_like(own)], axis=1)
    lane = lax.broadcasted_iota(I32, (1, 2 * CY), 1)
    below = (lane >= 3 * CY // 2) & (place_y == 0)
    above = (lane >= CY) & (lane < 3 * CY // 2) & (place_y == TILES_Y - 1)
    keep = jnp.where(below | above, 0.0, 1.0).astype(F32)
    rows = advance(rows, courant_ref, keep)
    rows = advance(rows, courant_ref, None)
    lane = lax.broadcasted_iota(I32, (MEMBERS, CY), 1)
    low = jnp.zeros((MEMBERS, CY), F32)
    high = jnp.zeros((MEMBERS, CY), F32)
    tile = {}
    for (group, x), value in rows.items():
        tile[group, x] = value[:, :CY]
        if 0 <= x < CX:
            own_ref[group, :, x * CY : (x + 1) * CY] = tile[group, x]
        edge = value[:, CY:]
        at = group * 16 + (x + 2) * 2
        there = (lane >> 1) == at // 2
        low = jnp.where(there, pltpu.roll(edge, at + 2, 1), low)
        high = jnp.where(there, pltpu.roll(edge, at, 1) if at else edge, high)
    rim = low + pltpu.roll(high, HALF, 1)
    even = (place_x & 1) == 0
    for group in range(GROUPS):
        for x in range(2):
            at = (group * 2 + x) * MEMBERS
            first_ref[at : at + MEMBERS] = jnp.where(even, tile[group, CX + x], tile[group, x - 2])
            second_ref[at : at + MEMBERS] = jnp.where(even, tile[group, x - 2], tile[group, CX + x])
    ground = jnp.concatenate(
        [
            jnp.concatenate([tile[2 * field, x] for x in range(-2, CX + 2)], axis=1)
            for field in range(2)
        ],
        axis=0,
    )
    parts = jnp.concatenate(thirds(ground), axis=0)
    rims = jnp.concatenate(thirds(rim), axis=0)
    blocks = []
    masks = []
    for turn in range(BATCHES):
        batch = order_ref[turn]
        owner = owner_ref[pl.ds(batch, 1), :]
        cell = cell_ref[pl.ds(batch, 1), :]
        kind = kind_ref[pl.ds(batch, 1), :]
        masks.append(mask_ref[pl.ds(batch, 1), :].astype(F32))
        at_x = ((owner >> 3) - place_x) * CX + (cell >> 7) + 2
        at_x = at_x & (NX - 1)
        at_y = ((owner & (TILES_Y - 1)) - place_y) * CY + (cell & (CY - 1))
        seen = at_x < CX + 4
        index = jnp.where(seen & (at_y >= 0) & (at_y < CY), at_x * CY + at_y, -1)
        corner = kind * 32 + at_x * 2
        edge = jnp.where(seen & (at_y >= -2) & (at_y < 0), corner + at_y + 2, -1)
        edge = jnp.where(seen & (at_y >= CY) & (at_y < CY + 2), corner + at_y - CY + HALF, edge)
        picked = jnp.zeros((parts.shape[0], OBS), F32)
        for start in range(0, WIDE, CHUNK):
            spot = lax.broadcasted_iota(I32, (CHUNK, OBS), 0) + start
            hot = jnp.where(spot == index, 1.0, 0.0).astype(BF16)
            picked = picked + mm(parts[:, start : start + CHUNK], hot)
        picked = picked[0:64] + picked[64:128] + picked[128:192]
        spot = lax.broadcasted_iota(I32, (CY, OBS), 0)
        found = mm(rims, jnp.where(spot == edge, 1.0, 0.0).astype(BF16))
        found = found[0:32] + found[32:64] + found[64:96]
        blocks.append(jnp.where(kind == 0, picked[0:32], picked[32:64]) + found)
    sub = lax.broadcasted_iota(I32, (MEMBERS, OBS), 0)
    blocks.append(jnp.where(sub == 0, masks[0], jnp.where(sub == 1, masks[1], 0.0)))
    turned = jnp.concatenate(blocks, axis=0).T
    lane = lax.broadcasted_iota(I32, (RIM, CY), 1)
    low = jnp.where(lane < HALF, low[:RIM], pltpu.roll(low[RIM:], HALF, 1))
    high = jnp.where(lane < HALF, high[:RIM], pltpu.roll(high[RIM:], HALF, 1))
    y = place_y & 3
    for plane in range(PLANES):
        at = plane * PLANE_ROWS
        send_ref[at : at + LAYERS, :] = turned[plane * LAYERS : (plane + 1) * LAYERS]
        up = flag((y + 1) & 3 == plane & 3)
        down = flag((y + 3) & 3 == plane & 3)
        send_ref[at + LAYERS : at + PLANE_ROWS, :] = up * high + down * low


def collect_kernel(place_ref, recv_ref, own_ref, near_ref, far_ref, joined_ref, send_ref):
    even = (place_ref[0] & 1) == 0
    for group in range(GROUPS):
        for column in range(CX):
            at = (group * 2 + column % 2) * MEMBERS
            part = slice(at, at + MEMBERS)
            near, far = near_ref[part], far_ref[part]
            other = jnp.where(even, far, near) if column < 2 else jnp.where(even, near, far)
            cells = slice(column * CY, (column + 1) * CY)
            joined_ref[group, :, cells] = own_ref[group, :, cells] + other
    place_x = place_ref[0]
    place_y = place_ref[1]
    x, z_lo, core = place_x >> 4, (place_x >> 1) & 7, place_x & 1
    z_hi, y = place_y >> 2, place_y & 3
    lane = lax.broadcasted_iota(I32, (LAYERS, CY), 1)
    total = jnp.zeros((LAYERS, CY), F32)
    marks = jnp.zeros((LAYERS, CY), F32)
    for plane in range(PLANES):
        rows = recv_ref[plane * PLANE_ROWS : plane * PLANE_ROWS + LAYERS, :]
        total = total + rows
        for turn in range(2):
            at = VALUES + turn
            marks = jnp.where(lane == turn * PLANES + plane, rows[:, at : at + 1], marks)

    spot = lane & 15
    hop = jnp.where(core == 0, z_lo == 7, z_lo == 0)
    side = jnp.where(hop, (x + jnp.where(core == 0, 3, 1)) & 3, x)
    first = flag(core == 0)
    second = 1.0 - first

    def rim(column, other, step):
        plane = (column * 2 + other) * 4 + ((y + step) & 3)
        start = pl.multiple_of(plane * PLANE_ROWS + LAYERS, RIM)
        return recv_ref[pl.ds(start, RIM), :]

    def from_left(block):
        return jnp.where((spot >= 4) & (spot < 8), pltpu.roll(block, CY - 8, 1), 0.0)

    def from_right(block):
        return jnp.where((spot >= 8) & (spot < 12), pltpu.roll(block, 8, 1), 0.0)

    here, there = [], []
    for step in (3, 1):
        mine = jnp.where((spot >= 4) & (spot < 12), rim(x, core, step), 0.0)
        twin = rim(x, 1 - core, step)
        far = rim(side, 1 - core, step)
        block = mine + first * from_right(twin) + second * from_left(twin)
        other = first * from_left(far) + second * from_right(far)
        here.append(pltpu.roll(block, 8, 1) if step == 1 else block)
        there.append(pltpu.roll(other, 8, 1) if step == 1 else other)
    target = jnp.where(core == 0, z_lo + 1, z_lo + 7) & 7
    below = jnp.where(y > 0, z_hi, jnp.where(z_hi == 0, 1, -1))
    above = jnp.where(y < 3, z_hi, jnp.where(z_hi == 1, 0, -1))
    for layer in range(LAYERS):
        lower, higher = flag(below == layer % 2), flag(above == layer % 2)
        same, next_to = flag(z_lo == layer // 2), flag(target == layer // 2)
        at = layer * LAYER_ROWS
        send_ref[at : at + RIM, :] = same * (lower * here[0] + higher * here[1]) + next_to * (
            lower * there[0] + higher * there[1]
        )
        pair = jnp.concatenate([total[layer : layer + 1], marks[layer : layer + 1]], axis=0)
        send_ref[at + RIM : at + RIM + 2, :] = pair
        send_ref[at + RIM + 2 : at + LAYER_ROWS, :] = jnp.zeros((LAYER_ROWS - RIM - 2, CY), F32)


def merge_kernel(
    order_ref,
    place_ref,
    relay_ref,
    joined_ref,
    recv_ref,
    forecast_ref,
    send_ref,
):
    relay = place_ref[2]
    lane = lax.broadcasted_iota(I32, (1, CY), 1)
    sums = recv_ref[pl.ds(RIM, LAYERS, stride=LAYER_ROWS), :]
    marks = recv_ref[pl.ds(RIM + 1, LAYERS, stride=LAYER_ROWS), :]
    top = jnp.sum(sums, axis=0, keepdims=True)
    top = jnp.where(lane < BATCHES * MEMBERS, top, 0.0)
    below = recv_ref[0:RIM, :]
    for layer in range(1, LAYERS):
        below = below + recv_ref[layer * LAYER_ROWS : layer * LAYER_ROWS + RIM, :]
    above = pltpu.roll(below, CY - 8, 1)
    below = jnp.concatenate([below, pltpu.roll(below, HALF, 1)], axis=0)
    above = jnp.concatenate([above, pltpu.roll(above, HALF, 1)], axis=0)
    wide = lax.broadcasted_iota(I32, (MEMBERS, CY), 1)
    for group in range(GROUPS):
        pieces = []
        for x in range(CX):
            at = group * 16 + (x + 2) * 2
            piece = joined_ref[group, :, x * CY : (x + 1) * CY]
            piece = piece + jnp.where(wide < 2, pltpu.roll(below, CY - at, 1), 0.0)
            piece = piece + jnp.where(wide >= CY - 2, pltpu.roll(above, CY - 2 - at, 1), 0.0)
            pieces.append(piece)
        value = jnp.concatenate(pieces, axis=1)
        forecast_ref[group] = value
        centre = jnp.sum(value, axis=0, keepdims=True) * (1.0 / MEMBERS)
        deviation = value - centre
        total = jnp.sum(jnp.sum(deviation * deviation, axis=0, keepdims=True), axis=1, keepdims=True)
        top = jnp.where(lane == BATCHES * MEMBERS + group, total, top)

    lanes = lax.broadcasted_iota(I32, (LAYERS, CY), 1)
    subs = lax.broadcasted_iota(I32, (LAYERS, CY), 0)
    tile_x = ((lanes >> 3) & 3) * 16 + (subs >> 1) * 2 + ((lanes >> 2) & 1)
    first = relay_ref[order_ref[0], relay] >> 3
    second = relay_ref[order_ref[1], relay] >> 3
    column = jnp.where(lanes < PLANES, first, second)
    near = ((tile_x - column + REACH) & (TILES_X - 1)) < SPAN
    marks = jnp.where(near & (lanes < 2 * PLANES), marks, 0.0)
    marks = marks[:8] + marks[8:]
    folded = marks
    for step in (8, 16, 24):
        folded = folded + pltpu.roll(marks, CY - step, 1)
    lanes = lax.broadcasted_iota(I32, (8, CY), 1)
    subs = lax.broadcasted_iota(I32, (8, CY), 0)
    bottom = jnp.zeros((8, CY), F32)
    for row in range(8):
        for turn in range(2):
            moved = pltpu.roll(folded, (turn * PLANES + row * 8) % CY, 1)
            there = (subs == row) & ((lanes >> 3) == turn * 8 + row)
            bottom = jnp.where(there, moved, bottom)
    bottom = jnp.sum(bottom, axis=0, keepdims=True)
    pair = jnp.concatenate([top, bottom] * 4, axis=0)
    send_ref[...] = jnp.concatenate([pair] * (2 * LAYERS // 8), axis=0)


def assimilate_kernel(
    order_ref,
    place_ref,
    spread_ref,
    error_ref,
    forecast_ref,
    recv_ref,
    owner_ref,
    cell_ref,
    kind_ref,
    value_ref,
    mask_ref,
    out_ref,
    state_ref,
    pack_ref,
    sheet_ref,
    drive_ref,
    order_of_ref,
    spots_ref,
    weight_ref,
):
    place_x = place_ref[0]
    place_y = place_ref[1]
    upper = recv_ref[pl.ds(0, TILES, stride=2), :].T
    stretch = []
    for group in range(GROUPS):
        row = BATCHES * MEMBERS + group
        total = jnp.sum(upper[row : row + 1], axis=1, keepdims=True)
        mean_var = total * (1.0 / ((MEMBERS - 1) * float(NX * NY)))
        stretch.append(jnp.sqrt(spread_ref[group // 2, group % 2] / (mean_var + spread_floor)))
    for group in range(GROUPS):
        value = forecast_ref[group]
        centre = jnp.sum(value, axis=0, keepdims=True) * (1.0 / MEMBERS)
        state_ref[:, group * CELLS : (group + 1) * CELLS] = centre + stretch[group] * (value - centre)

    kinds, xs, ys, values = [], [], [], []
    sub = lax.broadcasted_iota(I32, (CY, OBS), 0)
    table = jnp.zeros((CY, OBS), F32)
    near = []
    columns, spots = [], []
    for turn in range(BATCHES):
        batch = order_ref[turn]
        owner = owner_ref[pl.ds(batch, 1), :]
        cell = cell_ref[pl.ds(batch, 1), :]
        kinds.append(kind_ref[pl.ds(batch, 1), :])
        values.append(value_ref[pl.ds(batch, 1), :])
        mask = mask_ref[pl.ds(batch, 1), :].astype(F32)
        xs.append(((owner >> 3) * CX + (cell >> 7)).astype(F32))
        ys.append(((owner & (TILES_Y - 1)) * CY + (cell & (CY - 1))).astype(F32))
        tile_x = owner >> 3
        columns.append(tile_x + REACH)
        reach = REACH * (BATCHES - turn)
        near.append(flag(((tile_x - place_x + reach) & (TILES_X - 1)) <= 2 * reach))
        facts = (
            xs[turn],
            (owner & (TILES_Y - 1)).astype(F32),
            (cell & (CY - 1)).astype(F32),
            mask,
            tile_x.astype(F32),
        )
        for row, value in enumerate(facts):
            table = jnp.where(sub == turn * 8 + row, value, table)
        prior = upper[turn * MEMBERS : (turn + 1) * MEMBERS]
        centre = jnp.sum(prior, axis=0, keepdims=True) * (1.0 / MEMBERS)
        factor = jnp.where(kinds[turn] == 0, stretch[0], stretch[2])
        state_ref[:, AHEAD + turn * OBS : AHEAD + (turn + 1) * OBS] = centre + factor * (prior - centre)
        strip = ((tile_x >> 1) & 3) * 2 + ((owner >> 2) & 1)
        spots.append(strip * 8 + (tile_x & 1) * 4 + (owner & 3))
    for number, (turn, other) in enumerate(PAIRS):
        hot = jnp.where(sub == spots[other] + turn * HALF, 1.0, 0.0)
        spots_ref[:, number * OBS : (number + 1) * OBS] = hot.astype(BF16)
    sheet_ref[:, CY : 2 * CY] = table.T.astype(BF16)
    sheet_ref[:, 2 * CY : 3 * CY] = recv_ref[pl.ds(1, TILES, stride=2), :].astype(BF16)
    ahead = lax.broadcasted_iota(I32, (OBS, OBS), 0) <= lax.broadcasted_iota(I32, (OBS, OBS), 1)
    counts = jnp.concatenate([*near, jnp.zeros((8 - BATCHES, OBS), F32)], axis=0)
    counts = mm(counts.astype(BF16), jnp.where(ahead, 1.0, 0.0).astype(BF16))
    for turn in range(BATCHES):
        slot = jnp.where(near[turn] > 0.0, counts[turn : turn + 1] - 1.0, -1.0)
        order_of_ref[turn : turn + 1] = slot.astype(I32)

    lane = lax.broadcasted_iota(I32, (1, CY), 1)
    cell_x = (place_x * CX).astype(F32)
    cell_y = (place_y * CY + lane).astype(F32)

    for turn in range(BATCHES):
        prior = state_ref[:, AHEAD + turn * OBS : AHEAD + (turn + 1) * OBS]
        error = jnp.where(kinds[turn] == 0, error_ref[0], error_ref[1])
        centre = jnp.sum(prior, axis=0, keepdims=True) * (1.0 / MEMBERS)
        deviation = prior - centre
        variance = jnp.sum(deviation * deviation, axis=0, keepdims=True) / (MEMBERS - 1)
        gain = (values[turn] - centre) / (variance + error)
        shrink = -1.0 / (jnp.sqrt(error * (error + variance)) + error + variance)
        drive_high, drive_low = halves(gain + shrink * deviation)
        drive_ref[:MEMBERS] = drive_high
        drive_ref[MEMBERS:] = drive_low
        scaled = deviation * (1.0 / (MEMBERS - 1))
        scaled_high = scaled.astype(BF16).astype(F32)
        scaled_low = scaled - scaled_high
        packed = jnp.concatenate(
            [scaled_high, scaled_high, scaled_low, jnp.zeros_like(scaled)], axis=0
        )
        sheet_ref[:, :CY] = packed.T.astype(BF16)

        later = list(range(turn + 1, BATCHES))
        blocks = [slice(group * CELLS, (group + 1) * CELLS) for group in range(GROUPS)]
        blocks += [slice(AHEAD + other * OBS, AHEAD + (other + 1) * OBS) for other in later]
        for cols in blocks:
            state = state_ref[:, cols]
            state_dev = state - jnp.sum(state, axis=0, keepdims=True) * (1.0 / MEMBERS)
            high, low = halves(state_dev)
            pack_ref[0:32, cols] = high
            pack_ref[32:64, cols] = low
            pack_ref[64:96, cols] = high
            pack_ref[96:128, cols] = jnp.zeros_like(high)

        total = jnp.sum(near[turn])
        trips = jnp.int32(0)
        for start in range(0, OBS, GATHER):
            trips = trips + jnp.where(total > float(start), 1, 0)
        slot = order_of_ref[turn : turn + 1]

        @pl.loop(0, trips)
        def _(step):
            place = lax.broadcasted_iota(I32, (GATHER, OBS), 0) + step * GATHER
            hot = jnp.where(place == slot, 1.0, 0.0).astype(BF16)
            sheet = mm(hot, sheet_ref[...])
            left = sheet[:, :CY].astype(BF16)
            table = sheet[:, CY : 2 * CY]
            marks = sheet[:, 2 * CY :].astype(BF16)
            drive = lax.dot_general(
                drive_ref[...], hot, (((1,), (1,)), ((), ())), preferred_element_type=F32
            ).astype(BF16)
            x_col = table[:, turn * 8 : turn * 8 + 1]
            y_col = table[:, turn * 8 + 1 : turn * 8 + 2] * CY + table[:, turn * 8 + 2 : turn * 8 + 3]
            mask_col = table[:, turn * 8 + 3 : turn * 8 + 4]
            gap_y = y_col - cell_y
            drop_y = gap_y * gap_y * (1.0 / (LOC_Y * LOC_Y))
            for x in range(CX):
                gap_x = jnp.abs(x_col - (cell_x + x))
                gap_x = jnp.minimum(gap_x, NX - gap_x)
                room = jnp.maximum((1.0 - gap_x * gap_x * (1.0 / (LOC_X * LOC_X))) - drop_y, 0.0)
                weight_ref[:, x * CY : (x + 1) * CY] = room * room * mask_col
            if later:
                column = table[:, turn * 8 + 4 : turn * 8 + 5].astype(I32)
                for index, other in enumerate(later):
                    number = PAIRS.index((turn, other))
                    allowed = mm(marks, spots_ref[:, number * OBS : (number + 1) * OBS])
                    apart = (columns[other] - column) & (TILES_X - 1)
                    allowed = jnp.where(apart < SPAN, allowed, 0.0)
                    gap_x = jnp.abs(x_col - xs[other])
                    gap_x = jnp.minimum(gap_x, NX - gap_x)
                    gap_y = y_col - ys[other]
                    room = 1.0 - gap_x * gap_x * (1.0 / (LOC_X * LOC_X))
                    room = jnp.maximum(room - gap_y * gap_y * (1.0 / (LOC_Y * LOC_Y)), 0.0)
                    weight_ref[:, (index + 1) * OBS : (index + 2) * OBS] = room * room * allowed

            for number, cols in enumerate(blocks):
                at = max(0, number - GROUPS + 1) * OBS
                covariance = mm(left, pack_ref[:, cols]) * weight_ref[:, at : at + OBS]
                high, low = halves(covariance)
                both = mm(drive, high)
                rest = mm(drive[:MEMBERS], low)
                state_ref[:, cols] += both[:MEMBERS] + both[MEMBERS:] + rest

    for group in range(GROUPS):
        for x in range(CX):
            at = group * CELLS + x * CY
            out_ref[rows_of(group, x), :] = state_ref[:, at : at + CY]


def call(kernel, specs, outs, scratch=()):
    return pl.pallas_call(
        kernel,
        in_specs=specs,
        out_specs=[VMEM] * len(outs) if len(outs) > 1 else VMEM,
        out_shape=outs if len(outs) > 1 else outs[0],
        scratch_shapes=list(scratch),
        compiler_params=pltpu.CompilerParams(vmem_limit_bytes=48 * 1024 * 1024),
    )


def shape(*dims):
    return jax.ShapeDtypeStruct(dims, F32)


def swapped(value, axis, step, periodic):
    count = lax.axis_size(axis)
    pairs = []
    for source in range(count):
        target = source + (step if source % 2 == 0 else -step)
        if periodic or 0 <= target < count:
            pairs.append((source, target % count))
    return lax.ppermute(value, axis, pairs)


def local(
    ensemble,
    courant,
    target_spread,
    obs_error,
    obs_value,
    obs_owner,
    obs_cell,
    obs_kind,
    tile_mask,
    batch_order,
):
    place_x = lax.axis_index(GX)
    place_y = lax.axis_index(GY)
    relay = lax.axis_index(PLANE) * LAYERS + lax.axis_index(LAYER)
    place = jnp.stack([place_x, place_y, relay]).astype(I32)
    ens = ensemble.reshape(MEMBERS * GROUPS * CX, CY)
    mask = tile_mask.reshape(BATCHES, OBS)
    own, first, second, send = call(
        spread_kernel,
        [SMEM] * 3 + [VMEM] * 5,
        [
            shape(GROUPS, MEMBERS, CELLS),
            shape(SIDE, CY),
            shape(SIDE, CY),
            shape(PLANES * PLANE_ROWS, CY),
        ],
    )(batch_order, place, courant, ens, obs_owner, obs_cell, obs_kind, mask)
    recv = lax.all_to_all(send.reshape(PLANES, PLANE_ROWS, CY), PLANE, 0, 0)
    first = swapped(first, GX, 1, True)
    second = swapped(second, GX, -1, True)
    joined, send = call(
        collect_kernel,
        [SMEM] + [VMEM] * 4,
        [shape(GROUPS, MEMBERS, CELLS), shape(LAYERS * LAYER_ROWS, CY)],
    )(place, recv.reshape(PLANES * PLANE_ROWS, CY), own, first, second)
    recv = lax.all_to_all(send.reshape(LAYERS, LAYER_ROWS, CY), LAYER, 0, 0)
    recv = recv.reshape(LAYERS * LAYER_ROWS, CY)
    forecast, send = call(
        merge_kernel,
        [SMEM] * 3 + [VMEM] * 2,
        [shape(GROUPS, MEMBERS, CELLS), shape(2 * LAYERS, CY)],
    )(batch_order, place, obs_owner, joined, recv)
    recv = lax.all_to_all(send.reshape(LAYERS, 2, CY), LAYER, 0, 0)
    send = jnp.broadcast_to(recv.reshape(1, 2 * LAYERS, CY), (PLANES, 2 * LAYERS, CY))
    recv = lax.all_to_all(send, PLANE, 0, 0)
    out = call(
        assimilate_kernel,
        [SMEM] * 4 + [VMEM] * 7,
        [shape(MEMBERS * GROUPS * CX, CY)],
        [
            pltpu.VMEM((MEMBERS, AHEAD + BATCHES * OBS), F32),
            pltpu.VMEM((CY, AHEAD + BATCHES * OBS), BF16),
            pltpu.VMEM((OBS, 3 * CY), BF16),
            pltpu.VMEM((2 * MEMBERS, OBS), BF16),
            pltpu.VMEM((8, OBS), I32),
            pltpu.VMEM((CY, BATCHES * OBS), BF16),
            pltpu.VMEM((GATHER, BATCHES * OBS), F32),
        ],
    )(
        batch_order,
        place,
        target_spread,
        obs_error,
        forecast,
        recv.reshape(2 * TILES, CY),
        obs_owner,
        obs_cell,
        obs_kind,
        obs_value,
        mask,
    )
    return out.reshape(ensemble.shape)


def solution(mesh):
    fine = Mesh(mesh.devices.reshape(4, 8, 2, 2, 4), ("x", "z_lo", "core", "z_hi", "y"))
    in_specs = (
        P(None, None, None, GX, GY),
        P(),
        P(),
        P(),
        P(),
        P(),
        P(),
        P(),
        P(None, GX, GY, None),
        P(),
    )
    out_specs = P(None, None, None, GX, GY)
    return jax.shard_map(local, mesh=fine, in_specs=in_specs, out_specs=out_specs, check_vma=False)
```

```python
import jax
import jax.numpy as jnp
from jax import lax
from jax.experimental import pallas as pl
from jax.experimental.pallas import tpu as pltpu
from jax.sharding import Mesh
from jax.sharding import PartitionSpec as P

MEMBERS = 32
GROUPS = 4
CX = 4
CY = 128
CELLS = CX * CY
OBS = 512
BATCHES = 3
STEPS = 2
TILES_X = 64
TILES_Y = 8
TILES = TILES_X * TILES_Y
NX = TILES_X * CX
NY = TILES_Y * CY
LOC_X = 12.0
LOC_Y = 512.0
REACH = 2
SPAN = 2 * REACH + 1
PLANES = 32
LAYERS = 16
HALF = CY // 2
RIM = 16
VALUES = BATCHES * MEMBERS
PLANE_ROWS = LAYERS + RIM
LAYER_ROWS = 24
WIDE = (CX + 4) * CY
SIDE = 2 * GROUPS * MEMBERS
GX = ("x", "z_lo", "core")
GY = ("z_hi", "y")
PLANE = ("x", "core", "y")
LAYER = ("z_lo", "z_hi")
CHIP = ("x", "y")
CHUNK = 256
GATHER = 128
AHEAD = GROUPS * CELLS
PAIRS = ((0, 1), (0, 2), (1, 2))

diffuse_rate = 0.1
mixing_rate = 0.05
spread_floor = 1e-05

F32 = jnp.float32
BF16 = jnp.bfloat16
I32 = jnp.int32

VMEM = pl.BlockSpec(memory_space=pltpu.VMEM)
SMEM = pl.BlockSpec(memory_space=pltpu.SMEM)


def rows_of(group, x):
    return pl.ds(group * CX + x, MEMBERS, stride=GROUPS * CX)


def mm(a, b):
    return lax.dot_general(a, b, (((1,), (0,)), ((), ())), preferred_element_type=F32)


def flag(condition):
    return jnp.where(condition, 1.0, 0.0).astype(F32)


def halves(value):
    high = value.astype(BF16)
    return high, (value - high.astype(F32)).astype(BF16)


def thirds(value):
    high = value.astype(BF16)
    rest = value - high.astype(F32)
    middle = rest.astype(BF16)
    return high, middle, (rest - middle.astype(F32)).astype(BF16)


def advance(rows, courant_ref, keep):
    lowest = min(x for _, x in rows) - 1
    highest = max(x for _, x in rows) + 1
    width = 2 * CY
    after = {}
    for group in range(GROUPS):
        speed = courant_ref[group % 2]
        stay = 1.0 - speed - 4.0 * diffuse_rate - mixing_rate
        for x in range(lowest, highest + 1):
            terms = []
            if (group, x) in rows:
                here = rows[group, x]
                beside = pltpu.roll(here, 1, 1) + pltpu.roll(here, width - 1, 1)
                terms.append(stay * here + diffuse_rate * beside + mixing_rate * rows[group ^ 1, x])
            if (group, x - 1) in rows:
                terms.append((speed + diffuse_rate) * rows[group, x - 1])
            if (group, x + 1) in rows:
                terms.append(diffuse_rate * rows[group, x + 1])
            total = terms[0]
            for term in terms[1:]:
                total = total + term
            after[group, x] = total if keep is None else total * keep
    return after


def spread_kernel(
    order_ref,
    place_ref,
    courant_ref,
    ens_ref,
    owner_ref,
    cell_ref,
    kind_ref,
    mask_ref,
    own_ref,
    first_ref,
    second_ref,
    send_ref,
):
    place_x = place_ref[0]
    place_y = place_ref[1]
    rows = {}
    for group in range(GROUPS):
        for x in range(CX):
            own = ens_ref[rows_of(group, x), :]
            rows[group, x] = jnp.concatenate([own, jnp.zeros_like(own)], axis=1)
    lane = lax.broadcasted_iota(I32, (1, 2 * CY), 1)
    below = (lane >= 3 * CY // 2) & (place_y == 0)
    above = (lane >= CY) & (lane < 3 * CY // 2) & (place_y == TILES_Y - 1)
    keep = jnp.where(below | above, 0.0, 1.0).astype(F32)
    rows = advance(rows, courant_ref, keep)
    rows = advance(rows, courant_ref, None)
    lane = lax.broadcasted_iota(I32, (MEMBERS, CY), 1)
    low = jnp.zeros((MEMBERS, CY), F32)
    high = jnp.zeros((MEMBERS, CY), F32)
    tile = {}
    for (group, x), value in rows.items():
        tile[group, x] = value[:, :CY]
        if 0 <= x < CX:
            own_ref[group, :, x * CY : (x + 1) * CY] = tile[group, x]
        edge = value[:, CY:]
        at = group * 16 + (x + 2) * 2
        there = (lane >> 1) == at // 2
        low = jnp.where(there, pltpu.roll(edge, at + 2, 1), low)
        high = jnp.where(there, pltpu.roll(edge, at, 1) if at else edge, high)
    rim = low + pltpu.roll(high, HALF, 1)
    even = (place_x & 1) == 0
    for group in range(GROUPS):
        for x in range(2):
            at = (group * 2 + x) * MEMBERS
            first_ref[at : at + MEMBERS] = jnp.where(even, tile[group, CX + x], tile[group, x - 2])
            second_ref[at : at + MEMBERS] = jnp.where(even, tile[group, x - 2], tile[group, CX + x])
    ground = jnp.concatenate(
        [
            jnp.concatenate([tile[2 * field, x] for x in range(-2, CX + 2)], axis=1)
            for field in range(2)
        ],
        axis=0,
    )
    parts = jnp.concatenate(thirds(ground), axis=0)
    rims = jnp.concatenate(thirds(rim), axis=0)
    blocks = []
    masks = []
    for turn in range(BATCHES):
        batch = order_ref[turn]
        owner = owner_ref[pl.ds(batch, 1), :]
        cell = cell_ref[pl.ds(batch, 1), :]
        kind = kind_ref[pl.ds(batch, 1), :]
        masks.append(mask_ref[pl.ds(batch, 1), :].astype(F32))
        at_x = ((owner >> 3) - place_x) * CX + (cell >> 7) + 2
        at_x = at_x & (NX - 1)
        at_y = ((owner & (TILES_Y - 1)) - place_y) * CY + (cell & (CY - 1))
        seen = at_x < CX + 4
        index = jnp.where(seen & (at_y >= 0) & (at_y < CY), at_x * CY + at_y, -1)
        corner = kind * 32 + at_x * 2
        edge = jnp.where(seen & (at_y >= -2) & (at_y < 0), corner + at_y + 2, -1)
        edge = jnp.where(seen & (at_y >= CY) & (at_y < CY + 2), corner + at_y - CY + HALF, edge)
        picked = jnp.zeros((parts.shape[0], OBS), F32)
        for start in range(0, WIDE, CHUNK):
            spot = lax.broadcasted_iota(I32, (CHUNK, OBS), 0) + start
            hot = jnp.where(spot == index, 1.0, 0.0).astype(BF16)
            picked = picked + mm(parts[:, start : start + CHUNK], hot)
        picked = picked[0:64] + picked[64:128] + picked[128:192]
        spot = lax.broadcasted_iota(I32, (CY, OBS), 0)
        found = mm(rims, jnp.where(spot == edge, 1.0, 0.0).astype(BF16))
        found = found[0:32] + found[32:64] + found[64:96]
        blocks.append(jnp.where(kind == 0, picked[0:32], picked[32:64]) + found)
    sub = lax.broadcasted_iota(I32, (MEMBERS, OBS), 0)
    blocks.append(jnp.where(sub == 0, masks[0], jnp.where(sub == 1, masks[1], 0.0)))
    turned = jnp.concatenate(blocks, axis=0).T
    lane = lax.broadcasted_iota(I32, (RIM, CY), 1)
    low = jnp.where(lane < HALF, low[:RIM], pltpu.roll(low[RIM:], HALF, 1))
    high = jnp.where(lane < HALF, high[:RIM], pltpu.roll(high[RIM:], HALF, 1))
    y = place_y & 3
    for plane in range(PLANES):
        at = plane * PLANE_ROWS
        send_ref[at : at + LAYERS, :] = turned[plane * LAYERS : (plane + 1) * LAYERS]
        up = flag((y + 1) & 3 == plane & 3)
        down = flag((y + 3) & 3 == plane & 3)
        send_ref[at + LAYERS : at + PLANE_ROWS, :] = up * high + down * low


def collect_kernel(place_ref, recv_ref, own_ref, near_ref, far_ref, joined_ref, send_ref):
    even = (place_ref[0] & 1) == 0
    for group in range(GROUPS):
        for column in range(CX):
            at = (group * 2 + column % 2) * MEMBERS
            part = slice(at, at + MEMBERS)
            near, far = near_ref[part], far_ref[part]
            other = jnp.where(even, far, near) if column < 2 else jnp.where(even, near, far)
            cells = slice(column * CY, (column + 1) * CY)
            joined_ref[group, :, cells] = own_ref[group, :, cells] + other
    place_x = place_ref[0]
    place_y = place_ref[1]
    x, z_lo, core = place_x >> 4, (place_x >> 1) & 7, place_x & 1
    z_hi, y = place_y >> 2, place_y & 3
    lane = lax.broadcasted_iota(I32, (LAYERS, CY), 1)
    total = jnp.zeros((LAYERS, CY), F32)
    marks = jnp.zeros((LAYERS, CY), F32)
    for plane in range(PLANES):
        rows = recv_ref[plane * PLANE_ROWS : plane * PLANE_ROWS + LAYERS, :]
        total = total + rows
        for turn in range(2):
            at = VALUES + turn
            marks = jnp.where(lane == turn * PLANES + plane, rows[:, at : at + 1], marks)

    spot = lane & 15
    hop = jnp.where(core == 0, z_lo == 7, z_lo == 0)
    side = jnp.where(hop, (x + jnp.where(core == 0, 3, 1)) & 3, x)
    first = flag(core == 0)
    second = 1.0 - first

    def rim(column, other, step):
        plane = (column * 2 + other) * 4 + ((y + step) & 3)
        start = pl.multiple_of(plane * PLANE_ROWS + LAYERS, RIM)
        return recv_ref[pl.ds(start, RIM), :]

    def from_left(block):
        return jnp.where((spot >= 4) & (spot < 8), pltpu.roll(block, CY - 8, 1), 0.0)

    def from_right(block):
        return jnp.where((spot >= 8) & (spot < 12), pltpu.roll(block, 8, 1), 0.0)

    here, there = [], []
    for step in (3, 1):
        mine = jnp.where((spot >= 4) & (spot < 12), rim(x, core, step), 0.0)
        twin = rim(x, 1 - core, step)
        far = rim(side, 1 - core, step)
        block = mine + first * from_right(twin) + second * from_left(twin)
        other = first * from_left(far) + second * from_right(far)
        here.append(pltpu.roll(block, 8, 1) if step == 1 else block)
        there.append(pltpu.roll(other, 8, 1) if step == 1 else other)
    target = jnp.where(core == 0, z_lo + 1, z_lo + 7) & 7
    below = jnp.where(y > 0, z_hi, jnp.where(z_hi == 0, 1, -1))
    above = jnp.where(y < 3, z_hi, jnp.where(z_hi == 1, 0, -1))
    for layer in range(LAYERS):
        lower, higher = flag(below == layer % 2), flag(above == layer % 2)
        same, next_to = flag(z_lo == layer // 2), flag(target == layer // 2)
        at = layer * LAYER_ROWS
        send_ref[at : at + RIM, :] = same * (lower * here[0] + higher * here[1]) + next_to * (
            lower * there[0] + higher * there[1]
        )
        pair = jnp.concatenate([total[layer : layer + 1], marks[layer : layer + 1]], axis=0)
        send_ref[at + RIM : at + RIM + 2, :] = pair
        send_ref[at + RIM + 2 : at + LAYER_ROWS, :] = jnp.zeros((LAYER_ROWS - RIM - 2, CY), F32)


def merge_kernel(
    order_ref,
    place_ref,
    relay_ref,
    joined_ref,
    recv_ref,
    forecast_ref,
    send_ref,
):
    relay = place_ref[2]
    lane = lax.broadcasted_iota(I32, (1, CY), 1)
    sums = recv_ref[pl.ds(RIM, LAYERS, stride=LAYER_ROWS), :]
    marks = recv_ref[pl.ds(RIM + 1, LAYERS, stride=LAYER_ROWS), :]
    top = jnp.sum(sums, axis=0, keepdims=True)
    top = jnp.where(lane < BATCHES * MEMBERS, top, 0.0)
    below = recv_ref[0:RIM, :]
    for layer in range(1, LAYERS):
        below = below + recv_ref[layer * LAYER_ROWS : layer * LAYER_ROWS + RIM, :]
    above = pltpu.roll(below, CY - 8, 1)
    below = jnp.concatenate([below, pltpu.roll(below, HALF, 1)], axis=0)
    above = jnp.concatenate([above, pltpu.roll(above, HALF, 1)], axis=0)
    wide = lax.broadcasted_iota(I32, (MEMBERS, CY), 1)
    for group in range(GROUPS):
        pieces = []
        for x in range(CX):
            at = group * 16 + (x + 2) * 2
            piece = joined_ref[group, :, x * CY : (x + 1) * CY]
            piece = piece + jnp.where(wide < 2, pltpu.roll(below, CY - at, 1), 0.0)
            piece = piece + jnp.where(wide >= CY - 2, pltpu.roll(above, CY - 2 - at, 1), 0.0)
            pieces.append(piece)
        value = jnp.concatenate(pieces, axis=1)
        forecast_ref[group] = value
        centre = jnp.sum(value, axis=0, keepdims=True) * (1.0 / MEMBERS)
        deviation = value - centre
        total = jnp.sum(jnp.sum(deviation * deviation, axis=0, keepdims=True), axis=1, keepdims=True)
        top = jnp.where(lane == BATCHES * MEMBERS + group, total, top)

    lanes = lax.broadcasted_iota(I32, (LAYERS, CY), 1)
    subs = lax.broadcasted_iota(I32, (LAYERS, CY), 0)
    tile_x = ((lanes >> 3) & 3) * 16 + (subs >> 1) * 2 + ((lanes >> 2) & 1)
    first = relay_ref[order_ref[0], relay] >> 3
    second = relay_ref[order_ref[1], relay] >> 3
    column = jnp.where(lanes < PLANES, first, second)
    near = ((tile_x - column + REACH) & (TILES_X - 1)) < SPAN
    marks = jnp.where(near & (lanes < 2 * PLANES), marks, 0.0)
    marks = marks[:8] + marks[8:]
    folded = marks
    for step in (8, 16, 24):
        folded = folded + pltpu.roll(marks, CY - step, 1)
    lanes = lax.broadcasted_iota(I32, (8, CY), 1)
    subs = lax.broadcasted_iota(I32, (8, CY), 0)
    bottom = jnp.zeros((8, CY), F32)
    for row in range(8):
        for turn in range(2):
            moved = pltpu.roll(folded, (turn * PLANES + row * 8) % CY, 1)
            there = (subs == row) & ((lanes >> 3) == turn * 8 + row)
            bottom = jnp.where(there, moved, bottom)
    bottom = jnp.sum(bottom, axis=0, keepdims=True)
    pair = jnp.concatenate([top, bottom] * 4, axis=0)
    send_ref[...] = jnp.concatenate([pair] * (2 * LAYERS // 8), axis=0)


def assimilate_kernel(
    order_ref,
    place_ref,
    spread_ref,
    error_ref,
    forecast_ref,
    mine_ref,
    twin_ref,
    owner_ref,
    cell_ref,
    kind_ref,
    value_ref,
    mask_ref,
    out_ref,
    state_ref,
    pack_ref,
    sheet_ref,
    drive_ref,
    order_of_ref,
    spots_ref,
    weight_ref,
    recv_ref,
):
    place_x = place_ref[0]
    place_y = place_ref[1]
    first = (place_x & 1) == 0
    for plane in range(PLANES):
        source = (plane // 8 * 4 + plane % 4) * 2 * LAYERS
        source = slice(source, source + 2 * LAYERS)
        mine, twin = mine_ref[source], twin_ref[source]
        rows = jnp.where(first, twin, mine) if plane // 4 % 2 else jnp.where(first, mine, twin)
        recv_ref[plane * 2 * LAYERS : (plane + 1) * 2 * LAYERS] = rows
    upper = recv_ref[pl.ds(0, TILES, stride=2), :].T
    stretch = []
    for group in range(GROUPS):
        row = BATCHES * MEMBERS + group
        total = jnp.sum(upper[row : row + 1], axis=1, keepdims=True)
        mean_var = total * (1.0 / ((MEMBERS - 1) * float(NX * NY)))
        stretch.append(jnp.sqrt(spread_ref[group // 2, group % 2] / (mean_var + spread_floor)))
    for group in range(GROUPS):
        value = forecast_ref[group]
        centre = jnp.sum(value, axis=0, keepdims=True) * (1.0 / MEMBERS)
        state_ref[:, group * CELLS : (group + 1) * CELLS] = centre + stretch[group] * (value - centre)

    kinds, xs, ys, values = [], [], [], []
    sub = lax.broadcasted_iota(I32, (CY, OBS), 0)
    table = jnp.zeros((CY, OBS), F32)
    near = []
    columns, spots = [], []
    for turn in range(BATCHES):
        batch = order_ref[turn]
        owner = owner_ref[pl.ds(batch, 1), :]
        cell = cell_ref[pl.ds(batch, 1), :]
        kinds.append(kind_ref[pl.ds(batch, 1), :])
        values.append(value_ref[pl.ds(batch, 1), :])
        mask = mask_ref[pl.ds(batch, 1), :].astype(F32)
        xs.append(((owner >> 3) * CX + (cell >> 7)).astype(F32))
        ys.append(((owner & (TILES_Y - 1)) * CY + (cell & (CY - 1))).astype(F32))
        tile_x = owner >> 3
        columns.append(tile_x + REACH)
        reach = REACH * (BATCHES - turn)
        near.append(flag(((tile_x - place_x + reach) & (TILES_X - 1)) <= 2 * reach))
        facts = (
            xs[turn],
            (owner & (TILES_Y - 1)).astype(F32),
            (cell & (CY - 1)).astype(F32),
            mask,
            tile_x.astype(F32),
        )
        for row, value in enumerate(facts):
            table = jnp.where(sub == turn * 8 + row, value, table)
        prior = upper[turn * MEMBERS : (turn + 1) * MEMBERS]
        centre = jnp.sum(prior, axis=0, keepdims=True) * (1.0 / MEMBERS)
        factor = jnp.where(kinds[turn] == 0, stretch[0], stretch[2])
        state_ref[:, AHEAD + turn * OBS : AHEAD + (turn + 1) * OBS] = centre + factor * (prior - centre)
        strip = ((tile_x >> 1) & 3) * 2 + ((owner >> 2) & 1)
        spots.append(strip * 8 + (tile_x & 1) * 4 + (owner & 3))
    for number, (turn, other) in enumerate(PAIRS):
        hot = jnp.where(sub == spots[other] + turn * HALF, 1.0, 0.0)
        spots_ref[:, number * OBS : (number + 1) * OBS] = hot.astype(BF16)
    sheet_ref[:, CY : 2 * CY] = table.T.astype(BF16)
    sheet_ref[:, 2 * CY : 3 * CY] = recv_ref[pl.ds(1, TILES, stride=2), :].astype(BF16)
    ahead = lax.broadcasted_iota(I32, (OBS, OBS), 0) <= lax.broadcasted_iota(I32, (OBS, OBS), 1)
    counts = jnp.concatenate([*near, jnp.zeros((8 - BATCHES, OBS), F32)], axis=0)
    counts = mm(counts.astype(BF16), jnp.where(ahead, 1.0, 0.0).astype(BF16))
    for turn in range(BATCHES):
        slot = jnp.where(near[turn] > 0.0, counts[turn : turn + 1] - 1.0, -1.0)
        order_of_ref[turn : turn + 1] = slot.astype(I32)

    lane = lax.broadcasted_iota(I32, (1, CY), 1)
    cell_x = (place_x * CX).astype(F32)
    cell_y = (place_y * CY + lane).astype(F32)

    for turn in range(BATCHES):
        prior = state_ref[:, AHEAD + turn * OBS : AHEAD + (turn + 1) * OBS]
        error = jnp.where(kinds[turn] == 0, error_ref[0], error_ref[1])
        centre = jnp.sum(prior, axis=0, keepdims=True) * (1.0 / MEMBERS)
        deviation = prior - centre
        variance = jnp.sum(deviation * deviation, axis=0, keepdims=True) / (MEMBERS - 1)
        gain = (values[turn] - centre) / (variance + error)
        shrink = -1.0 / (jnp.sqrt(error * (error + variance)) + error + variance)
        drive_high, drive_low = halves(gain + shrink * deviation)
        drive_ref[:MEMBERS] = drive_high
        drive_ref[MEMBERS:] = drive_low
        scaled = deviation * (1.0 / (MEMBERS - 1))
        scaled_high = scaled.astype(BF16).astype(F32)
        scaled_low = scaled - scaled_high
        packed = jnp.concatenate(
            [scaled_high, scaled_high, scaled_low, jnp.zeros_like(scaled)], axis=0
        )
        sheet_ref[:, :CY] = packed.T.astype(BF16)

        later = list(range(turn + 1, BATCHES))
        blocks = [slice(group * CELLS, (group + 1) * CELLS) for group in range(GROUPS)]
        blocks += [slice(AHEAD + other * OBS, AHEAD + (other + 1) * OBS) for other in later]
        for cols in blocks:
            state = state_ref[:, cols]
            state_dev = state - jnp.sum(state, axis=0, keepdims=True) * (1.0 / MEMBERS)
            high, low = halves(state_dev)
            pack_ref[0:32, cols] = high
            pack_ref[32:64, cols] = low
            pack_ref[64:96, cols] = high
            pack_ref[96:128, cols] = jnp.zeros_like(high)

        total = jnp.sum(near[turn])
        trips = jnp.int32(0)
        for start in range(0, OBS, GATHER):
            trips = trips + jnp.where(total > float(start), 1, 0)
        slot = order_of_ref[turn : turn + 1]

        @pl.loop(0, trips)
        def _(step):
            place = lax.broadcasted_iota(I32, (GATHER, OBS), 0) + step * GATHER
            hot = jnp.where(place == slot, 1.0, 0.0).astype(BF16)
            sheet = mm(hot, sheet_ref[...])
            left = sheet[:, :CY].astype(BF16)
            table = sheet[:, CY : 2 * CY]
            marks = sheet[:, 2 * CY :].astype(BF16)
            drive = lax.dot_general(
                drive_ref[...], hot, (((1,), (1,)), ((), ())), preferred_element_type=F32
            ).astype(BF16)
            x_col = table[:, turn * 8 : turn * 8 + 1]
            y_col = table[:, turn * 8 + 1 : turn * 8 + 2] * CY + table[:, turn * 8 + 2 : turn * 8 + 3]
            mask_col = table[:, turn * 8 + 3 : turn * 8 + 4]
            gap_y = y_col - cell_y
            drop_y = gap_y * gap_y * (1.0 / (LOC_Y * LOC_Y))
            for x in range(CX):
                gap_x = jnp.abs(x_col - (cell_x + x))
                gap_x = jnp.minimum(gap_x, NX - gap_x)
                room = jnp.maximum((1.0 - gap_x * gap_x * (1.0 / (LOC_X * LOC_X))) - drop_y, 0.0)
                weight_ref[:, x * CY : (x + 1) * CY] = room * room * mask_col
            if later:
                column = table[:, turn * 8 + 4 : turn * 8 + 5].astype(I32)
                for index, other in enumerate(later):
                    number = PAIRS.index((turn, other))
                    allowed = mm(marks, spots_ref[:, number * OBS : (number + 1) * OBS])
                    apart = (columns[other] - column) & (TILES_X - 1)
                    allowed = jnp.where(apart < SPAN, allowed, 0.0)
                    gap_x = jnp.abs(x_col - xs[other])
                    gap_x = jnp.minimum(gap_x, NX - gap_x)
                    gap_y = y_col - ys[other]
                    room = 1.0 - gap_x * gap_x * (1.0 / (LOC_X * LOC_X))
                    room = jnp.maximum(room - gap_y * gap_y * (1.0 / (LOC_Y * LOC_Y)), 0.0)
                    weight_ref[:, (index + 1) * OBS : (index + 2) * OBS] = room * room * allowed

            for number, cols in enumerate(blocks):
                at = max(0, number - GROUPS + 1) * OBS
                covariance = mm(left, pack_ref[:, cols]) * weight_ref[:, at : at + OBS]
                high, low = halves(covariance)
                both = mm(drive, high)
                rest = mm(drive[:MEMBERS], low)
                state_ref[:, cols] += both[:MEMBERS] + both[MEMBERS:] + rest

    for group in range(GROUPS):
        for x in range(CX):
            at = group * CELLS + x * CY
            out_ref[rows_of(group, x), :] = state_ref[:, at : at + CY]


def call(kernel, specs, outs, scratch=()):
    return pl.pallas_call(
        kernel,
        in_specs=specs,
        out_specs=[VMEM] * len(outs) if len(outs) > 1 else VMEM,
        out_shape=outs if len(outs) > 1 else outs[0],
        scratch_shapes=list(scratch),
        compiler_params=pltpu.CompilerParams(vmem_limit_bytes=48 * 1024 * 1024),
    )


def shape(*dims):
    return jax.ShapeDtypeStruct(dims, F32)


def swapped(value, axis, step, periodic):
    count = lax.axis_size(axis)
    pairs = []
    for source in range(count):
        target = source + (step if source % 2 == 0 else -step)
        if periodic or 0 <= target < count:
            pairs.append((source, target % count))
    return lax.ppermute(value, axis, pairs)


def local(
    ensemble,
    courant,
    target_spread,
    obs_error,
    obs_value,
    obs_owner,
    obs_cell,
    obs_kind,
    tile_mask,
    batch_order,
):
    place_x = lax.axis_index(GX)
    place_y = lax.axis_index(GY)
    relay = lax.axis_index(PLANE) * LAYERS + lax.axis_index(LAYER)
    place = jnp.stack([place_x, place_y, relay]).astype(I32)
    ens = ensemble.reshape(MEMBERS * GROUPS * CX, CY)
    mask = tile_mask.reshape(BATCHES, OBS)
    own, first, second, send = call(
        spread_kernel,
        [SMEM] * 3 + [VMEM] * 5,
        [
            shape(GROUPS, MEMBERS, CELLS),
            shape(SIDE, CY),
            shape(SIDE, CY),
            shape(PLANES * PLANE_ROWS, CY),
        ],
    )(batch_order, place, courant, ens, obs_owner, obs_cell, obs_kind, mask)
    recv = lax.all_to_all(send.reshape(PLANES, PLANE_ROWS, CY), PLANE, 0, 0)
    first = swapped(first, GX, 1, True)
    second = swapped(second, GX, -1, True)
    joined, send = call(
        collect_kernel,
        [SMEM] + [VMEM] * 4,
        [shape(GROUPS, MEMBERS, CELLS), shape(LAYERS * LAYER_ROWS, CY)],
    )(place, recv.reshape(PLANES * PLANE_ROWS, CY), own, first, second)
    recv = lax.all_to_all(send.reshape(LAYERS, LAYER_ROWS, CY), LAYER, 0, 0)
    recv = recv.reshape(LAYERS * LAYER_ROWS, CY)
    forecast, send = call(
        merge_kernel,
        [SMEM] * 3 + [VMEM] * 2,
        [shape(GROUPS, MEMBERS, CELLS), shape(2 * LAYERS, CY)],
    )(batch_order, place, obs_owner, joined, recv)
    recv = lax.all_to_all(send.reshape(LAYERS, 2, CY), LAYER, 0, 0)
    chips = PLANES // 2
    send = jnp.broadcast_to(recv.reshape(1, 2 * LAYERS, CY), (chips, 2 * LAYERS, CY))
    mine = lax.all_to_all(send, CHIP, 0, 0).reshape(TILES, CY)
    twin = lax.ppermute(mine, "core", [(0, 1), (1, 0)])
    out = call(
        assimilate_kernel,
        [SMEM] * 4 + [VMEM] * 8,
        [shape(MEMBERS * GROUPS * CX, CY)],
        [
            pltpu.VMEM((MEMBERS, AHEAD + BATCHES * OBS), F32),
            pltpu.VMEM((CY, AHEAD + BATCHES * OBS), BF16),
            pltpu.VMEM((OBS, 3 * CY), BF16),
            pltpu.VMEM((2 * MEMBERS, OBS), BF16),
            pltpu.VMEM((8, OBS), I32),
            pltpu.VMEM((CY, BATCHES * OBS), BF16),
            pltpu.VMEM((GATHER, BATCHES * OBS), F32),
            pltpu.VMEM((2 * TILES, CY), F32),
        ],
    )(
        batch_order,
        place,
        target_spread,
        obs_error,
        forecast,
        mine,
        twin,
        obs_owner,
        obs_cell,
        obs_kind,
        obs_value,
        mask,
    )
    return out.reshape(ensemble.shape)


def solution(mesh):
    fine = Mesh(mesh.devices.reshape(4, 8, 2, 2, 4), ("x", "z_lo", "core", "z_hi", "y"))
    in_specs = (
        P(None, None, None, GX, GY),
        P(),
        P(),
        P(),
        P(),
        P(),
        P(),
        P(),
        P(None, GX, GY, None),
        P(),
    )
    out_specs = P(None, None, None, GX, GY)
    return jax.shard_map(local, mesh=fine, in_specs=in_specs, out_specs=out_specs, check_vma=False)
```

```python
import jax
import jax.numpy as jnp
from jax import lax
from jax.experimental import pallas as pl
from jax.experimental.pallas import tpu as pltpu
from jax.sharding import Mesh
from jax.sharding import PartitionSpec as P

MEMBERS = 32
GROUPS = 4
CX = 4
CY = 128
CELLS = CX * CY
OBS = 512
BATCHES = 3
STEPS = 2
TILES_X = 64
TILES_Y = 8
TILES = TILES_X * TILES_Y
NX = TILES_X * CX
NY = TILES_Y * CY
LOC_X = 12.0
LOC_Y = 512.0
REACH = 2
SPAN = 2 * REACH + 1
PLANES = 32
LAYERS = 16
HALF = CY // 2
RIM = 16
VALUES = BATCHES * MEMBERS
PLANE_ROWS = LAYERS + RIM
LAYER_ROWS = RIM + 2
WIDE = (CX + 4) * CY
SIDE = 2 * GROUPS * MEMBERS
PAD = 128
GX = ("x", "z_lo", "core")
GY = ("z_hi", "y")
PLANE = ("x", "core", "y")
LAYER = ("z_lo", "z_hi")
CHIP = ("x", "y")
CHUNK = 256
GATHER = 128
AHEAD = GROUPS * CELLS
PAIRS = ((0, 1), (0, 2), (1, 2))

diffuse_rate = 0.1
mixing_rate = 0.05
spread_floor = 1e-05

F32 = jnp.float32
BF16 = jnp.bfloat16
I32 = jnp.int32

VMEM = pl.BlockSpec(memory_space=pltpu.VMEM)
SMEM = pl.BlockSpec(memory_space=pltpu.SMEM)


def rows_of(group, x):
    return pl.ds(group * CX + x, MEMBERS, stride=GROUPS * CX)


def mm(a, b):
    return lax.dot_general(a, b, (((1,), (0,)), ((), ())), preferred_element_type=F32)


def flag(condition):
    return jnp.where(condition, 1.0, 0.0).astype(F32)


def halves(value):
    high = value.astype(BF16)
    return high, (value - high.astype(F32)).astype(BF16)


def thirds(value):
    high = value.astype(BF16)
    rest = value - high.astype(F32)
    middle = rest.astype(BF16)
    return high, middle, (rest - middle.astype(F32)).astype(BF16)


def advance(rows, courant_ref, keep):
    lowest = min(x for _, x in rows) - 1
    highest = max(x for _, x in rows) + 1
    width = 2 * CY
    after = {}
    for group in range(GROUPS):
        speed = courant_ref[group % 2]
        stay = 1.0 - speed - 4.0 * diffuse_rate - mixing_rate
        for x in range(lowest, highest + 1):
            terms = []
            if (group, x) in rows:
                here = rows[group, x]
                beside = pltpu.roll(here, 1, 1) + pltpu.roll(here, width - 1, 1)
                terms.append(stay * here + diffuse_rate * beside + mixing_rate * rows[group ^ 1, x])
            if (group, x - 1) in rows:
                terms.append((speed + diffuse_rate) * rows[group, x - 1])
            if (group, x + 1) in rows:
                terms.append(diffuse_rate * rows[group, x + 1])
            total = terms[0]
            for term in terms[1:]:
                total = total + term
            after[group, x] = total if keep is None else total * keep
    return after


def spread_kernel(
    order_ref,
    place_ref,
    courant_ref,
    ens_ref,
    owner_ref,
    cell_ref,
    kind_ref,
    mask_ref,
    own_ref,
    first_ref,
    second_ref,
    send_ref,
):
    place_x = place_ref[0]
    place_y = place_ref[1]
    rows = {}
    for group in range(GROUPS):
        for x in range(CX):
            own = ens_ref[rows_of(group, x), :]
            rows[group, x] = jnp.concatenate([own, jnp.zeros_like(own)], axis=1)
    lane = lax.broadcasted_iota(I32, (1, 2 * CY), 1)
    below = (lane >= 3 * CY // 2) & (place_y == 0)
    above = (lane >= CY) & (lane < 3 * CY // 2) & (place_y == TILES_Y - 1)
    keep = jnp.where(below | above, 0.0, 1.0).astype(F32)
    rows = advance(rows, courant_ref, keep)
    rows = advance(rows, courant_ref, None)
    lane = lax.broadcasted_iota(I32, (MEMBERS, CY), 1)
    low = jnp.zeros((MEMBERS, CY), F32)
    high = jnp.zeros((MEMBERS, CY), F32)
    tile = {}
    for (group, x), value in rows.items():
        tile[group, x] = value[:, :CY]
        if 0 <= x < CX:
            own_ref[group, :, x * CY : (x + 1) * CY] = tile[group, x]
        edge = value[:, CY:]
        at = group * 16 + (x + 2) * 2
        there = (lane >> 1) == at // 2
        low = jnp.where(there, pltpu.roll(edge, at + 2, 1), low)
        high = jnp.where(there, pltpu.roll(edge, at, 1) if at else edge, high)
    rim = low + pltpu.roll(high, HALF, 1)
    first_ref[SIDE:] = jnp.zeros((PAD, CY), F32)
    second_ref[SIDE:] = jnp.zeros((PAD, CY), F32)
    even = (place_x & 1) == 0
    for group in range(GROUPS):
        for x in range(2):
            at = (group * 2 + x) * MEMBERS
            first_ref[at : at + MEMBERS] = jnp.where(even, tile[group, CX + x], tile[group, x - 2])
            second_ref[at : at + MEMBERS] = jnp.where(even, tile[group, x - 2], tile[group, CX + x])
    ground = jnp.concatenate(
        [
            jnp.concatenate([tile[2 * field, x] for x in range(-2, CX + 2)], axis=1)
            for field in range(2)
        ],
        axis=0,
    )
    parts = jnp.concatenate(thirds(ground), axis=0)
    rims = jnp.concatenate(thirds(rim), axis=0)
    blocks = []
    masks = []
    for turn in range(BATCHES):
        batch = order_ref[turn]
        owner = owner_ref[pl.ds(batch, 1), :]
        cell = cell_ref[pl.ds(batch, 1), :]
        kind = kind_ref[pl.ds(batch, 1), :]
        masks.append(mask_ref[pl.ds(batch, 1), :].astype(F32))
        at_x = ((owner >> 3) - place_x) * CX + (cell >> 7) + 2
        at_x = at_x & (NX - 1)
        at_y = ((owner & (TILES_Y - 1)) - place_y) * CY + (cell & (CY - 1))
        seen = at_x < CX + 4
        index = jnp.where(seen & (at_y >= 0) & (at_y < CY), at_x * CY + at_y, -1)
        corner = kind * 32 + at_x * 2
        edge = jnp.where(seen & (at_y >= -2) & (at_y < 0), corner + at_y + 2, -1)
        edge = jnp.where(seen & (at_y >= CY) & (at_y < CY + 2), corner + at_y - CY + HALF, edge)
        picked = jnp.zeros((parts.shape[0], OBS), F32)
        for start in range(0, WIDE, CHUNK):
            spot = lax.broadcasted_iota(I32, (CHUNK, OBS), 0) + start
            hot = jnp.where(spot == index, 1.0, 0.0).astype(BF16)
            picked = picked + mm(parts[:, start : start + CHUNK], hot)
        picked = picked[0:64] + picked[64:128] + picked[128:192]
        spot = lax.broadcasted_iota(I32, (CY, OBS), 0)
        found = mm(rims, jnp.where(spot == edge, 1.0, 0.0).astype(BF16))
        found = found[0:32] + found[32:64] + found[64:96]
        blocks.append(jnp.where(kind == 0, picked[0:32], picked[32:64]) + found)
    sub = lax.broadcasted_iota(I32, (MEMBERS, OBS), 0)
    blocks.append(jnp.where(sub == 0, masks[0], jnp.where(sub == 1, masks[1], 0.0)))
    turned = jnp.concatenate(blocks, axis=0).T
    lane = lax.broadcasted_iota(I32, (RIM, CY), 1)
    low = jnp.where(lane < HALF, low[:RIM], pltpu.roll(low[RIM:], HALF, 1))
    high = jnp.where(lane < HALF, high[:RIM], pltpu.roll(high[RIM:], HALF, 1))
    y = place_y & 3
    for plane in range(PLANES):
        at = plane * PLANE_ROWS
        send_ref[at : at + LAYERS, :] = turned[plane * LAYERS : (plane + 1) * LAYERS]
        up = flag((y + 1) & 3 == plane & 3)
        down = flag((y + 3) & 3 == plane & 3)
        send_ref[at + LAYERS : at + PLANE_ROWS, :] = up * high + down * low


def collect_kernel(place_ref, recv_ref, send_ref):
    place_x = place_ref[0]
    place_y = place_ref[1]
    x, z_lo, core = place_x >> 4, (place_x >> 1) & 7, place_x & 1
    z_hi, y = place_y >> 2, place_y & 3
    lane = lax.broadcasted_iota(I32, (LAYERS, CY), 1)
    total = jnp.zeros((LAYERS, CY), F32)
    marks = jnp.zeros((LAYERS, CY), F32)
    for plane in range(PLANES):
        rows = recv_ref[plane * PLANE_ROWS : plane * PLANE_ROWS + LAYERS, :]
        total = total + rows
        for turn in range(2):
            at = VALUES + turn
            marks = jnp.where(lane == turn * PLANES + plane, rows[:, at : at + 1], marks)

    spot = lane & 15
    hop = jnp.where(core == 0, z_lo == 7, z_lo == 0)
    side = jnp.where(hop, (x + jnp.where(core == 0, 3, 1)) & 3, x)
    first = flag(core == 0)
    second = 1.0 - first

    def rim(column, other, step):
        plane = (column * 2 + other) * 4 + ((y + step) & 3)
        start = pl.multiple_of(plane * PLANE_ROWS + LAYERS, RIM)
        return recv_ref[pl.ds(start, RIM), :]

    def from_left(block):
        return jnp.where((spot >= 4) & (spot < 8), pltpu.roll(block, CY - 8, 1), 0.0)

    def from_right(block):
        return jnp.where((spot >= 8) & (spot < 12), pltpu.roll(block, 8, 1), 0.0)

    here, there = [], []
    for step in (3, 1):
        mine = jnp.where((spot >= 4) & (spot < 12), rim(x, core, step), 0.0)
        twin = rim(x, 1 - core, step)
        far = rim(side, 1 - core, step)
        block = mine + first * from_right(twin) + second * from_left(twin)
        other = first * from_left(far) + second * from_right(far)
        here.append(pltpu.roll(block, 8, 1) if step == 1 else block)
        there.append(pltpu.roll(other, 8, 1) if step == 1 else other)
    target = jnp.where(core == 0, z_lo + 1, z_lo + 7) & 7
    below = jnp.where(y > 0, z_hi, jnp.where(z_hi == 0, 1, -1))
    above = jnp.where(y < 3, z_hi, jnp.where(z_hi == 1, 0, -1))
    for layer in range(LAYERS):
        lower, higher = flag(below == layer % 2), flag(above == layer % 2)
        same, next_to = flag(z_lo == layer // 2), flag(target == layer // 2)
        at = layer * LAYER_ROWS
        send_ref[at : at + RIM, :] = same * (lower * here[0] + higher * here[1]) + next_to * (
            lower * there[0] + higher * there[1]
        )
        pair = jnp.concatenate([total[layer : layer + 1], marks[layer : layer + 1]], axis=0)
        send_ref[at + RIM : at + RIM + 2, :] = pair


def merge_kernel(
    order_ref,
    place_ref,
    relay_ref,
    own_ref,
    near_ref,
    far_ref,
    recv_ref,
    forecast_ref,
    send_ref,
):
    relay = place_ref[2]
    lane = lax.broadcasted_iota(I32, (1, CY), 1)
    sums = recv_ref[pl.ds(RIM, LAYERS, stride=LAYER_ROWS), :]
    marks = recv_ref[pl.ds(RIM + 1, LAYERS, stride=LAYER_ROWS), :]
    top = jnp.sum(sums, axis=0, keepdims=True)
    top = jnp.where(lane < BATCHES * MEMBERS, top, 0.0)
    below = recv_ref[0:RIM, :]
    for layer in range(1, LAYERS):
        below = below + recv_ref[layer * LAYER_ROWS : layer * LAYER_ROWS + RIM, :]
    above = pltpu.roll(below, CY - 8, 1)
    below = jnp.concatenate([below, pltpu.roll(below, HALF, 1)], axis=0)
    above = jnp.concatenate([above, pltpu.roll(above, HALF, 1)], axis=0)
    even = (place_ref[0] & 1) == 0
    wide = lax.broadcasted_iota(I32, (MEMBERS, CY), 1)
    for group in range(GROUPS):
        pieces = []
        for x in range(CX):
            at = group * 16 + (x + 2) * 2
            part = (group * 2 + x % 2) * MEMBERS
            near, far = near_ref[part : part + MEMBERS], far_ref[part : part + MEMBERS]
            other = jnp.where(even, far, near) if x < 2 else jnp.where(even, near, far)
            piece = own_ref[group, :, x * CY : (x + 1) * CY] + other
            piece = piece + jnp.where(wide < 2, pltpu.roll(below, CY - at, 1), 0.0)
            piece = piece + jnp.where(wide >= CY - 2, pltpu.roll(above, CY - 2 - at, 1), 0.0)
            pieces.append(piece)
        value = jnp.concatenate(pieces, axis=1)
        forecast_ref[group] = value
        centre = jnp.sum(value, axis=0, keepdims=True) * (1.0 / MEMBERS)
        deviation = value - centre
        total = jnp.sum(jnp.sum(deviation * deviation, axis=0, keepdims=True), axis=1, keepdims=True)
        top = jnp.where(lane == BATCHES * MEMBERS + group, total, top)

    lanes = lax.broadcasted_iota(I32, (LAYERS, CY), 1)
    subs = lax.broadcasted_iota(I32, (LAYERS, CY), 0)
    tile_x = ((lanes >> 3) & 3) * 16 + (subs >> 1) * 2 + ((lanes >> 2) & 1)
    first = relay_ref[order_ref[0], relay] >> 3
    second = relay_ref[order_ref[1], relay] >> 3
    column = jnp.where(lanes < PLANES, first, second)
    near = ((tile_x - column + REACH) & (TILES_X - 1)) < SPAN
    marks = jnp.where(near & (lanes < 2 * PLANES), marks, 0.0)
    marks = marks[:8] + marks[8:]
    folded = marks
    for step in (8, 16, 24):
        folded = folded + pltpu.roll(marks, CY - step, 1)
    lanes = lax.broadcasted_iota(I32, (8, CY), 1)
    subs = lax.broadcasted_iota(I32, (8, CY), 0)
    bottom = jnp.zeros((8, CY), F32)
    for row in range(8):
        for turn in range(2):
            moved = pltpu.roll(folded, (turn * PLANES + row * 8) % CY, 1)
            there = (subs == row) & ((lanes >> 3) == turn * 8 + row)
            bottom = jnp.where(there, moved, bottom)
    bottom = jnp.sum(bottom, axis=0, keepdims=True)
    pair = jnp.concatenate([top, bottom] * 4, axis=0)
    send_ref[...] = jnp.concatenate([pair] * (2 * LAYERS // 8), axis=0)


def assimilate_kernel(
    order_ref,
    place_ref,
    spread_ref,
    error_ref,
    forecast_ref,
    mine_ref,
    twin_ref,
    owner_ref,
    cell_ref,
    kind_ref,
    value_ref,
    mask_ref,
    out_ref,
    state_ref,
    pack_ref,
    sheet_ref,
    drive_ref,
    order_of_ref,
    spots_ref,
    weight_ref,
    recv_ref,
):
    place_x = place_ref[0]
    place_y = place_ref[1]
    first = (place_x & 1) == 0
    for plane in range(PLANES):
        source = (plane // 8 * 4 + plane % 4) * 2 * LAYERS
        source = slice(source, source + 2 * LAYERS)
        mine, twin = mine_ref[source], twin_ref[source]
        rows = jnp.where(first, twin, mine) if plane // 4 % 2 else jnp.where(first, mine, twin)
        recv_ref[plane * 2 * LAYERS : (plane + 1) * 2 * LAYERS] = rows
    upper = recv_ref[pl.ds(0, TILES, stride=2), :].T
    stretch = []
    for group in range(GROUPS):
        row = BATCHES * MEMBERS + group
        total = jnp.sum(upper[row : row + 1], axis=1, keepdims=True)
        mean_var = total * (1.0 / ((MEMBERS - 1) * float(NX * NY)))
        stretch.append(jnp.sqrt(spread_ref[group // 2, group % 2] / (mean_var + spread_floor)))
    for group in range(GROUPS):
        value = forecast_ref[group]
        centre = jnp.sum(value, axis=0, keepdims=True) * (1.0 / MEMBERS)
        state_ref[:, group * CELLS : (group + 1) * CELLS] = centre + stretch[group] * (value - centre)

    kinds, xs, ys, values = [], [], [], []
    sub = lax.broadcasted_iota(I32, (CY, OBS), 0)
    table = jnp.zeros((CY, OBS), F32)
    near = []
    columns, spots = [], []
    for turn in range(BATCHES):
        batch = order_ref[turn]
        owner = owner_ref[pl.ds(batch, 1), :]
        cell = cell_ref[pl.ds(batch, 1), :]
        kinds.append(kind_ref[pl.ds(batch, 1), :])
        values.append(value_ref[pl.ds(batch, 1), :])
        mask = mask_ref[pl.ds(batch, 1), :].astype(F32)
        xs.append(((owner >> 3) * CX + (cell >> 7)).astype(F32))
        ys.append(((owner & (TILES_Y - 1)) * CY + (cell & (CY - 1))).astype(F32))
        tile_x = owner >> 3
        columns.append(tile_x + REACH)
        reach = REACH * (BATCHES - turn)
        near.append(flag(((tile_x - place_x + reach) & (TILES_X - 1)) <= 2 * reach))
        facts = (
            xs[turn],
            (owner & (TILES_Y - 1)).astype(F32),
            (cell & (CY - 1)).astype(F32),
            mask,
            tile_x.astype(F32),
        )
        for row, value in enumerate(facts):
            table = jnp.where(sub == turn * 8 + row, value, table)
        prior = upper[turn * MEMBERS : (turn + 1) * MEMBERS]
        centre = jnp.sum(prior, axis=0, keepdims=True) * (1.0 / MEMBERS)
        factor = jnp.where(kinds[turn] == 0, stretch[0], stretch[2])
        state_ref[:, AHEAD + turn * OBS : AHEAD + (turn + 1) * OBS] = centre + factor * (prior - centre)
        strip = ((tile_x >> 1) & 3) * 2 + ((owner >> 2) & 1)
        spots.append(strip * 8 + (tile_x & 1) * 4 + (owner & 3))
    for number, (turn, other) in enumerate(PAIRS):
        hot = jnp.where(sub == spots[other] + turn * HALF, 1.0, 0.0)
        spots_ref[:, number * OBS : (number + 1) * OBS] = hot.astype(BF16)
    sheet_ref[:, CY : 2 * CY] = table.T.astype(BF16)
    sheet_ref[:, 2 * CY : 3 * CY] = recv_ref[pl.ds(1, TILES, stride=2), :].astype(BF16)
    ahead = lax.broadcasted_iota(I32, (OBS, OBS), 0) <= lax.broadcasted_iota(I32, (OBS, OBS), 1)
    counts = jnp.concatenate([*near, jnp.zeros((8 - BATCHES, OBS), F32)], axis=0)
    counts = mm(counts.astype(BF16), jnp.where(ahead, 1.0, 0.0).astype(BF16))
    for turn in range(BATCHES):
        slot = jnp.where(near[turn] > 0.0, counts[turn : turn + 1] - 1.0, -1.0)
        order_of_ref[turn : turn + 1] = slot.astype(I32)

    lane = lax.broadcasted_iota(I32, (1, CY), 1)
    cell_x = (place_x * CX).astype(F32)
    cell_y = (place_y * CY + lane).astype(F32)

    for turn in range(BATCHES):
        prior = state_ref[:, AHEAD + turn * OBS : AHEAD + (turn + 1) * OBS]
        error = jnp.where(kinds[turn] == 0, error_ref[0], error_ref[1])
        centre = jnp.sum(prior, axis=0, keepdims=True) * (1.0 / MEMBERS)
        deviation = prior - centre
        variance = jnp.sum(deviation * deviation, axis=0, keepdims=True) / (MEMBERS - 1)
        gain = (values[turn] - centre) / (variance + error)
        shrink = -1.0 / (jnp.sqrt(error * (error + variance)) + error + variance)
        drive_high, drive_low = halves(gain + shrink * deviation)
        drive_ref[:MEMBERS] = drive_high
        drive_ref[MEMBERS:] = drive_low
        scaled = deviation * (1.0 / (MEMBERS - 1))
        scaled_high = scaled.astype(BF16).astype(F32)
        scaled_low = scaled - scaled_high
        packed = jnp.concatenate(
            [scaled_high, scaled_high, scaled_low, jnp.zeros_like(scaled)], axis=0
        )
        sheet_ref[:, :CY] = packed.T.astype(BF16)

        later = list(range(turn + 1, BATCHES))
        blocks = [slice(group * CELLS, (group + 1) * CELLS) for group in range(GROUPS)]
        blocks += [slice(AHEAD + other * OBS, AHEAD + (other + 1) * OBS) for other in later]
        for cols in blocks:
            state = state_ref[:, cols]
            state_dev = state - jnp.sum(state, axis=0, keepdims=True) * (1.0 / MEMBERS)
            high, low = halves(state_dev)
            pack_ref[0:32, cols] = high
            pack_ref[32:64, cols] = low
            pack_ref[64:96, cols] = high
            pack_ref[96:128, cols] = jnp.zeros_like(high)

        total = jnp.sum(near[turn])
        trips = jnp.int32(0)
        for start in range(0, OBS, GATHER):
            trips = trips + jnp.where(total > float(start), 1, 0)
        slot = order_of_ref[turn : turn + 1]

        @pl.loop(0, trips)
        def _(step):
            place = lax.broadcasted_iota(I32, (GATHER, OBS), 0) + step * GATHER
            hot = jnp.where(place == slot, 1.0, 0.0).astype(BF16)
            sheet = mm(hot, sheet_ref[...])
            left = sheet[:, :CY].astype(BF16)
            table = sheet[:, CY : 2 * CY]
            marks = sheet[:, 2 * CY :].astype(BF16)
            drive = lax.dot_general(
                drive_ref[...], hot, (((1,), (1,)), ((), ())), preferred_element_type=F32
            ).astype(BF16)
            x_col = table[:, turn * 8 : turn * 8 + 1]
            y_col = table[:, turn * 8 + 1 : turn * 8 + 2] * CY + table[:, turn * 8 + 2 : turn * 8 + 3]
            mask_col = table[:, turn * 8 + 3 : turn * 8 + 4]
            gap_y = y_col - cell_y
            drop_y = gap_y * gap_y * (1.0 / (LOC_Y * LOC_Y))
            for x in range(CX):
                gap_x = jnp.abs(x_col - (cell_x + x))
                gap_x = jnp.minimum(gap_x, NX - gap_x)
                room = jnp.maximum((1.0 - gap_x * gap_x * (1.0 / (LOC_X * LOC_X))) - drop_y, 0.0)
                weight_ref[:, x * CY : (x + 1) * CY] = room * room * mask_col
            if later:
                column = table[:, turn * 8 + 4 : turn * 8 + 5].astype(I32)
                for index, other in enumerate(later):
                    number = PAIRS.index((turn, other))
                    allowed = mm(marks, spots_ref[:, number * OBS : (number + 1) * OBS])
                    apart = (columns[other] - column) & (TILES_X - 1)
                    allowed = jnp.where(apart < SPAN, allowed, 0.0)
                    gap_x = jnp.abs(x_col - xs[other])
                    gap_x = jnp.minimum(gap_x, NX - gap_x)
                    gap_y = y_col - ys[other]
                    room = 1.0 - gap_x * gap_x * (1.0 / (LOC_X * LOC_X))
                    room = jnp.maximum(room - gap_y * gap_y * (1.0 / (LOC_Y * LOC_Y)), 0.0)
                    weight_ref[:, (index + 1) * OBS : (index + 2) * OBS] = room * room * allowed

            for number, cols in enumerate(blocks):
                at = max(0, number - GROUPS + 1) * OBS
                covariance = mm(left, pack_ref[:, cols]) * weight_ref[:, at : at + OBS]
                high, low = halves(covariance)
                both = mm(drive, high)
                rest = mm(drive[:MEMBERS], low)
                state_ref[:, cols] += both[:MEMBERS] + both[MEMBERS:] + rest

    for group in range(GROUPS):
        for x in range(CX):
            at = group * CELLS + x * CY
            out_ref[rows_of(group, x), :] = state_ref[:, at : at + CY]


def call(kernel, specs, outs, scratch=()):
    return pl.pallas_call(
        kernel,
        in_specs=specs,
        out_specs=[VMEM] * len(outs) if len(outs) > 1 else VMEM,
        out_shape=outs if len(outs) > 1 else outs[0],
        scratch_shapes=list(scratch),
        compiler_params=pltpu.CompilerParams(vmem_limit_bytes=48 * 1024 * 1024),
    )


def shape(*dims):
    return jax.ShapeDtypeStruct(dims, F32)


def swapped(value, axis, step, periodic):
    count = lax.axis_size(axis)
    pairs = []
    for source in range(count):
        target = source + (step if source % 2 == 0 else -step)
        if periodic or 0 <= target < count:
            pairs.append((source, target % count))
    return lax.ppermute(value, axis, pairs)


def local(
    ensemble,
    courant,
    target_spread,
    obs_error,
    obs_value,
    obs_owner,
    obs_cell,
    obs_kind,
    tile_mask,
    batch_order,
):
    place_x = lax.axis_index(GX)
    place_y = lax.axis_index(GY)
    relay = lax.axis_index(PLANE) * LAYERS + lax.axis_index(LAYER)
    place = jnp.stack([place_x, place_y, relay]).astype(I32)
    ens = ensemble.reshape(MEMBERS * GROUPS * CX, CY)
    mask = tile_mask.reshape(BATCHES, OBS)
    own, first, second, send = call(
        spread_kernel,
        [SMEM] * 3 + [VMEM] * 5,
        [
            shape(GROUPS, MEMBERS, CELLS),
            shape(SIDE + PAD, CY),
            shape(SIDE + PAD, CY),
            shape(PLANES * PLANE_ROWS, CY),
        ],
    )(batch_order, place, courant, ens, obs_owner, obs_cell, obs_kind, mask)
    recv = lax.all_to_all(send.reshape(PLANES, PLANE_ROWS, CY), PLANE, 0, 0)
    first = swapped(first, GX, 1, True)
    second = swapped(second, GX, -1, True)
    send = call(collect_kernel, [SMEM, VMEM], [shape(LAYERS * LAYER_ROWS, CY)])(
        place, recv.reshape(PLANES * PLANE_ROWS, CY)
    )
    recv = lax.all_to_all(send.reshape(LAYERS, LAYER_ROWS // 2, 2, CY), LAYER, 0, 0)
    recv = recv.reshape(LAYERS * LAYER_ROWS, CY)
    forecast, send = call(
        merge_kernel,
        [SMEM] * 3 + [VMEM] * 4,
        [shape(GROUPS, MEMBERS, CELLS), shape(2 * LAYERS, CY)],
    )(batch_order, place, obs_owner, own, first, second, recv)
    recv = lax.all_to_all(send.reshape(LAYERS, 2, CY), LAYER, 0, 0)
    chips = PLANES // 2
    send = jnp.broadcast_to(recv.reshape(1, 2 * LAYERS, CY), (chips, 2 * LAYERS, CY))
    mine = lax.all_to_all(send, CHIP, 0, 0).reshape(TILES, CY)
    twin = lax.ppermute(mine, "core", [(0, 1), (1, 0)])
    out = call(
        assimilate_kernel,
        [SMEM] * 4 + [VMEM] * 8,
        [shape(MEMBERS * GROUPS * CX, CY)],
        [
            pltpu.VMEM((MEMBERS, AHEAD + BATCHES * OBS), F32),
            pltpu.VMEM((CY, AHEAD + BATCHES * OBS), BF16),
            pltpu.VMEM((OBS, 3 * CY), BF16),
            pltpu.VMEM((2 * MEMBERS, OBS), BF16),
            pltpu.VMEM((8, OBS), I32),
            pltpu.VMEM((CY, BATCHES * OBS), BF16),
            pltpu.VMEM((GATHER, BATCHES * OBS), F32),
            pltpu.VMEM((2 * TILES, CY), F32),
        ],
    )(
        batch_order,
        place,
        target_spread,
        obs_error,
        forecast,
        mine,
        twin,
        obs_owner,
        obs_cell,
        obs_kind,
        obs_value,
        mask,
    )
    return out.reshape(ensemble.shape)


def solution(mesh):
    fine = Mesh(mesh.devices.reshape(4, 8, 2, 2, 4), ("x", "z_lo", "core", "z_hi", "y"))
    in_specs = (
        P(None, None, None, GX, GY),
        P(),
        P(),
        P(),
        P(),
        P(),
        P(),
        P(),
        P(None, GX, GY, None),
        P(),
    )
    out_specs = P(None, None, None, GX, GY)
    return jax.shard_map(local, mesh=fine, in_specs=in_specs, out_specs=out_specs, check_vma=False)
```

```python
import jax
import jax.numpy as jnp
from jax import lax
from jax.experimental import pallas as pl
from jax.experimental.pallas import tpu as pltpu
from jax.sharding import Mesh
from jax.sharding import PartitionSpec as P

MEMBERS = 32
GROUPS = 4
CX = 4
CY = 128
CELLS = CX * CY
OBS = 512
BATCHES = 3
STEPS = 2
TILES_X = 64
TILES_Y = 8
TILES = TILES_X * TILES_Y
NX = TILES_X * CX
NY = TILES_Y * CY
LOC_X = 12.0
LOC_Y = 512.0
REACH = 2
SPAN = 2 * REACH + 1
PLANES = 32
LAYERS = 16
HALF = CY // 2
RIM = 16
VALUES = BATCHES * MEMBERS
PLANE_ROWS = LAYERS + RIM
LAYER_ROWS = RIM + 2
WIDE = (CX + 4) * CY
SIDE = 2 * GROUPS * MEMBERS
GX = ("x", "z_lo", "core")
GY = ("z_hi", "y")
PLANE = ("x", "core", "y")
LAYER = ("z_lo", "z_hi")
CHIP = ("x", "y")
CHUNK = 256
GATHER = 128
AHEAD = GROUPS * CELLS
PAIRS = ((0, 1), (0, 2), (1, 2))

diffuse_rate = 0.1
mixing_rate = 0.05
spread_floor = 1e-05

F32 = jnp.float32
BF16 = jnp.bfloat16
I32 = jnp.int32

VMEM = pl.BlockSpec(memory_space=pltpu.VMEM)
SMEM = pl.BlockSpec(memory_space=pltpu.SMEM)


def rows_of(group, x):
    return pl.ds(group * CX + x, MEMBERS, stride=GROUPS * CX)


def mm(a, b):
    return lax.dot_general(a, b, (((1,), (0,)), ((), ())), preferred_element_type=F32)


def flag(condition):
    return jnp.where(condition, 1.0, 0.0).astype(F32)


def halves(value):
    high = value.astype(BF16)
    return high, (value - high.astype(F32)).astype(BF16)


def thirds(value):
    high = value.astype(BF16)
    rest = value - high.astype(F32)
    middle = rest.astype(BF16)
    return high, middle, (rest - middle.astype(F32)).astype(BF16)


def advance(rows, courant_ref, keep):
    lowest = min(x for _, x in rows) - 1
    highest = max(x for _, x in rows) + 1
    width = 2 * CY
    after = {}
    for group in range(GROUPS):
        speed = courant_ref[group % 2]
        stay = 1.0 - speed - 4.0 * diffuse_rate - mixing_rate
        for x in range(lowest, highest + 1):
            terms = []
            if (group, x) in rows:
                here = rows[group, x]
                beside = pltpu.roll(here, 1, 1) + pltpu.roll(here, width - 1, 1)
                terms.append(stay * here + diffuse_rate * beside + mixing_rate * rows[group ^ 1, x])
            if (group, x - 1) in rows:
                terms.append((speed + diffuse_rate) * rows[group, x - 1])
            if (group, x + 1) in rows:
                terms.append(diffuse_rate * rows[group, x + 1])
            total = terms[0]
            for term in terms[1:]:
                total = total + term
            after[group, x] = total if keep is None else total * keep
    return after


def spread_kernel(
    order_ref,
    place_ref,
    courant_ref,
    ens_ref,
    owner_ref,
    cell_ref,
    kind_ref,
    mask_ref,
    own_ref,
    first_ref,
    second_ref,
    send_ref,
):
    place_x = place_ref[0]
    place_y = place_ref[1]
    rows = {}
    for group in range(GROUPS):
        for x in range(CX):
            own = ens_ref[rows_of(group, x), :]
            rows[group, x] = jnp.concatenate([own, jnp.zeros_like(own)], axis=1)
    lane = lax.broadcasted_iota(I32, (1, 2 * CY), 1)
    below = (lane >= 3 * CY // 2) & (place_y == 0)
    above = (lane >= CY) & (lane < 3 * CY // 2) & (place_y == TILES_Y - 1)
    keep = jnp.where(below | above, 0.0, 1.0).astype(F32)
    rows = advance(rows, courant_ref, keep)
    rows = advance(rows, courant_ref, None)
    lane = lax.broadcasted_iota(I32, (MEMBERS, CY), 1)
    low = jnp.zeros((MEMBERS, CY), F32)
    high = jnp.zeros((MEMBERS, CY), F32)
    tile = {}
    for (group, x), value in rows.items():
        tile[group, x] = value[:, :CY]
        if 0 <= x < CX:
            own_ref[group, :, x * CY : (x + 1) * CY] = tile[group, x]
        edge = value[:, CY:]
        at = group * 16 + (x + 2) * 2
        there = (lane >> 1) == at // 2
        low = jnp.where(there, pltpu.roll(edge, at + 2, 1), low)
        high = jnp.where(there, pltpu.roll(edge, at, 1) if at else edge, high)
    rim = low + pltpu.roll(high, HALF, 1)
    even = (place_x & 1) == 0
    for group in range(GROUPS):
        for x in range(2):
            at = (group * 2 + x) * MEMBERS
            first_ref[at : at + MEMBERS] = jnp.where(even, tile[group, CX + x], tile[group, x - 2])
            second_ref[at : at + MEMBERS] = jnp.where(even, tile[group, x - 2], tile[group, CX + x])
    ground = jnp.concatenate(
        [
            jnp.concatenate([tile[2 * field, x] for x in range(-2, CX + 2)], axis=1)
            for field in range(2)
        ],
        axis=0,
    )
    parts = jnp.concatenate(thirds(ground), axis=0)
    rims = jnp.concatenate(thirds(rim), axis=0)
    blocks = []
    masks = []
    for turn in range(BATCHES):
        batch = order_ref[turn]
        owner = owner_ref[pl.ds(batch, 1), :]
        cell = cell_ref[pl.ds(batch, 1), :]
        kind = kind_ref[pl.ds(batch, 1), :]
        masks.append(mask_ref[batch].astype(F32))
        at_x = ((owner >> 3) - place_x) * CX + (cell >> 7) + 2
        at_x = at_x & (NX - 1)
        at_y = ((owner & (TILES_Y - 1)) - place_y) * CY + (cell & (CY - 1))
        seen = at_x < CX + 4
        index = jnp.where(seen & (at_y >= 0) & (at_y < CY), at_x * CY + at_y, -1)
        corner = kind * 32 + at_x * 2
        edge = jnp.where(seen & (at_y >= -2) & (at_y < 0), corner + at_y + 2, -1)
        edge = jnp.where(seen & (at_y >= CY) & (at_y < CY + 2), corner + at_y - CY + HALF, edge)
        picked = jnp.zeros((parts.shape[0], OBS), F32)
        for start in range(0, WIDE, CHUNK):
            spot = lax.broadcasted_iota(I32, (CHUNK, OBS), 0) + start
            hot = jnp.where(spot == index, 1.0, 0.0).astype(BF16)
            picked = picked + mm(parts[:, start : start + CHUNK], hot)
        picked = picked[0:64] + picked[64:128] + picked[128:192]
        spot = lax.broadcasted_iota(I32, (CY, OBS), 0)
        found = mm(rims, jnp.where(spot == edge, 1.0, 0.0).astype(BF16))
        found = found[0:32] + found[32:64] + found[64:96]
        blocks.append(jnp.where(kind == 0, picked[0:32], picked[32:64]) + found)
    sub = lax.broadcasted_iota(I32, (MEMBERS, OBS), 0)
    blocks.append(jnp.where(sub == 0, masks[0], jnp.where(sub == 1, masks[1], 0.0)))
    turned = jnp.concatenate(blocks, axis=0).T
    lane = lax.broadcasted_iota(I32, (RIM, CY), 1)
    low = jnp.where(lane < HALF, low[:RIM], pltpu.roll(low[RIM:], HALF, 1))
    high = jnp.where(lane < HALF, high[:RIM], pltpu.roll(high[RIM:], HALF, 1))
    y = place_y & 3
    for plane in range(PLANES):
        at = plane * PLANE_ROWS
        send_ref[at : at + LAYERS, :] = turned[plane * LAYERS : (plane + 1) * LAYERS]
        up = flag((y + 1) & 3 == plane & 3)
        down = flag((y + 3) & 3 == plane & 3)
        send_ref[at + LAYERS : at + PLANE_ROWS, :] = up * high + down * low


def collect_kernel(place_ref, recv_ref, own_ref, near_ref, far_ref, joined_ref, send_ref):
    even = (place_ref[0] & 1) == 0
    for group in range(GROUPS):
        for column in range(CX):
            at = (group * 2 + column % 2) * MEMBERS
            part = slice(at, at + MEMBERS)
            near, far = near_ref[part], far_ref[part]
            other = jnp.where(even, far, near) if column < 2 else jnp.where(even, near, far)
            cells = slice(column * CY, (column + 1) * CY)
            joined_ref[group, :, cells] = own_ref[group, :, cells] + other
    place_x = place_ref[0]
    place_y = place_ref[1]
    x, z_lo, core = place_x >> 4, (place_x >> 1) & 7, place_x & 1
    z_hi, y = place_y >> 2, place_y & 3
    lane = lax.broadcasted_iota(I32, (LAYERS, CY), 1)
    total = jnp.zeros((LAYERS, CY), F32)
    marks = jnp.zeros((LAYERS, CY), F32)
    for plane in range(PLANES):
        rows = recv_ref[plane * PLANE_ROWS : plane * PLANE_ROWS + LAYERS, :]
        total = total + rows
        for turn in range(2):
            at = VALUES + turn
            marks = jnp.where(lane == turn * PLANES + plane, rows[:, at : at + 1], marks)

    spot = lane & 15
    hop = jnp.where(core == 0, z_lo == 7, z_lo == 0)
    side = jnp.where(hop, (x + jnp.where(core == 0, 3, 1)) & 3, x)
    first = flag(core == 0)
    second = 1.0 - first

    def rim(column, other, step):
        plane = (column * 2 + other) * 4 + ((y + step) & 3)
        start = pl.multiple_of(plane * PLANE_ROWS + LAYERS, RIM)
        return recv_ref[pl.ds(start, RIM), :]

    def from_left(block):
        return jnp.where((spot >= 4) & (spot < 8), pltpu.roll(block, CY - 8, 1), 0.0)

    def from_right(block):
        return jnp.where((spot >= 8) & (spot < 12), pltpu.roll(block, 8, 1), 0.0)

    here, there = [], []
    for step in (3, 1):
        mine = jnp.where((spot >= 4) & (spot < 12), rim(x, core, step), 0.0)
        twin = rim(x, 1 - core, step)
        far = rim(side, 1 - core, step)
        block = mine + first * from_right(twin) + second * from_left(twin)
        other = first * from_left(far) + second * from_right(far)
        here.append(pltpu.roll(block, 8, 1) if step == 1 else block)
        there.append(pltpu.roll(other, 8, 1) if step == 1 else other)
    target = jnp.where(core == 0, z_lo + 1, z_lo + 7) & 7
    below = jnp.where(y > 0, z_hi, jnp.where(z_hi == 0, 1, -1))
    above = jnp.where(y < 3, z_hi, jnp.where(z_hi == 1, 0, -1))
    for layer in range(LAYERS):
        lower, higher = flag(below == layer % 2), flag(above == layer % 2)
        same, next_to = flag(z_lo == layer // 2), flag(target == layer // 2)
        at = layer * LAYER_ROWS
        send_ref[at : at + RIM, :] = same * (lower * here[0] + higher * here[1]) + next_to * (
            lower * there[0] + higher * there[1]
        )
        pair = jnp.concatenate([total[layer : layer + 1], marks[layer : layer + 1]], axis=0)
        send_ref[at + RIM : at + RIM + 2, :] = pair


def merge_kernel(
    order_ref,
    place_ref,
    relay_ref,
    joined_ref,
    recv_ref,
    forecast_ref,
    send_ref,
):
    relay = place_ref[2]
    lane = lax.broadcasted_iota(I32, (1, CY), 1)
    sums = recv_ref[pl.ds(RIM, LAYERS, stride=LAYER_ROWS), :]
    marks = recv_ref[pl.ds(RIM + 1, LAYERS, stride=LAYER_ROWS), :]
    top = jnp.sum(sums, axis=0, keepdims=True)
    top = jnp.where(lane < BATCHES * MEMBERS, top, 0.0)
    below = recv_ref[0:RIM, :]
    for layer in range(1, LAYERS):
        below = below + recv_ref[layer * LAYER_ROWS : layer * LAYER_ROWS + RIM, :]
    above = pltpu.roll(below, CY - 8, 1)
    below = jnp.concatenate([below, pltpu.roll(below, HALF, 1)], axis=0)
    above = jnp.concatenate([above, pltpu.roll(above, HALF, 1)], axis=0)
    wide = lax.broadcasted_iota(I32, (MEMBERS, CY), 1)
    for group in range(GROUPS):
        pieces = []
        for x in range(CX):
            at = group * 16 + (x + 2) * 2
            piece = joined_ref[group, :, x * CY : (x + 1) * CY]
            piece = piece + jnp.where(wide < 2, pltpu.roll(below, CY - at, 1), 0.0)
            piece = piece + jnp.where(wide >= CY - 2, pltpu.roll(above, CY - 2 - at, 1), 0.0)
            pieces.append(piece)
        value = jnp.concatenate(pieces, axis=1)
        forecast_ref[group] = value
        centre = jnp.sum(value, axis=0, keepdims=True) * (1.0 / MEMBERS)
        deviation = value - centre
        total = jnp.sum(jnp.sum(deviation * deviation, axis=0, keepdims=True), axis=1, keepdims=True)
        top = jnp.where(lane == BATCHES * MEMBERS + group, total, top)

    lanes = lax.broadcasted_iota(I32, (LAYERS, CY), 1)
    subs = lax.broadcasted_iota(I32, (LAYERS, CY), 0)
    tile_x = ((lanes >> 3) & 3) * 16 + (subs >> 1) * 2 + ((lanes >> 2) & 1)
    first = relay_ref[order_ref[0], relay] >> 3
    second = relay_ref[order_ref[1], relay] >> 3
    column = jnp.where(lanes < PLANES, first, second)
    near = ((tile_x - column + REACH) & (TILES_X - 1)) < SPAN
    marks = jnp.where(near & (lanes < 2 * PLANES), marks, 0.0)
    marks = marks[:8] + marks[8:]
    folded = marks
    for step in (8, 16, 24):
        folded = folded + pltpu.roll(marks, CY - step, 1)
    lanes = lax.broadcasted_iota(I32, (8, CY), 1)
    subs = lax.broadcasted_iota(I32, (8, CY), 0)
    bottom = jnp.zeros((8, CY), F32)
    for row in range(8):
        for turn in range(2):
            moved = pltpu.roll(folded, (turn * PLANES + row * 8) % CY, 1)
            there = (subs == row) & ((lanes >> 3) == turn * 8 + row)
            bottom = jnp.where(there, moved, bottom)
    bottom = jnp.sum(bottom, axis=0, keepdims=True)
    pair = jnp.concatenate([top, bottom] * 4, axis=0)
    send_ref[...] = jnp.concatenate([pair] * (2 * LAYERS // 8), axis=0)


def assimilate_kernel(
    order_ref,
    place_ref,
    spread_ref,
    error_ref,
    forecast_ref,
    mine_ref,
    twin_ref,
    owner_ref,
    cell_ref,
    kind_ref,
    value_ref,
    mask_ref,
    out_ref,
    state_ref,
    pack_ref,
    sheet_ref,
    drive_ref,
    order_of_ref,
    spots_ref,
    weight_ref,
    recv_ref,
):
    place_x = place_ref[0]
    place_y = place_ref[1]
    first = (place_x & 1) == 0
    for plane in range(PLANES):
        source = (plane // 8 * 4 + plane % 4) * 2 * LAYERS
        source = slice(source, source + 2 * LAYERS)
        mine, twin = mine_ref[source], twin_ref[source]
        rows = jnp.where(first, twin, mine) if plane // 4 % 2 else jnp.where(first, mine, twin)
        recv_ref[plane * 2 * LAYERS : (plane + 1) * 2 * LAYERS] = rows
    upper = recv_ref[pl.ds(0, TILES, stride=2), :].T
    stretch = []
    for group in range(GROUPS):
        row = BATCHES * MEMBERS + group
        total = jnp.sum(upper[row : row + 1], axis=1, keepdims=True)
        mean_var = total * (1.0 / ((MEMBERS - 1) * float(NX * NY)))
        stretch.append(jnp.sqrt(spread_ref[group // 2, group % 2] / (mean_var + spread_floor)))
    for group in range(GROUPS):
        value = forecast_ref[group]
        centre = jnp.sum(value, axis=0, keepdims=True) * (1.0 / MEMBERS)
        state_ref[:, group * CELLS : (group + 1) * CELLS] = centre + stretch[group] * (value - centre)

    kinds, xs, ys, values = [], [], [], []
    sub = lax.broadcasted_iota(I32, (CY, OBS), 0)
    table = jnp.zeros((CY, OBS), F32)
    near = []
    columns, spots = [], []
    for turn in range(BATCHES):
        batch = order_ref[turn]
        owner = owner_ref[pl.ds(batch, 1), :]
        cell = cell_ref[pl.ds(batch, 1), :]
        kinds.append(kind_ref[pl.ds(batch, 1), :])
        values.append(value_ref[pl.ds(batch, 1), :])
        mask = mask_ref[batch].astype(F32)
        xs.append(((owner >> 3) * CX + (cell >> 7)).astype(F32))
        ys.append(((owner & (TILES_Y - 1)) * CY + (cell & (CY - 1))).astype(F32))
        tile_x = owner >> 3
        columns.append(tile_x + REACH)
        reach = REACH * (BATCHES - turn)
        near.append(flag(((tile_x - place_x + reach) & (TILES_X - 1)) <= 2 * reach))
        facts = (
            xs[turn],
            (owner & (TILES_Y - 1)).astype(F32),
            (cell & (CY - 1)).astype(F32),
            mask,
            tile_x.astype(F32),
        )
        for row, value in enumerate(facts):
            table = jnp.where(sub == turn * 8 + row, value, table)
        prior = upper[turn * MEMBERS : (turn + 1) * MEMBERS]
        centre = jnp.sum(prior, axis=0, keepdims=True) * (1.0 / MEMBERS)
        factor = jnp.where(kinds[turn] == 0, stretch[0], stretch[2])
        state_ref[:, AHEAD + turn * OBS : AHEAD + (turn + 1) * OBS] = centre + factor * (prior - centre)
        strip = ((tile_x >> 1) & 3) * 2 + ((owner >> 2) & 1)
        spots.append(strip * 8 + (tile_x & 1) * 4 + (owner & 3))
    for number, (turn, other) in enumerate(PAIRS):
        hot = jnp.where(sub == spots[other] + turn * HALF, 1.0, 0.0)
        spots_ref[:, number * OBS : (number + 1) * OBS] = hot.astype(BF16)
    sheet_ref[:, CY : 2 * CY] = table.T.astype(BF16)
    sheet_ref[:, 2 * CY : 3 * CY] = recv_ref[pl.ds(1, TILES, stride=2), :].astype(BF16)
    ahead = lax.broadcasted_iota(I32, (OBS, OBS), 0) <= lax.broadcasted_iota(I32, (OBS, OBS), 1)
    counts = jnp.concatenate([*near, jnp.zeros((8 - BATCHES, OBS), F32)], axis=0)
    counts = mm(counts.astype(BF16), jnp.where(ahead, 1.0, 0.0).astype(BF16))
    for turn in range(BATCHES):
        slot = jnp.where(near[turn] > 0.0, counts[turn : turn + 1] - 1.0, -1.0)
        order_of_ref[turn : turn + 1] = slot.astype(I32)

    lane = lax.broadcasted_iota(I32, (1, CY), 1)
    cell_x = (place_x * CX).astype(F32)
    cell_y = (place_y * CY + lane).astype(F32)

    for turn in range(BATCHES):
        prior = state_ref[:, AHEAD + turn * OBS : AHEAD + (turn + 1) * OBS]
        error = jnp.where(kinds[turn] == 0, error_ref[0], error_ref[1])
        centre = jnp.sum(prior, axis=0, keepdims=True) * (1.0 / MEMBERS)
        deviation = prior - centre
        variance = jnp.sum(deviation * deviation, axis=0, keepdims=True) / (MEMBERS - 1)
        gain = (values[turn] - centre) / (variance + error)
        shrink = -1.0 / (jnp.sqrt(error * (error + variance)) + error + variance)
        drive_high, drive_low = halves(gain + shrink * deviation)
        drive_ref[:MEMBERS] = drive_high
        drive_ref[MEMBERS:] = drive_low
        scaled = deviation * (1.0 / (MEMBERS - 1))
        scaled_high = scaled.astype(BF16).astype(F32)
        scaled_low = scaled - scaled_high
        packed = jnp.concatenate(
            [scaled_high, scaled_high, scaled_low, jnp.zeros_like(scaled)], axis=0
        )
        sheet_ref[:, :CY] = packed.T.astype(BF16)

        later = list(range(turn + 1, BATCHES))
        blocks = [slice(group * CELLS, (group + 1) * CELLS) for group in range(GROUPS)]
        blocks += [slice(AHEAD + other * OBS, AHEAD + (other + 1) * OBS) for other in later]
        for cols in blocks:
            state = state_ref[:, cols]
            state_dev = state - jnp.sum(state, axis=0, keepdims=True) * (1.0 / MEMBERS)
            high, low = halves(state_dev)
            pack_ref[0:32, cols] = high
            pack_ref[32:64, cols] = low
            pack_ref[64:96, cols] = high
            pack_ref[96:128, cols] = jnp.zeros_like(high)

        total = jnp.sum(near[turn])
        trips = jnp.int32(0)
        for start in range(0, OBS, GATHER):
            trips = trips + jnp.where(total > float(start), 1, 0)
        slot = order_of_ref[turn : turn + 1]

        @pl.loop(0, trips)
        def _(step):
            place = lax.broadcasted_iota(I32, (GATHER, OBS), 0) + step * GATHER
            hot = jnp.where(place == slot, 1.0, 0.0).astype(BF16)
            sheet = mm(hot, sheet_ref[...])
            left = sheet[:, :CY].astype(BF16)
            table = sheet[:, CY : 2 * CY]
            marks = sheet[:, 2 * CY :].astype(BF16)
            drive = lax.dot_general(
                drive_ref[...], hot, (((1,), (1,)), ((), ())), preferred_element_type=F32
            ).astype(BF16)
            x_col = table[:, turn * 8 : turn * 8 + 1]
            y_col = table[:, turn * 8 + 1 : turn * 8 + 2] * CY + table[:, turn * 8 + 2 : turn * 8 + 3]
            mask_col = table[:, turn * 8 + 3 : turn * 8 + 4]
            gap_y = y_col - cell_y
            drop_y = gap_y * gap_y * (1.0 / (LOC_Y * LOC_Y))
            for x in range(CX):
                gap_x = jnp.abs(x_col - (cell_x + x))
                gap_x = jnp.minimum(gap_x, NX - gap_x)
                room = jnp.maximum((1.0 - gap_x * gap_x * (1.0 / (LOC_X * LOC_X))) - drop_y, 0.0)
                weight_ref[:, x * CY : (x + 1) * CY] = room * room * mask_col
            if later:
                column = table[:, turn * 8 + 4 : turn * 8 + 5].astype(I32)
                for index, other in enumerate(later):
                    number = PAIRS.index((turn, other))
                    allowed = mm(marks, spots_ref[:, number * OBS : (number + 1) * OBS])
                    apart = (columns[other] - column) & (TILES_X - 1)
                    allowed = jnp.where(apart < SPAN, allowed, 0.0)
                    gap_x = jnp.abs(x_col - xs[other])
                    gap_x = jnp.minimum(gap_x, NX - gap_x)
                    gap_y = y_col - ys[other]
                    room = 1.0 - gap_x * gap_x * (1.0 / (LOC_X * LOC_X))
                    room = jnp.maximum(room - gap_y * gap_y * (1.0 / (LOC_Y * LOC_Y)), 0.0)
                    weight_ref[:, (index + 1) * OBS : (index + 2) * OBS] = room * room * allowed

            for number, cols in enumerate(blocks):
                at = max(0, number - GROUPS + 1) * OBS
                covariance = mm(left, pack_ref[:, cols]) * weight_ref[:, at : at + OBS]
                high, low = halves(covariance)
                both = mm(drive, high)
                rest = mm(drive[:MEMBERS], low)
                state_ref[:, cols] += both[:MEMBERS] + both[MEMBERS:] + rest

    for group in range(GROUPS):
        for x in range(CX):
            at = group * CELLS + x * CY
            out_ref[rows_of(group, x), :] = state_ref[:, at : at + CY]


def call(kernel, specs, outs, scratch=()):
    return pl.pallas_call(
        kernel,
        in_specs=specs,
        out_specs=[VMEM] * len(outs) if len(outs) > 1 else VMEM,
        out_shape=outs if len(outs) > 1 else outs[0],
        scratch_shapes=list(scratch),
        compiler_params=pltpu.CompilerParams(vmem_limit_bytes=48 * 1024 * 1024),
    )


def shape(*dims):
    return jax.ShapeDtypeStruct(dims, F32)


def swapped(value, axis, step, periodic):
    count = lax.axis_size(axis)
    pairs = []
    for source in range(count):
        target = source + (step if source % 2 == 0 else -step)
        if periodic or 0 <= target < count:
            pairs.append((source, target % count))
    return lax.ppermute(value, axis, pairs)


def local(
    ensemble,
    courant,
    target_spread,
    obs_error,
    obs_value,
    obs_owner,
    obs_cell,
    obs_kind,
    tile_mask,
    batch_order,
):
    place_x = lax.axis_index(GX)
    place_y = lax.axis_index(GY)
    relay = lax.axis_index(PLANE) * LAYERS + lax.axis_index(LAYER)
    place = jnp.stack([place_x, place_y, relay]).astype(I32)
    ens = ensemble.reshape(MEMBERS * GROUPS * CX, CY)
    mask = tile_mask.reshape(BATCHES, 1, OBS)
    own, first, second, send = call(
        spread_kernel,
        [SMEM] * 3 + [VMEM] * 5,
        [
            shape(GROUPS, MEMBERS, CELLS),
            shape(SIDE, CY),
            shape(SIDE, CY),
            shape(PLANES * PLANE_ROWS, CY),
        ],
    )(batch_order, place, courant, ens, obs_owner, obs_cell, obs_kind, mask)
    recv = lax.all_to_all(send.reshape(PLANES, PLANE_ROWS, CY), PLANE, 0, 0)
    first = swapped(first, GX, 1, True)
    second = swapped(second, GX, -1, True)
    joined, send = call(
        collect_kernel,
        [SMEM] + [VMEM] * 4,
        [shape(GROUPS, MEMBERS, CELLS), shape(LAYERS * LAYER_ROWS, CY)],
    )(place, recv.reshape(PLANES * PLANE_ROWS, CY), own, first, second)
    recv = lax.all_to_all(send.reshape(LAYERS, LAYER_ROWS // 2, 2, CY), LAYER, 0, 0)
    recv = recv.reshape(LAYERS * LAYER_ROWS, CY)
    forecast, send = call(
        merge_kernel,
        [SMEM] * 3 + [VMEM] * 2,
        [shape(GROUPS, MEMBERS, CELLS), shape(2 * LAYERS, CY)],
    )(batch_order, place, obs_owner, joined, recv)
    recv = lax.all_to_all(send.reshape(LAYERS, 2, CY), LAYER, 0, 0)
    chips = PLANES // 2
    send = jnp.broadcast_to(recv.reshape(1, 2 * LAYERS, CY), (chips, 2 * LAYERS, CY))
    mine = lax.all_to_all(send, CHIP, 0, 0).reshape(TILES, CY)
    twin = lax.ppermute(mine, "core", [(0, 1), (1, 0)])
    out = call(
        assimilate_kernel,
        [SMEM] * 4 + [VMEM] * 8,
        [shape(MEMBERS * GROUPS * CX, CY)],
        [
            pltpu.VMEM((MEMBERS, AHEAD + BATCHES * OBS), F32),
            pltpu.VMEM((CY, AHEAD + BATCHES * OBS), BF16),
            pltpu.VMEM((OBS, 3 * CY), BF16),
            pltpu.VMEM((2 * MEMBERS, OBS), BF16),
            pltpu.VMEM((8, OBS), I32),
            pltpu.VMEM((CY, BATCHES * OBS), BF16),
            pltpu.VMEM((GATHER, BATCHES * OBS), F32),
            pltpu.VMEM((2 * TILES, CY), F32),
        ],
    )(
        batch_order,
        place,
        target_spread,
        obs_error,
        forecast,
        mine,
        twin,
        obs_owner,
        obs_cell,
        obs_kind,
        obs_value,
        mask,
    )
    return out.reshape(ensemble.shape)


def solution(mesh):
    fine = Mesh(mesh.devices.reshape(4, 8, 2, 2, 4), ("x", "z_lo", "core", "z_hi", "y"))
    in_specs = (
        P(None, None, None, GX, GY),
        P(),
        P(),
        P(),
        P(),
        P(),
        P(),
        P(),
        P(None, GX, GY, None),
        P(),
    )
    out_specs = P(None, None, None, GX, GY)
    return jax.shard_map(local, mesh=fine, in_specs=in_specs, out_specs=out_specs, check_vma=False)
```

```python
import jax
import jax.numpy as jnp
from jax import lax
from jax.experimental import pallas as pl
from jax.experimental.pallas import tpu as pltpu
from jax.sharding import Mesh
from jax.sharding import PartitionSpec as P

MEMBERS = 32
GROUPS = 4
CX = 4
CY = 128
CELLS = CX * CY
OBS = 512
BATCHES = 3
STEPS = 2
TILES_X = 64
TILES_Y = 8
TILES = TILES_X * TILES_Y
NX = TILES_X * CX
NY = TILES_Y * CY
LOC_X = 12.0
LOC_Y = 512.0
REACH = 2
SPAN = 2 * REACH + 1
PLANES = 32
LAYERS = 16
HALF = CY // 2
RIM = 16
VALUES = BATCHES * MEMBERS
PLANE_ROWS = LAYERS + RIM
LAYER_ROWS = RIM + 2
WIDE = (CX + 4) * CY
SIDE = 2 * GROUPS * MEMBERS
GX = ("x", "z_lo", "core")
GY = ("z_hi", "y")
PLANE = ("x", "core", "y")
LAYER = ("z_lo", "z_hi")
CHIP = ("x", "y")
CHUNK = 256
GATHER = 128
AHEAD = GROUPS * CELLS
PAIRS = ((0, 1), (0, 2), (1, 2))

diffuse_rate = 0.1
mixing_rate = 0.05
spread_floor = 1e-05

F32 = jnp.float32
BF16 = jnp.bfloat16
I32 = jnp.int32

VMEM = pl.BlockSpec(memory_space=pltpu.VMEM)
SMEM = pl.BlockSpec(memory_space=pltpu.SMEM)


def rows_of(group, x):
    return pl.ds(group * CX + x, MEMBERS, stride=GROUPS * CX)


def mm(a, b):
    return lax.dot_general(a, b, (((1,), (0,)), ((), ())), preferred_element_type=F32)


def flag(condition):
    return jnp.where(condition, 1.0, 0.0).astype(F32)


def halves(value):
    high = value.astype(BF16)
    return high, (value - high.astype(F32)).astype(BF16)


def thirds(value):
    high = value.astype(BF16)
    rest = value - high.astype(F32)
    middle = rest.astype(BF16)
    return high, middle, (rest - middle.astype(F32)).astype(BF16)


def advance(rows, courant_ref, keep):
    lowest = min(x for _, x in rows) - 1
    highest = max(x for _, x in rows) + 1
    width = 2 * CY
    after = {}
    for group in range(GROUPS):
        speed = courant_ref[group % 2]
        stay = 1.0 - speed - 4.0 * diffuse_rate - mixing_rate
        for x in range(lowest, highest + 1):
            terms = []
            if (group, x) in rows:
                here = rows[group, x]
                beside = pltpu.roll(here, 1, 1) + pltpu.roll(here, width - 1, 1)
                terms.append(stay * here + diffuse_rate * beside + mixing_rate * rows[group ^ 1, x])
            if (group, x - 1) in rows:
                terms.append((speed + diffuse_rate) * rows[group, x - 1])
            if (group, x + 1) in rows:
                terms.append(diffuse_rate * rows[group, x + 1])
            total = terms[0]
            for term in terms[1:]:
                total = total + term
            after[group, x] = total if keep is None else total * keep
    return after


def spread_kernel(
    order_ref,
    place_ref,
    courant_ref,
    ens_ref,
    owner_ref,
    cell_ref,
    kind_ref,
    mask_ref,
    target_ref,
    error_ref,
    value_ref,
    own_ref,
    first_ref,
    second_ref,
    send_ref,
):
    place_x = place_ref[0]
    place_y = place_ref[1]
    rows = {}
    for group in range(GROUPS):
        for x in range(CX):
            own = ens_ref[rows_of(group, x), :]
            rows[group, x] = jnp.concatenate([own, jnp.zeros_like(own)], axis=1)
    lane = lax.broadcasted_iota(I32, (1, 2 * CY), 1)
    below = (lane >= 3 * CY // 2) & (place_y == 0)
    above = (lane >= CY) & (lane < 3 * CY // 2) & (place_y == TILES_Y - 1)
    keep = jnp.where(below | above, 0.0, 1.0).astype(F32)
    rows = advance(rows, courant_ref, keep)
    rows = advance(rows, courant_ref, None)
    lane = lax.broadcasted_iota(I32, (MEMBERS, CY), 1)
    low = jnp.zeros((MEMBERS, CY), F32)
    high = jnp.zeros((MEMBERS, CY), F32)
    tile = {}
    for (group, x), value in rows.items():
        tile[group, x] = value[:, :CY]
        if 0 <= x < CX:
            own_ref[group, :, x * CY : (x + 1) * CY] = tile[group, x]
        edge = value[:, CY:]
        at = group * 16 + (x + 2) * 2
        there = (lane >> 1) == at // 2
        low = jnp.where(there, pltpu.roll(edge, at + 2, 1), low)
        high = jnp.where(there, pltpu.roll(edge, at, 1) if at else edge, high)
    rim = low + pltpu.roll(high, HALF, 1)
    even = (place_x & 1) == 0
    for group in range(GROUPS):
        for x in range(2):
            at = (group * 2 + x) * MEMBERS
            first_ref[at : at + MEMBERS] = jnp.where(even, tile[group, CX + x], tile[group, x - 2])
            second_ref[at : at + MEMBERS] = jnp.where(even, tile[group, x - 2], tile[group, CX + x])
    ground = jnp.concatenate(
        [
            jnp.concatenate([tile[2 * field, x] for x in range(-2, CX + 2)], axis=1)
            for field in range(2)
        ],
        axis=0,
    )
    parts = jnp.concatenate(thirds(ground), axis=0)
    rims = jnp.concatenate(thirds(rim), axis=0)
    blocks = []
    masks = []
    for turn in range(BATCHES):
        batch = order_ref[turn]
        owner = owner_ref[pl.ds(batch, 1), :]
        cell = cell_ref[pl.ds(batch, 1), :]
        kind = kind_ref[pl.ds(batch, 1), :]
        masks.append(mask_ref[batch].astype(F32))
        at_x = ((owner >> 3) - place_x) * CX + (cell >> 7) + 2
        at_x = at_x & (NX - 1)
        at_y = ((owner & (TILES_Y - 1)) - place_y) * CY + (cell & (CY - 1))
        seen = at_x < CX + 4
        index = jnp.where(seen & (at_y >= 0) & (at_y < CY), at_x * CY + at_y, -1)
        corner = kind * 32 + at_x * 2
        edge = jnp.where(seen & (at_y >= -2) & (at_y < 0), corner + at_y + 2, -1)
        edge = jnp.where(seen & (at_y >= CY) & (at_y < CY + 2), corner + at_y - CY + HALF, edge)
        picked = jnp.zeros((parts.shape[0], OBS), F32)
        for start in range(0, WIDE, CHUNK):
            spot = lax.broadcasted_iota(I32, (CHUNK, OBS), 0) + start
            hot = jnp.where(spot == index, 1.0, 0.0).astype(BF16)
            picked = picked + mm(parts[:, start : start + CHUNK], hot)
        picked = picked[0:64] + picked[64:128] + picked[128:192]
        spot = lax.broadcasted_iota(I32, (CY, OBS), 0)
        found = mm(rims, jnp.where(spot == edge, 1.0, 0.0).astype(BF16))
        found = found[0:32] + found[32:64] + found[64:96]
        blocks.append(jnp.where(kind == 0, picked[0:32], picked[32:64]) + found)
    sub = lax.broadcasted_iota(I32, (MEMBERS, OBS), 0)
    blocks.append(jnp.where(sub == 0, masks[0], jnp.where(sub == 1, masks[1], 0.0)))
    turned = jnp.concatenate(blocks, axis=0).T
    lane = lax.broadcasted_iota(I32, (RIM, CY), 1)
    low = jnp.where(lane < HALF, low[:RIM], pltpu.roll(low[RIM:], HALF, 1))
    high = jnp.where(lane < HALF, high[:RIM], pltpu.roll(high[RIM:], HALF, 1))
    y = place_y & 3
    for plane in range(PLANES):
        at = plane * PLANE_ROWS
        send_ref[at : at + LAYERS, :] = turned[plane * LAYERS : (plane + 1) * LAYERS]
        up = flag((y + 1) & 3 == plane & 3)
        down = flag((y + 3) & 3 == plane & 3)
        send_ref[at + LAYERS : at + PLANE_ROWS, :] = up * high + down * low


def collect_kernel(place_ref, far_ref, near_ref, recv_ref, own_ref, joined_ref, send_ref):
    even = (place_ref[0] & 1) == 0
    for group in range(GROUPS):
        for column in range(CX):
            at = (group * 2 + column % 2) * MEMBERS
            part = slice(at, at + MEMBERS)
            near, far = near_ref[part], far_ref[part]
            other = jnp.where(even, far, near) if column < 2 else jnp.where(even, near, far)
            cells = slice(column * CY, (column + 1) * CY)
            joined_ref[group, :, cells] = own_ref[group, :, cells] + other
    place_x = place_ref[0]
    place_y = place_ref[1]
    x, z_lo, core = place_x >> 4, (place_x >> 1) & 7, place_x & 1
    z_hi, y = place_y >> 2, place_y & 3
    lane = lax.broadcasted_iota(I32, (LAYERS, CY), 1)
    total = jnp.zeros((LAYERS, CY), F32)
    marks = jnp.zeros((LAYERS, CY), F32)
    for plane in range(PLANES):
        rows = recv_ref[plane * PLANE_ROWS : plane * PLANE_ROWS + LAYERS, :]
        total = total + rows
        for turn in range(2):
            at = VALUES + turn
            marks = jnp.where(lane == turn * PLANES + plane, rows[:, at : at + 1], marks)

    spot = lane & 15
    hop = jnp.where(core == 0, z_lo == 7, z_lo == 0)
    side = jnp.where(hop, (x + jnp.where(core == 0, 3, 1)) & 3, x)
    first = flag(core == 0)
    second = 1.0 - first

    def rim(column, other, step):
        plane = (column * 2 + other) * 4 + ((y + step) & 3)
        start = pl.multiple_of(plane * PLANE_ROWS + LAYERS, RIM)
        return recv_ref[pl.ds(start, RIM), :]

    def from_left(block):
        return jnp.where((spot >= 4) & (spot < 8), pltpu.roll(block, CY - 8, 1), 0.0)

    def from_right(block):
        return jnp.where((spot >= 8) & (spot < 12), pltpu.roll(block, 8, 1), 0.0)

    here, there = [], []
    for step in (3, 1):
        mine = jnp.where((spot >= 4) & (spot < 12), rim(x, core, step), 0.0)
        twin = rim(x, 1 - core, step)
        far = rim(side, 1 - core, step)
        block = mine + first * from_right(twin) + second * from_left(twin)
        other = first * from_left(far) + second * from_right(far)
        here.append(pltpu.roll(block, 8, 1) if step == 1 else block)
        there.append(pltpu.roll(other, 8, 1) if step == 1 else other)
    target = jnp.where(core == 0, z_lo + 1, z_lo + 7) & 7
    below = jnp.where(y > 0, z_hi, jnp.where(z_hi == 0, 1, -1))
    above = jnp.where(y < 3, z_hi, jnp.where(z_hi == 1, 0, -1))
    for layer in range(LAYERS):
        lower, higher = flag(below == layer % 2), flag(above == layer % 2)
        same, next_to = flag(z_lo == layer // 2), flag(target == layer // 2)
        at = layer * LAYER_ROWS
        send_ref[at : at + RIM, :] = same * (lower * here[0] + higher * here[1]) + next_to * (
            lower * there[0] + higher * there[1]
        )
        pair = jnp.concatenate([total[layer : layer + 1], marks[layer : layer + 1]], axis=0)
        send_ref[at + RIM : at + RIM + 2, :] = pair


def merge_kernel(
    order_ref,
    place_ref,
    relay_ref,
    joined_ref,
    recv_ref,
    forecast_ref,
    send_ref,
):
    relay = place_ref[2]
    lane = lax.broadcasted_iota(I32, (1, CY), 1)
    sums = recv_ref[pl.ds(RIM, LAYERS, stride=LAYER_ROWS), :]
    marks = recv_ref[pl.ds(RIM + 1, LAYERS, stride=LAYER_ROWS), :]
    top = jnp.sum(sums, axis=0, keepdims=True)
    top = jnp.where(lane < BATCHES * MEMBERS, top, 0.0)
    below = recv_ref[0:RIM, :]
    for layer in range(1, LAYERS):
        below = below + recv_ref[layer * LAYER_ROWS : layer * LAYER_ROWS + RIM, :]
    above = pltpu.roll(below, CY - 8, 1)
    below = jnp.concatenate([below, pltpu.roll(below, HALF, 1)], axis=0)
    above = jnp.concatenate([above, pltpu.roll(above, HALF, 1)], axis=0)
    wide = lax.broadcasted_iota(I32, (MEMBERS, CY), 1)
    for group in range(GROUPS):
        pieces = []
        for x in range(CX):
            at = group * 16 + (x + 2) * 2
            piece = joined_ref[group, :, x * CY : (x + 1) * CY]
            piece = piece + jnp.where(wide < 2, pltpu.roll(below, CY - at, 1), 0.0)
            piece = piece + jnp.where(wide >= CY - 2, pltpu.roll(above, CY - 2 - at, 1), 0.0)
            pieces.append(piece)
        value = jnp.concatenate(pieces, axis=1)
        forecast_ref[group] = value
        centre = jnp.sum(value, axis=0, keepdims=True) * (1.0 / MEMBERS)
        deviation = value - centre
        total = jnp.sum(jnp.sum(deviation * deviation, axis=0, keepdims=True), axis=1, keepdims=True)
        top = jnp.where(lane == BATCHES * MEMBERS + group, total, top)

    lanes = lax.broadcasted_iota(I32, (LAYERS, CY), 1)
    subs = lax.broadcasted_iota(I32, (LAYERS, CY), 0)
    tile_x = ((lanes >> 3) & 3) * 16 + (subs >> 1) * 2 + ((lanes >> 2) & 1)
    first = relay_ref[order_ref[0], relay] >> 3
    second = relay_ref[order_ref[1], relay] >> 3
    column = jnp.where(lanes < PLANES, first, second)
    near = ((tile_x - column + REACH) & (TILES_X - 1)) < SPAN
    marks = jnp.where(near & (lanes < 2 * PLANES), marks, 0.0)
    marks = marks[:8] + marks[8:]
    folded = marks
    for step in (8, 16, 24):
        folded = folded + pltpu.roll(marks, CY - step, 1)
    lanes = lax.broadcasted_iota(I32, (8, CY), 1)
    subs = lax.broadcasted_iota(I32, (8, CY), 0)
    bottom = jnp.zeros((8, CY), F32)
    for row in range(8):
        for turn in range(2):
            moved = pltpu.roll(folded, (turn * PLANES + row * 8) % CY, 1)
            there = (subs == row) & ((lanes >> 3) == turn * 8 + row)
            bottom = jnp.where(there, moved, bottom)
    bottom = jnp.sum(bottom, axis=0, keepdims=True)
    pair = jnp.concatenate([top, bottom] * 4, axis=0)
    send_ref[...] = jnp.concatenate([pair] * (2 * LAYERS // 8), axis=0)


def assimilate_kernel(
    order_ref,
    place_ref,
    spread_ref,
    error_ref,
    forecast_ref,
    mine_ref,
    twin_ref,
    owner_ref,
    cell_ref,
    kind_ref,
    value_ref,
    mask_ref,
    out_ref,
    state_ref,
    pack_ref,
    sheet_ref,
    drive_ref,
    order_of_ref,
    spots_ref,
    weight_ref,
    recv_ref,
):
    place_x = place_ref[0]
    place_y = place_ref[1]
    first = (place_x & 1) == 0
    for plane in range(PLANES):
        source = (plane // 8 * 4 + plane % 4) * 2 * LAYERS
        source = slice(source, source + 2 * LAYERS)
        mine, twin = mine_ref[source], twin_ref[source]
        rows = jnp.where(first, twin, mine) if plane // 4 % 2 else jnp.where(first, mine, twin)
        recv_ref[plane * 2 * LAYERS : (plane + 1) * 2 * LAYERS] = rows
    upper = recv_ref[pl.ds(0, TILES, stride=2), :].T
    stretch = []
    for group in range(GROUPS):
        row = BATCHES * MEMBERS + group
        total = jnp.sum(upper[row : row + 1], axis=1, keepdims=True)
        mean_var = total * (1.0 / ((MEMBERS - 1) * float(NX * NY)))
        stretch.append(jnp.sqrt(spread_ref[group // 2, group % 2] / (mean_var + spread_floor)))
    for group in range(GROUPS):
        value = forecast_ref[group]
        centre = jnp.sum(value, axis=0, keepdims=True) * (1.0 / MEMBERS)
        state_ref[:, group * CELLS : (group + 1) * CELLS] = centre + stretch[group] * (value - centre)

    kinds, xs, ys, values = [], [], [], []
    sub = lax.broadcasted_iota(I32, (CY, OBS), 0)
    table = jnp.zeros((CY, OBS), F32)
    near = []
    columns, spots = [], []
    for turn in range(BATCHES):
        batch = order_ref[turn]
        owner = owner_ref[pl.ds(batch, 1), :]
        cell = cell_ref[pl.ds(batch, 1), :]
        kinds.append(kind_ref[pl.ds(batch, 1), :])
        values.append(value_ref[pl.ds(batch, 1), :])
        mask = mask_ref[batch].astype(F32)
        xs.append(((owner >> 3) * CX + (cell >> 7)).astype(F32))
        ys.append(((owner & (TILES_Y - 1)) * CY + (cell & (CY - 1))).astype(F32))
        tile_x = owner >> 3
        columns.append(tile_x + REACH)
        reach = REACH * (BATCHES - turn)
        near.append(flag(((tile_x - place_x + reach) & (TILES_X - 1)) <= 2 * reach))
        facts = (
            xs[turn],
            (owner & (TILES_Y - 1)).astype(F32),
            (cell & (CY - 1)).astype(F32),
            mask,
            tile_x.astype(F32),
        )
        for row, value in enumerate(facts):
            table = jnp.where(sub == turn * 8 + row, value, table)
        prior = upper[turn * MEMBERS : (turn + 1) * MEMBERS]
        centre = jnp.sum(prior, axis=0, keepdims=True) * (1.0 / MEMBERS)
        factor = jnp.where(kinds[turn] == 0, stretch[0], stretch[2])
        state_ref[:, AHEAD + turn * OBS : AHEAD + (turn + 1) * OBS] = centre + factor * (prior - centre)
        strip = ((tile_x >> 1) & 3) * 2 + ((owner >> 2) & 1)
        spots.append(strip * 8 + (tile_x & 1) * 4 + (owner & 3))
    for number, (turn, other) in enumerate(PAIRS):
        hot = jnp.where(sub == spots[other] + turn * HALF, 1.0, 0.0)
        spots_ref[:, number * OBS : (number + 1) * OBS] = hot.astype(BF16)
    sheet_ref[:, CY : 2 * CY] = table.T.astype(BF16)
    sheet_ref[:, 2 * CY : 3 * CY] = recv_ref[pl.ds(1, TILES, stride=2), :].astype(BF16)
    ahead = lax.broadcasted_iota(I32, (OBS, OBS), 0) <= lax.broadcasted_iota(I32, (OBS, OBS), 1)
    counts = jnp.concatenate([*near, jnp.zeros((8 - BATCHES, OBS), F32)], axis=0)
    counts = mm(counts.astype(BF16), jnp.where(ahead, 1.0, 0.0).astype(BF16))
    for turn in range(BATCHES):
        slot = jnp.where(near[turn] > 0.0, counts[turn : turn + 1] - 1.0, -1.0)
        order_of_ref[turn : turn + 1] = slot.astype(I32)

    lane = lax.broadcasted_iota(I32, (1, CY), 1)
    cell_x = (place_x * CX).astype(F32)
    cell_y = (place_y * CY + lane).astype(F32)

    for turn in range(BATCHES):
        prior = state_ref[:, AHEAD + turn * OBS : AHEAD + (turn + 1) * OBS]
        error = jnp.where(kinds[turn] == 0, error_ref[0], error_ref[1])
        centre = jnp.sum(prior, axis=0, keepdims=True) * (1.0 / MEMBERS)
        deviation = prior - centre
        variance = jnp.sum(deviation * deviation, axis=0, keepdims=True) / (MEMBERS - 1)
        gain = (values[turn] - centre) / (variance + error)
        shrink = -1.0 / (jnp.sqrt(error * (error + variance)) + error + variance)
        drive_high, drive_low = halves(gain + shrink * deviation)
        drive_ref[:MEMBERS] = drive_high
        drive_ref[MEMBERS:] = drive_low
        scaled = deviation * (1.0 / (MEMBERS - 1))
        scaled_high = scaled.astype(BF16).astype(F32)
        scaled_low = scaled - scaled_high
        packed = jnp.concatenate(
            [scaled_high, scaled_high, scaled_low, jnp.zeros_like(scaled)], axis=0
        )
        sheet_ref[:, :CY] = packed.T.astype(BF16)

        later = list(range(turn + 1, BATCHES))
        blocks = [slice(group * CELLS, (group + 1) * CELLS) for group in range(GROUPS)]
        blocks += [slice(AHEAD + other * OBS, AHEAD + (other + 1) * OBS) for other in later]
        for cols in blocks:
            state = state_ref[:, cols]
            state_dev = state - jnp.sum(state, axis=0, keepdims=True) * (1.0 / MEMBERS)
            high, low = halves(state_dev)
            pack_ref[0:32, cols] = high
            pack_ref[32:64, cols] = low
            pack_ref[64:96, cols] = high
            pack_ref[96:128, cols] = jnp.zeros_like(high)

        total = jnp.sum(near[turn])
        trips = jnp.int32(0)
        for start in range(0, OBS, GATHER):
            trips = trips + jnp.where(total > float(start), 1, 0)
        slot = order_of_ref[turn : turn + 1]

        @pl.loop(0, trips)
        def _(step):
            place = lax.broadcasted_iota(I32, (GATHER, OBS), 0) + step * GATHER
            hot = jnp.where(place == slot, 1.0, 0.0).astype(BF16)
            sheet = mm(hot, sheet_ref[...])
            left = sheet[:, :CY].astype(BF16)
            table = sheet[:, CY : 2 * CY]
            marks = sheet[:, 2 * CY :].astype(BF16)
            drive = lax.dot_general(
                drive_ref[...], hot, (((1,), (1,)), ((), ())), preferred_element_type=F32
            ).astype(BF16)
            x_col = table[:, turn * 8 : turn * 8 + 1]
            y_col = table[:, turn * 8 + 1 : turn * 8 + 2] * CY + table[:, turn * 8 + 2 : turn * 8 + 3]
            mask_col = table[:, turn * 8 + 3 : turn * 8 + 4]
            gap_y = y_col - cell_y
            drop_y = gap_y * gap_y * (1.0 / (LOC_Y * LOC_Y))
            for x in range(CX):
                gap_x = jnp.abs(x_col - (cell_x + x))
                gap_x = jnp.minimum(gap_x, NX - gap_x)
                room = jnp.maximum((1.0 - gap_x * gap_x * (1.0 / (LOC_X * LOC_X))) - drop_y, 0.0)
                weight_ref[:, x * CY : (x + 1) * CY] = room * room * mask_col
            if later:
                column = table[:, turn * 8 + 4 : turn * 8 + 5].astype(I32)
                for index, other in enumerate(later):
                    number = PAIRS.index((turn, other))
                    allowed = mm(marks, spots_ref[:, number * OBS : (number + 1) * OBS])
                    apart = (columns[other] - column) & (TILES_X - 1)
                    allowed = jnp.where(apart < SPAN, allowed, 0.0)
                    gap_x = jnp.abs(x_col - xs[other])
                    gap_x = jnp.minimum(gap_x, NX - gap_x)
                    gap_y = y_col - ys[other]
                    room = 1.0 - gap_x * gap_x * (1.0 / (LOC_X * LOC_X))
                    room = jnp.maximum(room - gap_y * gap_y * (1.0 / (LOC_Y * LOC_Y)), 0.0)
                    weight_ref[:, (index + 1) * OBS : (index + 2) * OBS] = room * room * allowed

            for number, cols in enumerate(blocks):
                at = max(0, number - GROUPS + 1) * OBS
                covariance = mm(left, pack_ref[:, cols]) * weight_ref[:, at : at + OBS]
                high, low = halves(covariance)
                both = mm(drive, high)
                rest = mm(drive[:MEMBERS], low)
                state_ref[:, cols] += both[:MEMBERS] + both[MEMBERS:] + rest

    for group in range(GROUPS):
        for x in range(CX):
            at = group * CELLS + x * CY
            out_ref[rows_of(group, x), :] = state_ref[:, at : at + CY]


def call(kernel, specs, outs, scratch=()):
    return pl.pallas_call(
        kernel,
        in_specs=specs,
        out_specs=[VMEM] * len(outs) if len(outs) > 1 else VMEM,
        out_shape=outs if len(outs) > 1 else outs[0],
        scratch_shapes=list(scratch),
        compiler_params=pltpu.CompilerParams(vmem_limit_bytes=48 * 1024 * 1024),
    )


def shape(*dims):
    return jax.ShapeDtypeStruct(dims, F32)


def swapped(value, axis, step, periodic):
    count = lax.axis_size(axis)
    pairs = []
    for source in range(count):
        target = source + (step if source % 2 == 0 else -step)
        if periodic or 0 <= target < count:
            pairs.append((source, target % count))
    return lax.ppermute(value, axis, pairs)


def local(
    ensemble,
    courant,
    target_spread,
    obs_error,
    obs_value,
    obs_owner,
    obs_cell,
    obs_kind,
    tile_mask,
    batch_order,
):
    place_x = lax.axis_index(GX)
    place_y = lax.axis_index(GY)
    relay = lax.axis_index(PLANE) * LAYERS + lax.axis_index(LAYER)
    place = jnp.stack([place_x, place_y, relay]).astype(I32)
    ens = ensemble.reshape(MEMBERS * GROUPS * CX, CY)
    mask = tile_mask.reshape(BATCHES, 1, OBS)
    own, first, second, send = call(
        spread_kernel,
        [SMEM] * 3 + [VMEM] * 8,
        [
            shape(GROUPS, MEMBERS, CELLS),
            shape(SIDE, CY),
            shape(SIDE, CY),
            shape(PLANES * PLANE_ROWS, CY),
        ],
    )(
        batch_order,
        place,
        courant,
        ens,
        obs_owner,
        obs_cell,
        obs_kind,
        mask,
        target_spread,
        obs_error,
        obs_value,
    )
    recv = lax.all_to_all(send.reshape(PLANES, PLANE_ROWS, CY), PLANE, 0, 0)
    second = swapped(second, GX, -1, True)
    first = swapped(first, GX, 1, True)
    joined, send = call(
        collect_kernel,
        [SMEM] + [VMEM] * 4,
        [shape(GROUPS, MEMBERS, CELLS), shape(LAYERS * LAYER_ROWS, CY)],
    )(place, second, first, recv.reshape(PLANES * PLANE_ROWS, CY), own)
    recv = lax.all_to_all(send.reshape(LAYERS, LAYER_ROWS // 2, 2, CY), LAYER, 0, 0)
    recv = recv.reshape(LAYERS * LAYER_ROWS, CY)
    forecast, send = call(
        merge_kernel,
        [SMEM] * 3 + [VMEM] * 2,
        [shape(GROUPS, MEMBERS, CELLS), shape(2 * LAYERS, CY)],
    )(batch_order, place, obs_owner, joined, recv)
    recv = lax.all_to_all(send.reshape(LAYERS, 2, CY), LAYER, 0, 0)
    chips = PLANES // 2
    send = jnp.broadcast_to(recv.reshape(1, 2 * LAYERS, CY), (chips, 2 * LAYERS, CY))
    mine = lax.all_to_all(send, CHIP, 0, 0).reshape(TILES, CY)
    twin = lax.ppermute(mine, "core", [(0, 1), (1, 0)])
    out = call(
        assimilate_kernel,
        [SMEM] * 4 + [VMEM] * 8,
        [shape(MEMBERS * GROUPS * CX, CY)],
        [
            pltpu.VMEM((MEMBERS, AHEAD + BATCHES * OBS), F32),
            pltpu.VMEM((CY, AHEAD + BATCHES * OBS), BF16),
            pltpu.VMEM((OBS, 3 * CY), BF16),
            pltpu.VMEM((2 * MEMBERS, OBS), BF16),
            pltpu.VMEM((8, OBS), I32),
            pltpu.VMEM((CY, BATCHES * OBS), BF16),
            pltpu.VMEM((GATHER, BATCHES * OBS), F32),
            pltpu.VMEM((2 * TILES, CY), F32),
        ],
    )(
        batch_order,
        place,
        target_spread,
        obs_error,
        forecast,
        mine,
        twin,
        obs_owner,
        obs_cell,
        obs_kind,
        obs_value,
        mask,
    )
    return out.reshape(ensemble.shape)


def solution(mesh):
    fine = Mesh(mesh.devices.reshape(4, 8, 2, 2, 4), ("x", "z_lo", "core", "z_hi", "y"))
    in_specs = (
        P(None, None, None, GX, GY),
        P(),
        P(),
        P(),
        P(),
        P(),
        P(),
        P(),
        P(None, GX, GY, None),
        P(),
    )
    out_specs = P(None, None, None, GX, GY)
    return jax.shard_map(local, mesh=fine, in_specs=in_specs, out_specs=out_specs, check_vma=False)
```

```python
import jax
import jax.numpy as jnp
from jax import lax
from jax.experimental import pallas as pl
from jax.experimental.pallas import tpu as pltpu
from jax.sharding import Mesh
from jax.sharding import PartitionSpec as P

MEMBERS = 32
GROUPS = 4
CX = 4
CY = 128
CELLS = CX * CY
OBS = 512
BATCHES = 3
STEPS = 2
TILES_X = 64
TILES_Y = 8
TILES = TILES_X * TILES_Y
NX = TILES_X * CX
NY = TILES_Y * CY
LOC_X = 12.0
LOC_Y = 512.0
REACH = 2
SPAN = 2 * REACH + 1
PLANES = 32
LAYERS = 16
HALF = CY // 2
RIM = 16
VALUES = BATCHES * MEMBERS
PLANE_ROWS = LAYERS + RIM
LAYER_ROWS = RIM + 2
WIDE = (CX + 4) * CY
SIDE = 2 * GROUPS * MEMBERS
GX = ("x", "z_lo", "core")
GY = ("z_hi", "y")
PLANE = ("x", "core", "y")
LAYER = ("z_lo", "z_hi")
CHIP = ("x", "y")
CHUNK = 256
GATHER = 128
AHEAD = GROUPS * CELLS
PAIRS = ((0, 1), (0, 2), (1, 2))

diffuse_rate = 0.1
mixing_rate = 0.05
spread_floor = 1e-05

F32 = jnp.float32
BF16 = jnp.bfloat16
I32 = jnp.int32

VMEM = pl.BlockSpec(memory_space=pltpu.VMEM)
SMEM = pl.BlockSpec(memory_space=pltpu.SMEM)


def rows_of(group, x):
    return pl.ds(group * CX + x, MEMBERS, stride=GROUPS * CX)


def mm(a, b):
    return lax.dot_general(a, b, (((1,), (0,)), ((), ())), preferred_element_type=F32)


def flag(condition):
    return jnp.where(condition, 1.0, 0.0).astype(F32)


def halves(value):
    high = value.astype(BF16)
    return high, (value - high.astype(F32)).astype(BF16)


def thirds(value):
    high = value.astype(BF16)
    rest = value - high.astype(F32)
    middle = rest.astype(BF16)
    return high, middle, (rest - middle.astype(F32)).astype(BF16)


def advance(rows, courant_ref, keep):
    lowest = min(x for _, x in rows) - 1
    highest = max(x for _, x in rows) + 1
    width = 2 * CY
    after = {}
    for group in range(GROUPS):
        speed = courant_ref[group % 2]
        stay = 1.0 - speed - 4.0 * diffuse_rate - mixing_rate
        for x in range(lowest, highest + 1):
            terms = []
            if (group, x) in rows:
                here = rows[group, x]
                beside = pltpu.roll(here, 1, 1) + pltpu.roll(here, width - 1, 1)
                terms.append(stay * here + diffuse_rate * beside + mixing_rate * rows[group ^ 1, x])
            if (group, x - 1) in rows:
                terms.append((speed + diffuse_rate) * rows[group, x - 1])
            if (group, x + 1) in rows:
                terms.append(diffuse_rate * rows[group, x + 1])
            total = terms[0]
            for term in terms[1:]:
                total = total + term
            after[group, x] = total if keep is None else total * keep
    return after


def spread_kernel(
    order_ref,
    place_ref,
    courant_ref,
    ens_ref,
    owner_ref,
    cell_ref,
    kind_ref,
    mask_ref,
    target_ref,
    error_ref,
    value_ref,
    own_ref,
    first_ref,
    second_ref,
    send_ref,
):
    place_x = place_ref[0]
    place_y = place_ref[1]
    rows = {}
    for group in range(GROUPS):
        for x in range(CX):
            own = ens_ref[rows_of(group, x), :]
            rows[group, x] = jnp.concatenate([own, jnp.zeros_like(own)], axis=1)
    lane = lax.broadcasted_iota(I32, (1, 2 * CY), 1)
    below = (lane >= 3 * CY // 2) & (place_y == 0)
    above = (lane >= CY) & (lane < 3 * CY // 2) & (place_y == TILES_Y - 1)
    keep = jnp.where(below | above, 0.0, 1.0).astype(F32)
    rows = advance(rows, courant_ref, keep)
    rows = advance(rows, courant_ref, None)
    lane = lax.broadcasted_iota(I32, (MEMBERS, CY), 1)
    low = jnp.zeros((MEMBERS, CY), F32)
    high = jnp.zeros((MEMBERS, CY), F32)
    tile = {}
    for (group, x), value in rows.items():
        tile[group, x] = value[:, :CY]
        if 0 <= x < CX:
            own_ref[group, :, x * CY : (x + 1) * CY] = tile[group, x]
        edge = value[:, CY:]
        at = group * 16 + (x + 2) * 2
        there = (lane >> 1) == at // 2
        low = jnp.where(there, pltpu.roll(edge, at + 2, 1), low)
        high = jnp.where(there, pltpu.roll(edge, at, 1) if at else edge, high)
    rim = low + pltpu.roll(high, HALF, 1)
    even = (place_x & 1) == 0
    for group in range(GROUPS):
        for x in range(2):
            at = (group * 2 + x) * MEMBERS
            first_ref[at : at + MEMBERS] = jnp.where(even, tile[group, CX + x], tile[group, x - 2])
            second_ref[at : at + MEMBERS] = jnp.where(even, tile[group, x - 2], tile[group, CX + x])
    ground = jnp.concatenate(
        [
            jnp.concatenate([tile[2 * field, x] for x in range(-2, CX + 2)], axis=1)
            for field in range(2)
        ],
        axis=0,
    )
    parts = jnp.concatenate(thirds(ground), axis=0)
    rims = jnp.concatenate(thirds(rim), axis=0)
    blocks = []
    masks = []
    for turn in range(BATCHES):
        batch = order_ref[turn]
        owner = owner_ref[pl.ds(batch, 1), :]
        cell = cell_ref[pl.ds(batch, 1), :]
        kind = kind_ref[pl.ds(batch, 1), :]
        masks.append(mask_ref[batch].astype(F32))
        at_x = ((owner >> 3) - place_x) * CX + (cell >> 7) + 2
        at_x = at_x & (NX - 1)
        at_y = ((owner & (TILES_Y - 1)) - place_y) * CY + (cell & (CY - 1))
        seen = at_x < CX + 4
        index = jnp.where(seen & (at_y >= 0) & (at_y < CY), at_x * CY + at_y, -1)
        corner = kind * 32 + at_x * 2
        edge = jnp.where(seen & (at_y >= -2) & (at_y < 0), corner + at_y + 2, -1)
        edge = jnp.where(seen & (at_y >= CY) & (at_y < CY + 2), corner + at_y - CY + HALF, edge)
        picked = jnp.zeros((parts.shape[0], OBS), F32)
        for start in range(0, WIDE, CHUNK):
            spot = lax.broadcasted_iota(I32, (CHUNK, OBS), 0) + start
            hot = jnp.where(spot == index, 1.0, 0.0).astype(BF16)
            picked = picked + mm(parts[:, start : start + CHUNK], hot)
        picked = picked[0:64] + picked[64:128] + picked[128:192]
        spot = lax.broadcasted_iota(I32, (CY, OBS), 0)
        found = mm(rims, jnp.where(spot == edge, 1.0, 0.0).astype(BF16))
        found = found[0:32] + found[32:64] + found[64:96]
        blocks.append(jnp.where(kind == 0, picked[0:32], picked[32:64]) + found)
    sub = lax.broadcasted_iota(I32, (MEMBERS, OBS), 0)
    blocks.append(jnp.where(sub == 0, masks[0], jnp.where(sub == 1, masks[1], 0.0)))
    turned = jnp.concatenate(blocks, axis=0).T
    lane = lax.broadcasted_iota(I32, (RIM, CY), 1)
    low = jnp.where(lane < HALF, low[:RIM], pltpu.roll(low[RIM:], HALF, 1))
    high = jnp.where(lane < HALF, high[:RIM], pltpu.roll(high[RIM:], HALF, 1))
    y = place_y & 3
    for plane in range(PLANES):
        at = plane * PLANE_ROWS
        send_ref[at : at + LAYERS, :] = turned[plane * LAYERS : (plane + 1) * LAYERS]
        up = flag((y + 1) & 3 == plane & 3)
        down = flag((y + 3) & 3 == plane & 3)
        send_ref[at + LAYERS : at + PLANE_ROWS, :] = up * high + down * low


def collect_kernel(place_ref, far_ref, recv_ref, own_ref, joined_ref, send_ref):
    even = (place_ref[0] & 1) == 0
    for group in range(GROUPS):
        for column in range(CX):
            at = (group * 2 + column % 2) * MEMBERS
            part = slice(at, at + MEMBERS)
            far = far_ref[part]
            other = jnp.where(even, far, 0.0) if column < 2 else jnp.where(even, 0.0, far)
            cells = slice(column * CY, (column + 1) * CY)
            joined_ref[group, :, cells] = own_ref[group, :, cells] + other
    place_x = place_ref[0]
    place_y = place_ref[1]
    x, z_lo, core = place_x >> 4, (place_x >> 1) & 7, place_x & 1
    z_hi, y = place_y >> 2, place_y & 3
    lane = lax.broadcasted_iota(I32, (LAYERS, CY), 1)
    total = jnp.zeros((LAYERS, CY), F32)
    marks = jnp.zeros((LAYERS, CY), F32)
    for plane in range(PLANES):
        rows = recv_ref[plane * PLANE_ROWS : plane * PLANE_ROWS + LAYERS, :]
        total = total + rows
        for turn in range(2):
            at = VALUES + turn
            marks = jnp.where(lane == turn * PLANES + plane, rows[:, at : at + 1], marks)

    spot = lane & 15
    hop = jnp.where(core == 0, z_lo == 7, z_lo == 0)
    side = jnp.where(hop, (x + jnp.where(core == 0, 3, 1)) & 3, x)
    first = flag(core == 0)
    second = 1.0 - first

    def rim(column, other, step):
        plane = (column * 2 + other) * 4 + ((y + step) & 3)
        start = pl.multiple_of(plane * PLANE_ROWS + LAYERS, RIM)
        return recv_ref[pl.ds(start, RIM), :]

    def from_left(block):
        return jnp.where((spot >= 4) & (spot < 8), pltpu.roll(block, CY - 8, 1), 0.0)

    def from_right(block):
        return jnp.where((spot >= 8) & (spot < 12), pltpu.roll(block, 8, 1), 0.0)

    here, there = [], []
    for step in (3, 1):
        mine = jnp.where((spot >= 4) & (spot < 12), rim(x, core, step), 0.0)
        twin = rim(x, 1 - core, step)
        far = rim(side, 1 - core, step)
        block = mine + first * from_right(twin) + second * from_left(twin)
        other = first * from_left(far) + second * from_right(far)
        here.append(pltpu.roll(block, 8, 1) if step == 1 else block)
        there.append(pltpu.roll(other, 8, 1) if step == 1 else other)
    target = jnp.where(core == 0, z_lo + 1, z_lo + 7) & 7
    below = jnp.where(y > 0, z_hi, jnp.where(z_hi == 0, 1, -1))
    above = jnp.where(y < 3, z_hi, jnp.where(z_hi == 1, 0, -1))
    for layer in range(LAYERS):
        lower, higher = flag(below == layer % 2), flag(above == layer % 2)
        same, next_to = flag(z_lo == layer // 2), flag(target == layer // 2)
        at = layer * LAYER_ROWS
        send_ref[at : at + RIM, :] = same * (lower * here[0] + higher * here[1]) + next_to * (
            lower * there[0] + higher * there[1]
        )
        pair = jnp.concatenate([total[layer : layer + 1], marks[layer : layer + 1]], axis=0)
        send_ref[at + RIM : at + RIM + 2, :] = pair


def merge_kernel(
    order_ref,
    place_ref,
    relay_ref,
    joined_ref,
    near_ref,
    recv_ref,
    forecast_ref,
    send_ref,
):
    relay = place_ref[2]
    lane = lax.broadcasted_iota(I32, (1, CY), 1)
    sums = recv_ref[pl.ds(RIM, LAYERS, stride=LAYER_ROWS), :]
    marks = recv_ref[pl.ds(RIM + 1, LAYERS, stride=LAYER_ROWS), :]
    top = jnp.sum(sums, axis=0, keepdims=True)
    top = jnp.where(lane < BATCHES * MEMBERS, top, 0.0)
    below = recv_ref[0:RIM, :]
    for layer in range(1, LAYERS):
        below = below + recv_ref[layer * LAYER_ROWS : layer * LAYER_ROWS + RIM, :]
    above = pltpu.roll(below, CY - 8, 1)
    below = jnp.concatenate([below, pltpu.roll(below, HALF, 1)], axis=0)
    above = jnp.concatenate([above, pltpu.roll(above, HALF, 1)], axis=0)
    even = (place_ref[0] & 1) == 0
    wide = lax.broadcasted_iota(I32, (MEMBERS, CY), 1)
    for group in range(GROUPS):
        pieces = []
        for x in range(CX):
            at = group * 16 + (x + 2) * 2
            part = (group * 2 + x % 2) * MEMBERS
            near = near_ref[part : part + MEMBERS]
            near = jnp.where(even, 0.0, near) if x < 2 else jnp.where(even, near, 0.0)
            piece = joined_ref[group, :, x * CY : (x + 1) * CY] + near
            piece = piece + jnp.where(wide < 2, pltpu.roll(below, CY - at, 1), 0.0)
            piece = piece + jnp.where(wide >= CY - 2, pltpu.roll(above, CY - 2 - at, 1), 0.0)
            pieces.append(piece)
        value = jnp.concatenate(pieces, axis=1)
        forecast_ref[group] = value
        centre = jnp.sum(value, axis=0, keepdims=True) * (1.0 / MEMBERS)
        deviation = value - centre
        total = jnp.sum(jnp.sum(deviation * deviation, axis=0, keepdims=True), axis=1, keepdims=True)
        top = jnp.where(lane == BATCHES * MEMBERS + group, total, top)

    lanes = lax.broadcasted_iota(I32, (LAYERS, CY), 1)
    subs = lax.broadcasted_iota(I32, (LAYERS, CY), 0)
    tile_x = ((lanes >> 3) & 3) * 16 + (subs >> 1) * 2 + ((lanes >> 2) & 1)
    first = relay_ref[order_ref[0], relay] >> 3
    second = relay_ref[order_ref[1], relay] >> 3
    column = jnp.where(lanes < PLANES, first, second)
    near = ((tile_x - column + REACH) & (TILES_X - 1)) < SPAN
    marks = jnp.where(near & (lanes < 2 * PLANES), marks, 0.0)
    marks = marks[:8] + marks[8:]
    folded = marks
    for step in (8, 16, 24):
        folded = folded + pltpu.roll(marks, CY - step, 1)
    lanes = lax.broadcasted_iota(I32, (8, CY), 1)
    subs = lax.broadcasted_iota(I32, (8, CY), 0)
    bottom = jnp.zeros((8, CY), F32)
    for row in range(8):
        for turn in range(2):
            moved = pltpu.roll(folded, (turn * PLANES + row * 8) % CY, 1)
            there = (subs == row) & ((lanes >> 3) == turn * 8 + row)
            bottom = jnp.where(there, moved, bottom)
    bottom = jnp.sum(bottom, axis=0, keepdims=True)
    pair = jnp.concatenate([top, bottom] * 4, axis=0)
    send_ref[...] = jnp.concatenate([pair] * (2 * LAYERS // 8), axis=0)


def assimilate_kernel(
    order_ref,
    place_ref,
    spread_ref,
    error_ref,
    forecast_ref,
    mine_ref,
    twin_ref,
    owner_ref,
    cell_ref,
    kind_ref,
    value_ref,
    mask_ref,
    out_ref,
    state_ref,
    pack_ref,
    sheet_ref,
    drive_ref,
    order_of_ref,
    spots_ref,
    weight_ref,
    recv_ref,
):
    place_x = place_ref[0]
    place_y = place_ref[1]
    first = (place_x & 1) == 0
    for plane in range(PLANES):
        source = (plane // 8 * 4 + plane % 4) * 2 * LAYERS
        source = slice(source, source + 2 * LAYERS)
        mine, twin = mine_ref[source], twin_ref[source]
        rows = jnp.where(first, twin, mine) if plane // 4 % 2 else jnp.where(first, mine, twin)
        recv_ref[plane * 2 * LAYERS : (plane + 1) * 2 * LAYERS] = rows
    upper = recv_ref[pl.ds(0, TILES, stride=2), :].T
    stretch = []
    for group in range(GROUPS):
        row = BATCHES * MEMBERS + group
        total = jnp.sum(upper[row : row + 1], axis=1, keepdims=True)
        mean_var = total * (1.0 / ((MEMBERS - 1) * float(NX * NY)))
        stretch.append(jnp.sqrt(spread_ref[group // 2, group % 2] / (mean_var + spread_floor)))
    for group in range(GROUPS):
        value = forecast_ref[group]
        centre = jnp.sum(value, axis=0, keepdims=True) * (1.0 / MEMBERS)
        state_ref[:, group * CELLS : (group + 1) * CELLS] = centre + stretch[group] * (value - centre)

    kinds, xs, ys, values = [], [], [], []
    sub = lax.broadcasted_iota(I32, (CY, OBS), 0)
    table = jnp.zeros((CY, OBS), F32)
    near = []
    columns, spots = [], []
    for turn in range(BATCHES):
        batch = order_ref[turn]
        owner = owner_ref[pl.ds(batch, 1), :]
        cell = cell_ref[pl.ds(batch, 1), :]
        kinds.append(kind_ref[pl.ds(batch, 1), :])
        values.append(value_ref[pl.ds(batch, 1), :])
        mask = mask_ref[batch].astype(F32)
        xs.append(((owner >> 3) * CX + (cell >> 7)).astype(F32))
        ys.append(((owner & (TILES_Y - 1)) * CY + (cell & (CY - 1))).astype(F32))
        tile_x = owner >> 3
        columns.append(tile_x + REACH)
        reach = REACH * (BATCHES - turn)
        near.append(flag(((tile_x - place_x + reach) & (TILES_X - 1)) <= 2 * reach))
        facts = (
            xs[turn],
            (owner & (TILES_Y - 1)).astype(F32),
            (cell & (CY - 1)).astype(F32),
            mask,
            tile_x.astype(F32),
        )
        for row, value in enumerate(facts):
            table = jnp.where(sub == turn * 8 + row, value, table)
        prior = upper[turn * MEMBERS : (turn + 1) * MEMBERS]
        centre = jnp.sum(prior, axis=0, keepdims=True) * (1.0 / MEMBERS)
        factor = jnp.where(kinds[turn] == 0, stretch[0], stretch[2])
        state_ref[:, AHEAD + turn * OBS : AHEAD + (turn + 1) * OBS] = centre + factor * (prior - centre)
        strip = ((tile_x >> 1) & 3) * 2 + ((owner >> 2) & 1)
        spots.append(strip * 8 + (tile_x & 1) * 4 + (owner & 3))
    for number, (turn, other) in enumerate(PAIRS):
        hot = jnp.where(sub == spots[other] + turn * HALF, 1.0, 0.0)
        spots_ref[:, number * OBS : (number + 1) * OBS] = hot.astype(BF16)
    sheet_ref[:, CY : 2 * CY] = table.T.astype(BF16)
    sheet_ref[:, 2 * CY : 3 * CY] = recv_ref[pl.ds(1, TILES, stride=2), :].astype(BF16)
    ahead = lax.broadcasted_iota(I32, (OBS, OBS), 0) <= lax.broadcasted_iota(I32, (OBS, OBS), 1)
    counts = jnp.concatenate([*near, jnp.zeros((8 - BATCHES, OBS), F32)], axis=0)
    counts = mm(counts.astype(BF16), jnp.where(ahead, 1.0, 0.0).astype(BF16))
    for turn in range(BATCHES):
        slot = jnp.where(near[turn] > 0.0, counts[turn : turn + 1] - 1.0, -1.0)
        order_of_ref[turn : turn + 1] = slot.astype(I32)

    lane = lax.broadcasted_iota(I32, (1, CY), 1)
    cell_x = (place_x * CX).astype(F32)
    cell_y = (place_y * CY + lane).astype(F32)

    for turn in range(BATCHES):
        prior = state_ref[:, AHEAD + turn * OBS : AHEAD + (turn + 1) * OBS]
        error = jnp.where(kinds[turn] == 0, error_ref[0], error_ref[1])
        centre = jnp.sum(prior, axis=0, keepdims=True) * (1.0 / MEMBERS)
        deviation = prior - centre
        variance = jnp.sum(deviation * deviation, axis=0, keepdims=True) / (MEMBERS - 1)
        gain = (values[turn] - centre) / (variance + error)
        shrink = -1.0 / (jnp.sqrt(error * (error + variance)) + error + variance)
        drive_high, drive_low = halves(gain + shrink * deviation)
        drive_ref[:MEMBERS] = drive_high
        drive_ref[MEMBERS:] = drive_low
        scaled = deviation * (1.0 / (MEMBERS - 1))
        scaled_high = scaled.astype(BF16).astype(F32)
        scaled_low = scaled - scaled_high
        packed = jnp.concatenate(
            [scaled_high, scaled_high, scaled_low, jnp.zeros_like(scaled)], axis=0
        )
        sheet_ref[:, :CY] = packed.T.astype(BF16)

        later = list(range(turn + 1, BATCHES))
        blocks = [slice(group * CELLS, (group + 1) * CELLS) for group in range(GROUPS)]
        blocks += [slice(AHEAD + other * OBS, AHEAD + (other + 1) * OBS) for other in later]
        for cols in blocks:
            state = state_ref[:, cols]
            state_dev = state - jnp.sum(state, axis=0, keepdims=True) * (1.0 / MEMBERS)
            high, low = halves(state_dev)
            pack_ref[0:32, cols] = high
            pack_ref[32:64, cols] = low
            pack_ref[64:96, cols] = high
            pack_ref[96:128, cols] = jnp.zeros_like(high)

        total = jnp.sum(near[turn])
        trips = jnp.int32(0)
        for start in range(0, OBS, GATHER):
            trips = trips + jnp.where(total > float(start), 1, 0)
        slot = order_of_ref[turn : turn + 1]

        @pl.loop(0, trips)
        def _(step):
            place = lax.broadcasted_iota(I32, (GATHER, OBS), 0) + step * GATHER
            hot = jnp.where(place == slot, 1.0, 0.0).astype(BF16)
            sheet = mm(hot, sheet_ref[...])
            left = sheet[:, :CY].astype(BF16)
            table = sheet[:, CY : 2 * CY]
            marks = sheet[:, 2 * CY :].astype(BF16)
            drive = lax.dot_general(
                drive_ref[...], hot, (((1,), (1,)), ((), ())), preferred_element_type=F32
            ).astype(BF16)
            x_col = table[:, turn * 8 : turn * 8 + 1]
            y_col = table[:, turn * 8 + 1 : turn * 8 + 2] * CY + table[:, turn * 8 + 2 : turn * 8 + 3]
            mask_col = table[:, turn * 8 + 3 : turn * 8 + 4]
            gap_y = y_col - cell_y
            drop_y = gap_y * gap_y * (1.0 / (LOC_Y * LOC_Y))
            for x in range(CX):
                gap_x = jnp.abs(x_col - (cell_x + x))
                gap_x = jnp.minimum(gap_x, NX - gap_x)
                room = jnp.maximum((1.0 - gap_x * gap_x * (1.0 / (LOC_X * LOC_X))) - drop_y, 0.0)
                weight_ref[:, x * CY : (x + 1) * CY] = room * room * mask_col
            if later:
                column = table[:, turn * 8 + 4 : turn * 8 + 5].astype(I32)
                for index, other in enumerate(later):
                    number = PAIRS.index((turn, other))
                    allowed = mm(marks, spots_ref[:, number * OBS : (number + 1) * OBS])
                    apart = (columns[other] - column) & (TILES_X - 1)
                    allowed = jnp.where(apart < SPAN, allowed, 0.0)
                    gap_x = jnp.abs(x_col - xs[other])
                    gap_x = jnp.minimum(gap_x, NX - gap_x)
                    gap_y = y_col - ys[other]
                    room = 1.0 - gap_x * gap_x * (1.0 / (LOC_X * LOC_X))
                    room = jnp.maximum(room - gap_y * gap_y * (1.0 / (LOC_Y * LOC_Y)), 0.0)
                    weight_ref[:, (index + 1) * OBS : (index + 2) * OBS] = room * room * allowed

            for number, cols in enumerate(blocks):
                at = max(0, number - GROUPS + 1) * OBS
                covariance = mm(left, pack_ref[:, cols]) * weight_ref[:, at : at + OBS]
                high, low = halves(covariance)
                both = mm(drive, high)
                rest = mm(drive[:MEMBERS], low)
                state_ref[:, cols] += both[:MEMBERS] + both[MEMBERS:] + rest

    for group in range(GROUPS):
        for x in range(CX):
            at = group * CELLS + x * CY
            out_ref[rows_of(group, x), :] = state_ref[:, at : at + CY]


def call(kernel, specs, outs, scratch=()):
    return pl.pallas_call(
        kernel,
        in_specs=specs,
        out_specs=[VMEM] * len(outs) if len(outs) > 1 else VMEM,
        out_shape=outs if len(outs) > 1 else outs[0],
        scratch_shapes=list(scratch),
        compiler_params=pltpu.CompilerParams(vmem_limit_bytes=48 * 1024 * 1024),
    )


def shape(*dims):
    return jax.ShapeDtypeStruct(dims, F32)


def swapped(value, axis, step, periodic):
    count = lax.axis_size(axis)
    pairs = []
    for source in range(count):
        target = source + (step if source % 2 == 0 else -step)
        if periodic or 0 <= target < count:
            pairs.append((source, target % count))
    return lax.ppermute(value, axis, pairs)


def local(
    ensemble,
    courant,
    target_spread,
    obs_error,
    obs_value,
    obs_owner,
    obs_cell,
    obs_kind,
    tile_mask,
    batch_order,
):
    place_x = lax.axis_index(GX)
    place_y = lax.axis_index(GY)
    relay = lax.axis_index(PLANE) * LAYERS + lax.axis_index(LAYER)
    place = jnp.stack([place_x, place_y, relay]).astype(I32)
    ens = ensemble.reshape(MEMBERS * GROUPS * CX, CY)
    mask = tile_mask.reshape(BATCHES, 1, OBS)
    own, first, second, send = call(
        spread_kernel,
        [SMEM] * 3 + [VMEM] * 8,
        [
            shape(GROUPS, MEMBERS, CELLS),
            shape(SIDE, CY),
            shape(SIDE, CY),
            shape(PLANES * PLANE_ROWS, CY),
        ],
    )(
        batch_order,
        place,
        courant,
        ens,
        obs_owner,
        obs_cell,
        obs_kind,
        mask,
        target_spread,
        obs_error,
        obs_value,
    )
    recv = lax.all_to_all(send.reshape(PLANES, PLANE_ROWS, CY), PLANE, 0, 0)
    second = swapped(second, GX, -1, True)
    first = swapped(first, GX, 1, True)
    joined, send = call(
        collect_kernel,
        [SMEM] + [VMEM] * 3,
        [shape(GROUPS, MEMBERS, CELLS), shape(LAYERS * LAYER_ROWS, CY)],
    )(place, second, recv.reshape(PLANES * PLANE_ROWS, CY), own)
    recv = lax.all_to_all(send.reshape(LAYERS, LAYER_ROWS // 2, 2, CY), LAYER, 0, 0)
    recv = recv.reshape(LAYERS * LAYER_ROWS, CY)
    forecast, send = call(
        merge_kernel,
        [SMEM] * 3 + [VMEM] * 3,
        [shape(GROUPS, MEMBERS, CELLS), shape(2 * LAYERS, CY)],
    )(batch_order, place, obs_owner, joined, first, recv)
    recv = lax.all_to_all(send.reshape(LAYERS, 2, CY), LAYER, 0, 0)
    chips = PLANES // 2
    send = jnp.broadcast_to(recv.reshape(1, 2 * LAYERS, CY), (chips, 2 * LAYERS, CY))
    mine = lax.all_to_all(send, CHIP, 0, 0).reshape(TILES, CY)
    twin = lax.ppermute(mine, "core", [(0, 1), (1, 0)])
    out = call(
        assimilate_kernel,
        [SMEM] * 4 + [VMEM] * 8,
        [shape(MEMBERS * GROUPS * CX, CY)],
        [
            pltpu.VMEM((MEMBERS, AHEAD + BATCHES * OBS), F32),
            pltpu.VMEM((CY, AHEAD + BATCHES * OBS), BF16),
            pltpu.VMEM((OBS, 3 * CY), BF16),
            pltpu.VMEM((2 * MEMBERS, OBS), BF16),
            pltpu.VMEM((8, OBS), I32),
            pltpu.VMEM((CY, BATCHES * OBS), BF16),
            pltpu.VMEM((GATHER, BATCHES * OBS), F32),
            pltpu.VMEM((2 * TILES, CY), F32),
        ],
    )(
        batch_order,
        place,
        target_spread,
        obs_error,
        forecast,
        mine,
        twin,
        obs_owner,
        obs_cell,
        obs_kind,
        obs_value,
        mask,
    )
    return out.reshape(ensemble.shape)


def solution(mesh):
    fine = Mesh(mesh.devices.reshape(4, 8, 2, 2, 4), ("x", "z_lo", "core", "z_hi", "y"))
    in_specs = (
        P(None, None, None, GX, GY),
        P(),
        P(),
        P(),
        P(),
        P(),
        P(),
        P(),
        P(None, GX, GY, None),
        P(),
    )
    out_specs = P(None, None, None, GX, GY)
    return jax.shard_map(local, mesh=fine, in_specs=in_specs, out_specs=out_specs, check_vma=False)
```
